512 devices in a mesh: sec: 4 (over z_lo, core), sp: 128 (over x, z_hi, y).
Axes of the slice: x: 4, y: 8, z: 8 (z_hi: 4, z_lo: 2; z = z_hi * 2 + z_lo), core: 2. Of those that a mesh axis runs over, the one named last changes fastest.
Arguments:
- queries: bfloat16 [10240, 4096], P('sp', 'sec'), may hold values from -30 to 30
- keys: bfloat16 [12288, 4096], P('sp', 'sec'), may hold values from -30 to 30
- values: bfloat16 [12288, 4096], P('sp', 'sec'), may hold values from -6 to 6
- query_positions: int32 [3, 10240], P(None, 'sp'), may hold values from 0 to 255, as said below
- key_positions: int32 [3, 12288], P(None, 'sp'), may hold values from 0 to 255, as said below
- mixing: bfloat16 [4096, 64], P('sec'), may hold values from -6 to 6
- kernel: bfloat16 [432, 384], replicated, may hold values from -0.3125 to 0.3125
- bias: float32 [384], replicated, may hold values from -1 to 1
- cache: bfloat16 [2, 128, 2, 40, 16], P(None, 'sp'), may hold values from -6 to 6
Outputs:
- decoded: bfloat16 [4, 128, 2, 40, 384], P('sec', 'sp')
The draws below stay inside these ranges and needn't reach their ends.
Inputs may be any that keep to these rules, and one draw needn't show every extreme that they name: `key_positions`: rows are the time, row and column positions of packed tokens. `query_positions`: the positions of the last 10240 tokens of key_positions, in order.
All inputs are finite; a program needn't handle non-finite values.
Results may differ from the reference program's by a relative error of at most 0.009.
Values may be sent and summed in bfloat16 or wider, within the bound.
No kernel may reach another device: no remote copies, remote signals or barrier semaphores. Data moves between devices by JAX's collectives and lax.ppermute only.
A program may use at most 64 MiB of HBM per device.

```python
import math
import jax
import jax.numpy as jnp
from jax import lax

HD = 128
LAT_CH = 16
C_OUT = 384
GRID_W = 80
HEADS = 32
MIX = 64
KEYS = 12288
TILES_W = 4
GRID_H = 32
TILE_LW = 40
SLAB = 10240
LAT_H = 64
LAT_W = 160
N_SEC = 4
N_SP = 128


def position_table(key):
    return jax.random.randint(jax.random.fold_in(key, 101), (3, KEYS), 0, 256, dtype=jnp.int32)


def shared_rows(key):
    return jnp.clip(jax.random.normal(jax.random.fold_in(key, 202), (KEYS, HEADS * HD), jnp.float32), -6.0, 6.0)


def draw_keys(key, part):
    base = shared_rows(key)
    return base.astype(jnp.bfloat16)


def draw_queries(key, part):
    key = jax.random.fold_in(key, 5)
    fresh = jnp.clip(jax.random.normal(key, (SLAB, HEADS * HD), jnp.float32), -6.0, 6.0)
    return fresh.astype(jnp.bfloat16)


def draw_key_positions(key, part):
    return position_table(key)


def draw_query_positions(key, part):
    return position_table(key)[:, KEYS - SLAB:]


def level_of(key, shape, cuts, low, top_value):
    def one(axis_at, parts):
        steps = jax.random.uniform(jax.random.fold_in(jax.random.fold_in(key, 6), axis_at), (parts,), jnp.float32, low / len(cuts), top_value / len(cuts))
        return jnp.repeat(jnp.exp(steps), shape[axis_at] // parts).reshape((-1,) + (1,) * (len(shape) - axis_at - 1))

    level = one(*cuts[0])
    for cut in cuts[1:]:
        level = level * one(*cut)
    return level


def normal_values(own_key, shape, scale, most, pieces=(), kind=jnp.bfloat16):
    values = jax.random.normal(own_key, shape, jnp.float32) * scale
    if len(pieces) > 0:
        values = level_of(own_key, shape, pieces, -0.22, 0.18) * values
    return jnp.clip(values, min=-most, max=most).astype(kind)


def setup_inputs(seed: int = 0) -> dict:
    streams_of = jax.random.split(jax.random.key(seed), 10)
    queries = draw_queries(jax.random.fold_in(streams_of[9], 71), 0)
    keys = draw_keys(jax.random.fold_in(streams_of[9], 71), 0)
    values = normal_values(streams_of[2], (KEYS, HEADS * HD), 1.0, 6.0, ((0, 128), (1, 4)))
    query_positions = draw_query_positions(jax.random.fold_in(streams_of[9], 71), 0)
    key_positions = draw_key_positions(jax.random.fold_in(streams_of[9], 71), 0)
    mixing = normal_values(streams_of[5], (HEADS * HD, MIX), 1.0, 6.0, ((0, 4),))
    kernel = normal_values(streams_of[6], (27 * LAT_CH, C_OUT), (27 * LAT_CH) ** -0.5, 0.3125)
    bias = normal_values(streams_of[7], (C_OUT,), 0.2, 1.0, (), jnp.float32)
    cache = normal_values(streams_of[8], (2, N_SP, 2, TILE_LW, LAT_CH), 1.0, 6.0, ((1, 128),))
    return {"queries": queries, "keys": keys, "values": values, "query_positions": query_positions, "key_positions": key_positions, "mixing": mixing, "kernel": kernel, "bias": bias, "cache": cache}


def rotate(vectors, positions):
    count, heads, width = vectors.shape
    sixth = width // 6
    time_pairs = (width - 4 * sixth) // 2
    time_freq = jnp.power(jnp.float32(10000.0), -jnp.arange(time_pairs, dtype=jnp.float32) / time_pairs)
    space_freq = jnp.power(jnp.float32(10000.0), -jnp.arange(sixth, dtype=jnp.float32) / sixth)
    angles = jnp.concatenate([positions[0].astype(jnp.float32)[:, None] * time_freq[None, :], positions[1].astype(jnp.float32)[:, None] * space_freq[None, :], positions[2].astype(jnp.float32)[:, None] * space_freq[None, :]], axis=1)
    cosine = jnp.cos(angles)[:, None, :]
    sine = jnp.sin(angles)[:, None, :]
    halves = vectors.astype(jnp.float32).reshape(count, heads, width // 2, 2)
    first = halves[..., 0]
    second = halves[..., 1]
    turned = jnp.stack([first * cosine - second * sine, first * sine + second * cosine], axis=-1)
    return turned.reshape(count, heads, width).astype(jnp.bfloat16)

def head_term(query_head, key_head, value_head, mixing_head):
    scale = jnp.float32(1.0 / math.sqrt(HD))
    block = math.gcd(SLAB, 1024)
    blocks = query_head.reshape(SLAB // block, block, HD)

    def one_block(query_block):
        scores = jnp.dot(query_block, key_head.T, preferred_element_type=jnp.float32) * scale
        row_max = lax.optimization_barrier(jnp.max(scores, axis=1, keepdims=True))
        expon = jnp.exp(scores - row_max)
        totals = lax.optimization_barrier(jnp.sum(expon, axis=1))
        sums = jnp.dot(expon.astype(jnp.bfloat16), value_head, preferred_element_type=jnp.float32)
        mixed = jnp.dot(sums, mixing_head.astype(jnp.float32), precision=lax.Precision.HIGHEST)
        return mixed / totals[:, None]
    return lax.map(one_block, blocks).reshape(SLAB, MIX)

def reference(queries, keys, values, query_positions, key_positions, mixing, kernel, bias, cache):
    query_rot = rotate(queries.reshape(SLAB, HEADS, HD), query_positions)
    key_rot = rotate(keys.reshape(KEYS, HEADS, HD), key_positions)
    value_rows = values.reshape(KEYS, HEADS, HD)

    def per_head(total, index):
        query_head = lax.dynamic_index_in_dim(query_rot, index, 1, keepdims=False)
        key_head = lax.dynamic_index_in_dim(key_rot, index, 1, keepdims=False)
        value_head = lax.dynamic_index_in_dim(value_rows, index, 1, keepdims=False)
        mixing_head = lax.dynamic_slice_in_dim(mixing, index * HD, HD, 0)
        return (total + head_term(query_head, key_head, value_head, mixing_head), None)
    patch_values, _ = lax.scan(per_head, jnp.zeros((SLAB, MIX), jnp.float32), jnp.arange(HEADS, dtype=jnp.int32))
    patches = patch_values.astype(jnp.bfloat16)
    latent = patches.reshape(N_SEC, GRID_H, GRID_W, LAT_CH, 2, 2).transpose(0, 1, 4, 2, 5, 3)
    latent = latent.reshape(N_SEC, LAT_H, LAT_W, LAT_CH)
    full_cache = cache.reshape(2, GRID_H, TILES_W, 2, TILE_LW, LAT_CH).transpose(0, 1, 3, 2, 4, 5)
    full_cache = full_cache.reshape(2, LAT_H, LAT_W, LAT_CH)
    extended = jnp.concatenate([full_cache, latent], axis=0)
    extended = jnp.pad(extended, ((0, 0), (1, 1), (1, 1), (0, 0)))
    output = jnp.zeros((N_SEC * LAT_H * LAT_W, C_OUT), jnp.float32)
    for step_t in range(3):
        for step_y in range(3):
            for step_x in range(3):
                window = extended[step_t:step_t + N_SEC, step_y:step_y + LAT_H, step_x:step_x + LAT_W, :]
                offset = ((step_t * 3 + step_y) * 3 + step_x) * LAT_CH
                output = output + jnp.dot(window.reshape(-1, LAT_CH), kernel[offset:offset + LAT_CH], preferred_element_type=jnp.float32)
    output = output + bias.astype(jnp.float32)[None, :]
    output = output.reshape(N_SEC, GRID_H, 2, TILES_W, TILE_LW, C_OUT).transpose(0, 1, 3, 2, 4, 5)
    return output.reshape(N_SEC, N_SP, 2, TILE_LW, C_OUT).astype(jnp.bfloat16)
```

```python
import math

import jax
import jax.numpy as jnp
import numpy as np
from jax import lax
from jax.experimental import pallas as pl
from jax.experimental.pallas import tpu as pltpu
from jax.sharding import Mesh
from jax.sharding import PartitionSpec as P

HD = 128
HEADS_SEC = 8
Q_OWN = 80
K_OWN = 96
V_ROWS = K_OWN // 2
KV_ROWS = K_OWN + V_ROWS
MIX = 64
GRID_W = 80
HALF_W = GRID_W // 2
FRAME = 2560
KEYS_PART = 3072
Q_BLOCK = 640
ROWS_BLOCK = Q_BLOCK // GRID_W
ROWS_WIN = ROWS_BLOCK + 2
MSG = HALF_W + 8
TILE_W = 20
ALL = ("sec", "x", "zh", "y")
SP = ("x", "zh", "y")
VMEM = 56 * 1024 * 1024


def frequency_row():
    sixth = HD // 6
    time_pairs = (HD - 4 * sixth) // 2
    time = 10000.0 ** (-np.arange(time_pairs) / time_pairs)
    space = 10000.0 ** (-np.arange(sixth) / sixth)
    pairs = np.concatenate([time, space, space])
    return np.repeat(pairs, 2).astype(np.float32)[None, :]


def column_order():
    order = np.zeros((2, MIX, 2 * MIX), np.float32)
    for ch in range(16):
        for ab in range(4):
            for side in range(2):
                order[side, ch * 4 + ab, side * MIX + ab * 16 + ch] = 1.0
    return order


def turn_tables(positions, freq):
    lane = lax.broadcasted_iota(jnp.int32, (positions.shape[0], HD), 1)
    base = jnp.where(lane < 44, positions[:, 0:1], jnp.where(lane < 86, positions[:, 1:2], positions[:, 2:3]))
    angle = base * freq
    cosine = jnp.cos(angle)
    sine = jnp.sin(angle)
    even = lax.rem(lane, 2) == 0
    zero = jnp.zeros_like(sine)
    return cosine, jnp.where(even, -sine, zero), jnp.where(even, zero, sine)


def turn(vectors, tables):
    cosine, from_next, from_last = tables
    wide = vectors.astype(jnp.float32)
    out = wide * cosine + pltpu.roll(wide, HD - 1, 1) * from_next + pltpu.roll(wide, 1, 1) * from_last
    return out.astype(jnp.bfloat16)


def prepare_kernel(qpos, kpos, freq, order, queries, keys, values, mixing, kv_out, q_out):
    freq_row = freq[...]
    q_tables = turn_tables(qpos[...], freq_row)
    k_tables = turn_tables(kpos[...], freq_row)
    low, high = order[0], order[1]
    for head in range(HEADS_SEC):
        cols = slice(head * HD, (head + 1) * HD)
        kv_out[head, 0:K_OWN, :] = turn(keys[:, cols], k_tables)
        mix = mixing[cols, :]
        mix_low = jnp.dot(mix, low, preferred_element_type=jnp.float32).astype(jnp.bfloat16)
        mix_high = jnp.dot(mix, high, preferred_element_type=jnp.float32).astype(jnp.bfloat16)
        value = values[:, cols]
        mixed = jnp.dot(value[:V_ROWS], mix_low, preferred_element_type=jnp.float32)
        mixed = mixed + jnp.dot(value[V_ROWS:], mix_high, preferred_element_type=jnp.float32)
        kv_out[head, K_OWN:KV_ROWS, :] = mixed.astype(jnp.bfloat16)
        q_out[head] = turn(queries[:, cols], q_tables)


def prepare(qpos, kpos, queries, keys, values, mixing):
    return pl.pallas_call(
        prepare_kernel,
        out_shape=(
            jax.ShapeDtypeStruct((HEADS_SEC, KV_ROWS, HD), jnp.bfloat16),
            jax.ShapeDtypeStruct((HEADS_SEC, Q_OWN, HD), jnp.bfloat16),
        ),
        compiler_params=pltpu.CompilerParams(vmem_limit_bytes=VMEM),
        name="prepare",
    )(
        qpos.T.astype(jnp.float32),
        kpos.T.astype(jnp.float32),
        jnp.asarray(frequency_row()),
        jnp.asarray(column_order(), jnp.bfloat16),
        queries,
        keys,
        values,
        mixing,
    )


def attend_kernel(q_ref, kv_ref, o_ref, k_buf, v_buf):
    parts = kv_ref.shape[0]

    @pl.when(pl.program_id(0) == 0)
    def _():
        lane = lax.broadcasted_iota(jnp.int32, (V_ROWS, HD), 1)
        ones = jnp.where(lane == MIX, 1.0, 0.0)

        def unpack(part, carry):
            at = pl.multiple_of(part * K_OWN, 16)
            k_buf[pl.ds(at, K_OWN), :] = kv_ref[part, 0:K_OWN, :]
            both = kv_ref[part, K_OWN:KV_ROWS, :].astype(jnp.float32)
            v_buf[pl.ds(at, V_ROWS), :] = jnp.where(lane < MIX, both, ones).astype(jnp.bfloat16)
            other = pltpu.roll(both, MIX, 1)
            at = pl.multiple_of(part * K_OWN + V_ROWS, 16)
            v_buf[pl.ds(at, V_ROWS), :] = jnp.where(lane < MIX, other, ones).astype(jnp.bfloat16)
            return carry

        lax.fori_loop(0, parts, unpack, 0)

    scale = jnp.float32(math.log2(math.e) / math.sqrt(HD))
    scores = lax.dot_general(
        q_ref[...], k_buf[...], (((1,), (1,)), ((), ())), preferred_element_type=jnp.float32
    )
    top = jnp.max(scores, axis=1, keepdims=True)
    weights = jnp.exp2((scores - top) * scale).astype(jnp.bfloat16)
    sums = jnp.dot(weights, v_buf[...], preferred_element_type=jnp.float32)
    total = sums[:, MIX : MIX + 1]
    mean = sums / total
    level = top * scale + jnp.log2(total)
    lane = lax.broadcasted_iota(jnp.int32, (GRID_W, HD), 1)
    row = lax.broadcasted_iota(jnp.int32, (GRID_W, HD), 0)
    low_lane = lax.broadcasted_iota(jnp.int32, (HALF_W, HD), 1) < MIX
    for patch_row in range(ROWS_BLOCK):
        at = patch_row * GRID_W
        low = mean[at : at + HALF_W]
        high = pltpu.roll(mean[at + HALF_W : at + GRID_W], MIX, 1)
        packed = jnp.where(low_lane, low, high)
        line = jnp.sum(jnp.where(lane == row, level[at : at + GRID_W], 0.0), axis=0, keepdims=True)
        first = line.astype(jnp.bfloat16).astype(jnp.float32)
        line = line - first
        second = line.astype(jnp.bfloat16).astype(jnp.float32)
        third = line - second
        message = jnp.concatenate([packed, first, second, third, jnp.zeros((5, HD), jnp.float32)], axis=0)
        o_ref[patch_row] = message.astype(jnp.bfloat16)


def attend(queries, pairs):
    blocks = FRAME // Q_BLOCK
    return pl.pallas_call(
        attend_kernel,
        grid=(blocks,),
        in_specs=[
            pl.BlockSpec((Q_BLOCK, HD), lambda i: (i, 0)),
            pl.BlockSpec(pairs.shape, lambda i: (0, 0, 0)),
        ],
        out_specs=pl.BlockSpec((ROWS_BLOCK, MSG, HD), lambda i: (i, 0, 0)),
        out_shape=jax.ShapeDtypeStruct((FRAME // GRID_W, MSG, HD), jnp.bfloat16),
        scratch_shapes=[
            pltpu.VMEM((KEYS_PART, HD), jnp.bfloat16),
            pltpu.VMEM((KEYS_PART, HD), jnp.bfloat16),
        ],
        compiler_params=pltpu.CompilerParams(vmem_limit_bytes=VMEM),
        name="attend",
    )(queries, pairs)


def combine_kernel(r_ref, o_ref):
    shares = r_ref.shape[0]
    lane = lax.broadcasted_iota(jnp.int32, (HALF_W, HD), 1)
    row = lax.broadcasted_iota(jnp.int32, (HALF_W, HD), 0)
    rows = []
    for win_row in range(ROWS_WIN):
        blocks = [r_ref[share, win_row].astype(jnp.float32) for share in range(shares)]
        levels = [b[HALF_W : HALF_W + 1] + b[HALF_W + 1 : HALF_W + 2] + b[HALF_W + 2 : HALF_W + 3] for b in blocks]
        top = levels[0]
        for level in levels[1:]:
            top = jnp.maximum(top, level)
        powers = [jnp.exp2(level - top) for level in levels]
        total = powers[0]
        for power in powers[1:]:
            total = total + power
        result = jnp.zeros((HALF_W, HD), jnp.float32)
        for block, power in zip(blocks, powers):
            weight = power / total
            low = jnp.sum(jnp.where(lane == row, weight, 0.0), axis=1, keepdims=True)
            high = jnp.sum(jnp.where(lane == row + HALF_W, weight, 0.0), axis=1, keepdims=True)
            result = result + jnp.where(lane < MIX, low, high) * block[:HALF_W]
        rows.append(result)
    zeros = jnp.zeros((16, HD), jnp.float32)
    low_lane = lax.broadcasted_iota(jnp.int32, (16, HD), 1) < MIX
    for win_row in range(ROWS_WIN):
        result = rows[win_row]
        line = jnp.concatenate([zeros[:1], result, pltpu.roll(result, MIX, 1), zeros], axis=0)
        moved = pltpu.roll(line[: 2 * HALF_W + 16], MIX, 1)
        for tile in range(4):
            at = tile * TILE_W
            piece = jnp.where(low_lane, line[at : at + 16], moved[at + 11 : at + 27])
            piece = piece.astype(jnp.bfloat16)
            for step in range(3):
                target = win_row - step
                if 0 <= target < ROWS_BLOCK:
                    o_ref[tile * ROWS_BLOCK + target, step] = piece


def combine(received):
    return pl.pallas_call(
        combine_kernel,
        out_shape=jax.ShapeDtypeStruct((4 * ROWS_BLOCK, 3, 16, HD), jnp.bfloat16),
        compiler_params=pltpu.CompilerParams(vmem_limit_bytes=VMEM),
        name="combine",
    )(received)


def shifted(value, axes, steps, count):
    first, last = (max(0, -steps), min(count, count - steps))
    return lax.ppermute(value, axes, [(source, source + steps) for source in range(first, last)])


def cache_tile(cache, tile_col):
    lat_ch = cache.shape[4]
    wide = cache.reshape(2, 2, -1)
    left = shifted(wide[:, :, -lat_ch:], SP, 1, 128)
    right = shifted(wide[:, :, :lat_ch], SP, -1, 128)
    left = jnp.where(tile_col > 0, left, jnp.zeros_like(left))
    right = jnp.where(tile_col < 3, right, jnp.zeros_like(right))
    sides = jnp.concatenate([left, wide, right], axis=2)
    above = shifted(sides[:, -1:], SP, 4, 128)
    below = shifted(sides[:, :1], SP, -4, 128)
    return jnp.concatenate([above, sides, below], axis=1).reshape(2, 4, -1, lat_ch)


def on_device(queries, keys, values, query_positions, key_positions, mixing, kernel, bias, cache):
    sp_index = lax.axis_index(SP)
    section = lax.axis_index("sec")
    tile_col = sp_index % 4
    tile_row = sp_index // 4
    kv_send, q_send = prepare(query_positions, key_positions, queries, keys, values, mixing)
    kv_head = lax.all_to_all(kv_send, "y", 0, 0)
    q_head = lax.all_to_all(q_send, "y", 0, 0)
    pairs = lax.all_gather(kv_head, "x", axis=0, tiled=True)
    query_all = lax.all_gather(q_head, "zh", axis=0, tiled=True).reshape(FRAME, HD)
    cached = cache_tile(cache, tile_col)
    parts = attend(query_all, pairs)
    before = jnp.concatenate([parts[:1], parts[:-1]], axis=0)[:: ROWS_BLOCK, None]
    behind = jnp.concatenate([parts[1:], parts[-1:]], axis=0)[ROWS_BLOCK - 1 :: ROWS_BLOCK, None]
    windows = jnp.concatenate([before, parts.reshape(4, ROWS_BLOCK, MSG, HD), behind], axis=1)
    shares = lax.all_to_all(windows, "zh", 0, 0)
    tiles = lax.all_to_all(combine(shares), ("sec", "y"), 0, 0)
    strip = jnp.sum(tiles.astype(jnp.float32), axis=0).astype(jnp.bfloat16)
    moved = []
    for step in range(3):
        pairs_at = [
            (((s * 4 + f) * 4 + z) * 8 + y, (f + step) * 128 + (8 * z + y) * 4 + s)
            for s in range(4)
            for f in range(4 - step)
            for z in range(4)
            for y in range(8)
        ]
        moved.append(lax.ppermute(strip, ALL, pairs_at))
    frames = jnp.stack([moved[2], moved[1], moved[0]])
    frames = frames.reshape(3, 3, 16, 2, MIX)[:, :, :11].transpose(0, 1, 3, 2, 4)
    frames = frames.reshape(3, 3, 22, 2, 2, 16).transpose(0, 1, 3, 2, 4, 5).reshape(3, 6, 44, 16)
    frames = frames[:, 1:5, 1:43]
    line = jnp.arange(4)[:, None, None]
    spot = jnp.arange(42)[None, :, None]
    outside = (
        ((tile_row == 0) & (line == 0))
        | ((tile_row == 31) & (line == 3))
        | ((tile_col == 0) & (spot == 0))
        | ((tile_col == 3) & (spot == 41))
    )
    frames = jnp.where(outside[None], jnp.zeros_like(frames), frames)
    minus_two = jnp.where(section >= 2, frames[0], jnp.where(section == 1, cached[1], cached[0]))
    minus_one = jnp.where(section >= 1, frames[1], cached[1])
    frames = jnp.stack([minus_two, minus_one, frames[2]])
    windows = [
        frames[step_t, step_y : step_y + 2, step_x : step_x + 40, :]
        for step_t in range(3)
        for step_y in range(3)
        for step_x in range(3)
    ]
    columns = jnp.stack(windows, axis=2).reshape(80, 27 * 16)
    output = jnp.dot(columns, kernel, preferred_element_type=jnp.float32) + bias[None, :]
    return output.reshape(1, 1, 2, 40, kernel.shape[1]).astype(jnp.bfloat16)


def solution(mesh):
    fine = Mesh(mesh.devices.reshape(4, 4, 4, 8), ALL)
    placed = (
        P(SP, "sec"),
        P(SP, "sec"),
        P(SP, "sec"),
        P(None, SP),
        P(None, SP),
        P("sec", None),
        P(),
        P(),
        P(None, SP, None, None, None),
    )
    return jax.shard_map(
        on_device,
        mesh=fine,
        in_specs=placed,
        out_specs=P("sec", SP, None, None, None),
        check_vma=False,
    )
```

```python
import math

import jax
import jax.numpy as jnp
import numpy as np
from jax import lax
from jax.experimental import pallas as pl
from jax.experimental.pallas import tpu as pltpu
from jax.sharding import Mesh
from jax.sharding import PartitionSpec as P

HD = 128
HEADS_SEC = 8
Q_OWN = 80
K_OWN = 96
V_ROWS = K_OWN // 2
KV_ROWS = K_OWN + V_ROWS
MIX = 64
GRID_W = 80
HALF_W = GRID_W // 2
FRAME = 2560
KEYS_PART = 3072
Q_BLOCK = 640
ROWS_BLOCK = Q_BLOCK // GRID_W
ROWS_WIN = ROWS_BLOCK + 2
SUB = 320
MSG = HALF_W + 8
TILE_W = 20
ALL = ("sec", "x", "zh", "y")
SP = ("x", "zh", "y")
MIB = 1024 * 1024
HERE = pl.BlockSpec(memory_space=pltpu.VMEM)


def frequency_row():
    sixth = HD // 6
    time_pairs = (HD - 4 * sixth) // 2
    time = 10000.0 ** (-np.arange(time_pairs) / time_pairs)
    space = 10000.0 ** (-np.arange(sixth) / sixth)
    pairs = np.concatenate([time, space, space])
    return np.repeat(pairs, 2).astype(np.float32)[None, :]


def row_order():
    order = np.zeros((2, 2 * MIX, MIX), np.float32)
    for ch in range(16):
        for ab in range(4):
            for side in range(2):
                order[side, side * MIX + ab * 16 + ch, ch * 4 + ab] = 1.0
    return order


def turn_tables(positions, freq):
    count = positions.shape[1]
    spot = positions.astype(jnp.float32)
    same = lax.broadcasted_iota(jnp.int32, (count, count), 0) == lax.broadcasted_iota(jnp.int32, (count, count), 1)
    column = [jnp.sum(jnp.where(same, spot[i : i + 1], 0.0), axis=1, keepdims=True) for i in range(3)]
    lane = lax.broadcasted_iota(jnp.int32, (count, HD), 1)
    base = jnp.where(lane < 44, column[0], jnp.where(lane < 86, column[1], column[2]))
    angle = base * freq
    cosine = jnp.cos(angle)
    sine = jnp.sin(angle)
    even = lax.rem(lane, 2) == 0
    zero = jnp.zeros_like(sine)
    return cosine, jnp.where(even, -sine, zero), jnp.where(even, zero, sine)


def turn(vectors, tables):
    cosine, from_next, from_last = tables
    wide = vectors.astype(jnp.float32)
    out = wide * cosine + pltpu.roll(wide, HD - 1, 1) * from_next + pltpu.roll(wide, 1, 1) * from_last
    return out.astype(jnp.bfloat16)


def prepare_queries_kernel(qpos, freq, queries, q_out):
    tables = turn_tables(qpos[...], freq[...])
    for head in range(HEADS_SEC):
        q_out[head] = turn(queries[:, head * HD : (head + 1) * HD], tables)


def prepare_queries(qpos, queries):
    return pl.pallas_call(
        prepare_queries_kernel,
        in_specs=[HERE] * 3,
        out_specs=HERE,
        out_shape=jax.ShapeDtypeStruct((HEADS_SEC, Q_OWN, HD), jnp.bfloat16),
        compiler_params=pltpu.CompilerParams(vmem_limit_bytes=56 * MIB),
        cost_estimate=pl.CostEstimate(flops=1000000, bytes_accessed=400000, transcendentals=0),
        name="prepare_queries",
    )(qpos, jnp.asarray(frequency_row()), queries)


def prepare_pairs_kernel(kpos, freq, order, keys, values, mixing, kv_out):
    tables = turn_tables(kpos[...], freq[...])
    mixed = [
        jnp.dot(order[side], mixing[...], preferred_element_type=jnp.float32).astype(jnp.bfloat16)
        for side in range(2)
    ]
    for head in range(HEADS_SEC):
        cols = slice(head * HD, (head + 1) * HD)
        kv_out[head, 0:K_OWN, :] = turn(keys[:, cols], tables)
        value = values[:, cols]
        low = value[:V_ROWS]
        high = value[V_ROWS:]
        out = lax.dot_general(
            low, mixed[0][:, cols], (((1,), (1,)), ((), ())), preferred_element_type=jnp.float32
        )
        out = out + lax.dot_general(
            high, mixed[1][:, cols], (((1,), (1,)), ((), ())), preferred_element_type=jnp.float32
        )
        kv_out[head, K_OWN:KV_ROWS, :] = out.astype(jnp.bfloat16)


def prepare_pairs(kpos, keys, values, mixing):
    return pl.pallas_call(
        prepare_pairs_kernel,
        in_specs=[HERE] * 6,
        out_specs=HERE,
        out_shape=jax.ShapeDtypeStruct((HEADS_SEC, KV_ROWS, HD), jnp.bfloat16),
        compiler_params=pltpu.CompilerParams(vmem_limit_bytes=56 * MIB),
        cost_estimate=pl.CostEstimate(flops=50000000, bytes_accessed=900000, transcendentals=0),
        name="prepare_pairs",
    )(
        kpos,
        jnp.asarray(frequency_row()),
        jnp.asarray(row_order(), jnp.bfloat16),
        keys,
        values,
        mixing.T,
    )


def attend_kernel(*refs):
    q_refs, kv_refs, o_refs = refs[0:4], refs[4:8], refs[8:12]
    q_buf, k_buf, v_buf, s_even, s_odd, m_buf = refs[12:]
    lane = lax.broadcasted_iota(jnp.int32, (V_ROWS, HD), 1)
    ones = jnp.where(lane == MIX, 1.0, 0.0)
    for piece in range(4):
        for part in range(8):
            q_buf[piece * Q_BLOCK + part * Q_OWN : piece * Q_BLOCK + (part + 1) * Q_OWN] = q_refs[piece][part]

        def unpack(part, carry, piece=piece):
            at = pl.multiple_of(piece * 8 * K_OWN + part * K_OWN, 16)
            k_buf[pl.ds(at, K_OWN), :] = kv_refs[piece][part, 0:K_OWN, :]
            both = kv_refs[piece][part, K_OWN:KV_ROWS, :].astype(jnp.float32)
            v_buf[pl.ds(at, V_ROWS), :] = jnp.where(lane < MIX, both, ones).astype(jnp.bfloat16)
            other = pltpu.roll(both, MIX, 1)
            at = pl.multiple_of(piece * 8 * K_OWN + part * K_OWN + V_ROWS, 16)
            v_buf[pl.ds(at, V_ROWS), :] = jnp.where(lane < MIX, other, ones).astype(jnp.bfloat16)
            return carry

        lax.fori_loop(0, 8, unpack, 0)

    scale = jnp.float32(math.log2(math.e) / math.sqrt(HD))
    diagonal = lax.broadcasted_iota(jnp.int32, (GRID_W, HD), 1) == lax.broadcasted_iota(jnp.int32, (GRID_W, HD), 0)
    low_lane = lax.broadcasted_iota(jnp.int32, (HALF_W, HD), 1) < MIX

    def score(block):
        at = pl.multiple_of(block * SUB, 16)
        return lax.dot_general(
            q_buf[pl.ds(at, SUB), :], k_buf[...], (((1,), (1,)), ((), ())), preferred_element_type=jnp.float32
        )

    def finish(block, s_ref):
        scores = s_ref[...]
        top = jnp.max(scores, axis=1, keepdims=True)
        weights = jnp.exp2((scores - top) * scale).astype(jnp.bfloat16)
        sums = jnp.dot(weights, v_buf[...], preferred_element_type=jnp.float32)
        total = sums[:, MIX : MIX + 1]
        mean = sums / total
        level = top * scale + jnp.log2(total)
        for patch_row in range(SUB // GRID_W):
            at = patch_row * GRID_W
            low = mean[at : at + HALF_W]
            high = pltpu.roll(mean[at + HALF_W : at + GRID_W], MIX, 1)
            packed = jnp.where(low_lane, low, high)
            line = jnp.sum(jnp.where(diagonal, level[at : at + GRID_W], 0.0), axis=0, keepdims=True)
            first = line.astype(jnp.bfloat16).astype(jnp.float32)
            line = line - first
            second = line.astype(jnp.bfloat16).astype(jnp.float32)
            third = line - second
            message = jnp.concatenate([packed, first, second, third, jnp.zeros((5, HD), jnp.float32)], axis=0)
            m_buf[block * (SUB // GRID_W) + patch_row] = message.astype(jnp.bfloat16)

    s_even[...] = score(0)
    blocks = FRAME // SUB

    def pair(step, carry):
        s_odd[...] = score(2 * step + 1)
        finish(2 * step, s_even)
        s_even[...] = score(jnp.minimum(2 * step + 2, blocks - 1))
        finish(2 * step + 1, s_odd)
        return carry

    lax.fori_loop(0, blocks // 2, pair, 0)
    rows = FRAME // GRID_W
    for piece in range(4):
        first = piece * ROWS_BLOCK
        o_refs[piece][0] = m_buf[(first - 1) % rows]
        o_refs[piece][1 : 1 + ROWS_BLOCK] = m_buf[first : first + ROWS_BLOCK]
        o_refs[piece][1 + ROWS_BLOCK] = m_buf[(first + ROWS_BLOCK) % rows]


def attend(queries, pairs):
    return pl.pallas_call(
        attend_kernel,
        in_specs=[HERE] * 8,
        out_specs=[HERE] * 4,
        out_shape=[jax.ShapeDtypeStruct((ROWS_WIN, MSG, HD), jnp.bfloat16)] * 4,
        scratch_shapes=[
            pltpu.VMEM((FRAME, HD), jnp.bfloat16),
            pltpu.VMEM((KEYS_PART, HD), jnp.bfloat16),
            pltpu.VMEM((KEYS_PART, HD), jnp.bfloat16),
            pltpu.VMEM((SUB, KEYS_PART), jnp.float32),
            pltpu.VMEM((SUB, KEYS_PART), jnp.float32),
            pltpu.VMEM((FRAME // GRID_W, MSG, HD), jnp.bfloat16),
        ],
        compiler_params=pltpu.CompilerParams(vmem_limit_bytes=28 * MIB),
        cost_estimate=pl.CostEstimate(flops=4 * FRAME * KEYS_PART * HD, bytes_accessed=2000000, transcendentals=0),
        name="attend",
    )(*queries, *pairs)


def combine_kernel(*refs):
    shares, o_ref = refs[:-1], refs[-1]
    lane = lax.broadcasted_iota(jnp.int32, (HALF_W, HD), 1)
    row = lax.broadcasted_iota(jnp.int32, (HALF_W, HD), 0)
    rows = []
    for win_row in range(ROWS_WIN):
        blocks = [share[win_row].astype(jnp.float32) for share in shares]
        levels = [b[HALF_W : HALF_W + 1] + b[HALF_W + 1 : HALF_W + 2] + b[HALF_W + 2 : HALF_W + 3] for b in blocks]
        top = levels[0]
        for level in levels[1:]:
            top = jnp.maximum(top, level)
        powers = [jnp.exp2(level - top) for level in levels]
        total = powers[0]
        for power in powers[1:]:
            total = total + power
        result = jnp.zeros((HALF_W, HD), jnp.float32)
        for block, power in zip(blocks, powers):
            weight = power / total
            low = jnp.sum(jnp.where(lane == row, weight, 0.0), axis=1, keepdims=True)
            high = jnp.sum(jnp.where(lane == row + HALF_W, weight, 0.0), axis=1, keepdims=True)
            result = result + jnp.where(lane < MIX, low, high) * block[:HALF_W]
        rows.append(result)
    zeros = jnp.zeros((16, HD), jnp.float32)
    low_lane = lax.broadcasted_iota(jnp.int32, (16, HD), 1) < MIX
    for win_row in range(ROWS_WIN):
        result = rows[win_row]
        line = jnp.concatenate([zeros[:1], result, pltpu.roll(result, MIX, 1), zeros], axis=0)
        moved = pltpu.roll(line[: 2 * HALF_W + 16], MIX, 1)
        for tile in range(4):
            at = tile * TILE_W
            piece = jnp.where(low_lane, line[at : at + 16], moved[at + 11 : at + 27])
            piece = piece.astype(jnp.bfloat16)
            for step in range(3):
                target = win_row - step
                if 0 <= target < ROWS_BLOCK:
                    o_ref[tile * ROWS_BLOCK + target, step] = piece


def combine(received):
    return pl.pallas_call(
        combine_kernel,
        in_specs=[HERE] * 4,
        out_specs=HERE,
        out_shape=jax.ShapeDtypeStruct((4 * ROWS_BLOCK, 3, 16, HD), jnp.bfloat16),
        compiler_params=pltpu.CompilerParams(vmem_limit_bytes=8 * MIB),
        cost_estimate=pl.CostEstimate(flops=1000000, bytes_accessed=900000, transcendentals=0),
        name="combine",
    )(*received)


def shifted(value, axes, steps, count):
    first, last = (max(0, -steps), min(count, count - steps))
    return lax.ppermute(value, axes, [(source, source + steps) for source in range(first, last)])


def from_ahead(value, axis, steps):
    return lax.ppermute(value, axis, [((spot + steps) % 4, spot) for spot in range(4)])


def cache_tile(cache, tile_col):
    lat_ch = cache.shape[4]
    wide = cache.reshape(2, 2, -1)
    left = shifted(wide[:, :, -lat_ch:], SP, 1, 128)
    right = shifted(wide[:, :, :lat_ch], SP, -1, 128)
    left = jnp.where(tile_col > 0, left, jnp.zeros_like(left))
    right = jnp.where(tile_col < 3, right, jnp.zeros_like(right))
    sides = jnp.concatenate([left, wide, right], axis=2)
    above = shifted(sides[:, -1:], SP, 4, 128)
    below = shifted(sides[:, :1], SP, -4, 128)
    return jnp.concatenate([above, sides, below], axis=1).reshape(2, 4, -1, lat_ch)


def on_device(queries, keys, values, query_positions, key_positions, mixing, kernel, bias, cache):
    sp_index = lax.axis_index(SP)
    section = lax.axis_index("sec")
    tile_col = sp_index % 4
    tile_row = sp_index // 4
    q_own = lax.all_to_all(prepare_queries(query_positions, queries), "y", 0, 0)
    kv_own = lax.all_to_all(prepare_pairs(key_positions, keys, values, mixing), "y", 0, 0)
    query_all = [q_own] + [from_ahead(q_own, "zh", step) for step in (1, 2, 3)]
    pairs = [kv_own] + [from_ahead(kv_own, "x", step) for step in (1, 2, 3)]
    cached = cache_tile(cache, tile_col)
    query_all, pairs, cached = lax.optimization_barrier((query_all, pairs, cached))
    parts = attend(query_all, pairs)
    shares = [parts[0]] + [from_ahead(parts[step], "zh", -step) for step in (1, 2, 3)]
    tiles = lax.all_to_all(combine(shares), ("sec", "y"), 0, 0)
    strip = jnp.sum(tiles.astype(jnp.float32), axis=0).astype(jnp.bfloat16)
    moved = []
    for step in range(3):
        pairs_at = [
            (((s * 4 + f) * 4 + z) * 8 + y, (f + step) * 128 + (8 * z + y) * 4 + s)
            for s in range(4)
            for f in range(4 - step)
            for z in range(4)
            for y in range(8)
        ]
        moved.append(lax.ppermute(strip, ALL, pairs_at))
    frames = jnp.stack([moved[2], moved[1], moved[0]])
    frames = frames.reshape(3, 3, 16, 2, MIX)[:, :, :11].transpose(0, 1, 3, 2, 4)
    frames = frames.reshape(3, 3, 22, 2, 2, 16).transpose(0, 1, 3, 2, 4, 5).reshape(3, 6, 44, 16)
    frames = frames[:, 1:5, 1:43]
    line = jnp.arange(4)[:, None, None]
    spot = jnp.arange(42)[None, :, None]
    outside = (
        ((tile_row == 0) & (line == 0))
        | ((tile_row == 31) & (line == 3))
        | ((tile_col == 0) & (spot == 0))
        | ((tile_col == 3) & (spot == 41))
    )
    frames = jnp.where(outside[None], jnp.zeros_like(frames), frames)
    minus_two = jnp.where(section >= 2, frames[0], jnp.where(section == 1, cached[1], cached[0]))
    minus_one = jnp.where(section >= 1, frames[1], cached[1])
    frames = jnp.stack([minus_two, minus_one, frames[2]])
    windows = [
        frames[step_t, step_y : step_y + 2, step_x : step_x + 40, :]
        for step_t in range(3)
        for step_y in range(3)
        for step_x in range(3)
    ]
    columns = jnp.stack(windows, axis=2).reshape(80, 27 * 16)
    output = jnp.dot(columns, kernel, preferred_element_type=jnp.float32) + bias[None, :]
    return output.reshape(1, 1, 2, 40, kernel.shape[1]).astype(jnp.bfloat16)


def solution(mesh):
    fine = Mesh(mesh.devices.reshape(4, 4, 4, 8), ALL)
    placed = (
        P(SP, "sec"),
        P(SP, "sec"),
        P(SP, "sec"),
        P(None, SP),
        P(None, SP),
        P("sec", None),
        P(),
        P(),
        P(None, SP, None, None, None),
    )
    return jax.shard_map(
        on_device,
        mesh=fine,
        in_specs=placed,
        out_specs=P("sec", SP, None, None, None),
        check_vma=False,
    )
```

```python
import math

import jax
import jax.numpy as jnp
import numpy as np
from jax import lax
from jax.experimental import pallas as pl
from jax.experimental.pallas import tpu as pltpu
from jax.sharding import Mesh
from jax.sharding import PartitionSpec as P

HD = 128
HEADS_SEC = 8
Q_OWN = 80
K_OWN = 96
V_ROWS = K_OWN // 2
KV_ROWS = K_OWN + V_ROWS
MIX = 64
GRID_W = 80
HALF_W = GRID_W // 2
FRAME = 2560
KEYS_PART = 3072
Q_BLOCK = 640
ROWS_BLOCK = Q_BLOCK // GRID_W
SUB = 320
MSG = HALF_W + 8
TILE_W = 20
ALL = ("sec", "x", "zh", "y")
SP = ("x", "zh", "y")
MIB = 1024 * 1024
HERE = pl.BlockSpec(memory_space=pltpu.VMEM)


def frequency_row():
    sixth = HD // 6
    time_pairs = (HD - 4 * sixth) // 2
    time = 10000.0 ** (-np.arange(time_pairs) / time_pairs)
    space = 10000.0 ** (-np.arange(sixth) / sixth)
    pairs = np.concatenate([time, space, space])
    return np.repeat(pairs, 2).astype(np.float32)[None, :]


def row_order():
    order = np.zeros((2, 2 * MIX, MIX), np.float32)
    for ch in range(16):
        for ab in range(4):
            for side in range(2):
                order[side, side * MIX + ab * 16 + ch, ch * 4 + ab] = 1.0
    return order


def turn_tables(positions, freq):
    count = positions.shape[1]
    spot = positions.astype(jnp.float32)
    same = lax.broadcasted_iota(jnp.int32, (count, count), 0) == lax.broadcasted_iota(jnp.int32, (count, count), 1)
    column = [jnp.sum(jnp.where(same, spot[i : i + 1], 0.0), axis=1, keepdims=True) for i in range(3)]
    lane = lax.broadcasted_iota(jnp.int32, (count, HD), 1)
    base = jnp.where(lane < 44, column[0], jnp.where(lane < 86, column[1], column[2]))
    angle = base * freq
    cosine = jnp.cos(angle)
    sine = jnp.sin(angle)
    even = lax.rem(lane, 2) == 0
    zero = jnp.zeros_like(sine)
    return cosine, jnp.where(even, -sine, zero), jnp.where(even, zero, sine)


def turn(vectors, tables):
    cosine, from_next, from_last = tables
    wide = vectors.astype(jnp.float32)
    out = wide * cosine + pltpu.roll(wide, HD - 1, 1) * from_next + pltpu.roll(wide, 1, 1) * from_last
    return out.astype(jnp.bfloat16)


def prepare_queries_kernel(qpos, freq, queries, q_out):
    tables = turn_tables(qpos[...], freq[...])
    for head in range(HEADS_SEC):
        q_out[head] = turn(queries[:, head * HD : (head + 1) * HD], tables)


def prepare_queries(qpos, queries):
    return pl.pallas_call(
        prepare_queries_kernel,
        in_specs=[HERE] * 3,
        out_specs=HERE,
        out_shape=jax.ShapeDtypeStruct((HEADS_SEC, Q_OWN, HD), jnp.bfloat16),
        compiler_params=pltpu.CompilerParams(vmem_limit_bytes=56 * MIB),
        cost_estimate=pl.CostEstimate(flops=1000000, bytes_accessed=400000, transcendentals=0),
        name="prepare_queries",
    )(qpos, jnp.asarray(frequency_row()), queries)


def prepare_pairs_kernel(kpos, freq, order, keys, values, mixing, kv_out):
    tables = turn_tables(kpos[...], freq[...])
    mixed = [
        jnp.dot(order[side], mixing[...], preferred_element_type=jnp.float32).astype(jnp.bfloat16)
        for side in range(2)
    ]
    for head in range(HEADS_SEC):
        cols = slice(head * HD, (head + 1) * HD)
        kv_out[head, 0:K_OWN, :] = turn(keys[:, cols], tables)
        value = values[:, cols]
        low = value[:V_ROWS]
        high = value[V_ROWS:]
        out = lax.dot_general(
            low, mixed[0][:, cols], (((1,), (1,)), ((), ())), preferred_element_type=jnp.float32
        )
        out = out + lax.dot_general(
            high, mixed[1][:, cols], (((1,), (1,)), ((), ())), preferred_element_type=jnp.float32
        )
        kv_out[head, K_OWN:KV_ROWS, :] = out.astype(jnp.bfloat16)


def prepare_pairs(kpos, keys, values, mixing):
    return pl.pallas_call(
        prepare_pairs_kernel,
        in_specs=[HERE] * 6,
        out_specs=HERE,
        out_shape=jax.ShapeDtypeStruct((HEADS_SEC, KV_ROWS, HD), jnp.bfloat16),
        compiler_params=pltpu.CompilerParams(vmem_limit_bytes=56 * MIB),
        cost_estimate=pl.CostEstimate(flops=50000000, bytes_accessed=900000, transcendentals=0),
        name="prepare_pairs",
    )(
        kpos,
        jnp.asarray(frequency_row()),
        jnp.asarray(row_order(), jnp.bfloat16),
        keys,
        values,
        mixing.T,
    )


def attend_kernel(*refs):
    place, q_refs, kv_refs, o_ref = refs[0], refs[1:5], refs[5:9], refs[9]
    q_buf, k_buf, v_buf, s_even, s_odd = refs[10:]
    lane = lax.broadcasted_iota(jnp.int32, (V_ROWS, HD), 1)
    ones = jnp.where(lane == MIX, 1.0, 0.0)
    for piece in range(4):
        for part in range(8):
            q_buf[piece * Q_BLOCK + part * Q_OWN : piece * Q_BLOCK + (part + 1) * Q_OWN] = q_refs[piece][part]

        def unpack(part, carry, piece=piece):
            at = pl.multiple_of(piece * 8 * K_OWN + part * K_OWN, 16)
            k_buf[pl.ds(at, K_OWN), :] = kv_refs[piece][part, 0:K_OWN, :]
            both = kv_refs[piece][part, K_OWN:KV_ROWS, :].astype(jnp.float32)
            v_buf[pl.ds(at, V_ROWS), :] = jnp.where(lane < MIX, both, ones).astype(jnp.bfloat16)
            other = pltpu.roll(both, MIX, 1)
            at = pl.multiple_of(piece * 8 * K_OWN + part * K_OWN + V_ROWS, 16)
            v_buf[pl.ds(at, V_ROWS), :] = jnp.where(lane < MIX, other, ones).astype(jnp.bfloat16)
            return carry

        lax.fori_loop(0, 8, unpack, 0)

    scale = jnp.float32(math.log2(math.e) / math.sqrt(HD))
    diagonal = lax.broadcasted_iota(jnp.int32, (GRID_W, HD), 1) == lax.broadcasted_iota(jnp.int32, (GRID_W, HD), 0)
    low_lane = lax.broadcasted_iota(jnp.int32, (HALF_W, HD), 1) < MIX

    def score(block):
        at = pl.multiple_of(block * SUB, 16)
        return lax.dot_general(
            q_buf[pl.ds(at, SUB), :], k_buf[...], (((1,), (1,)), ((), ())), preferred_element_type=jnp.float32
        )

    def finish(piece, block, s_ref):
        scores = s_ref[...]
        top = jnp.max(scores, axis=1, keepdims=True)
        weights = jnp.exp2((scores - top) * scale).astype(jnp.bfloat16)
        sums = jnp.dot(weights, v_buf[...], preferred_element_type=jnp.float32)
        total = sums[:, MIX : MIX + 1]
        mean = sums / total
        level = top * scale + jnp.log2(total)
        for patch_row in range(SUB // GRID_W):
            at = patch_row * GRID_W
            low = mean[at : at + HALF_W]
            high = pltpu.roll(mean[at + HALF_W : at + GRID_W], MIX, 1)
            packed = jnp.where(low_lane, low, high)
            line = jnp.sum(jnp.where(diagonal, level[at : at + GRID_W], 0.0), axis=0, keepdims=True)
            first = line.astype(jnp.bfloat16).astype(jnp.float32)
            line = line - first
            second = line.astype(jnp.bfloat16).astype(jnp.float32)
            third = line - second
            message = jnp.concatenate([packed, first, second, third, jnp.zeros((5, HD), jnp.float32)], axis=0)
            spot = block * (SUB // GRID_W) + patch_row
            o_ref[lax.rem(place[0] + piece, 4), spot] = message.astype(jnp.bfloat16)

    s_even[...] = score(0)
    blocks = FRAME // SUB

    def pair(step, carry):
        s_odd[...] = score(2 * step + 1)
        finish(step, 0, s_even)
        s_even[...] = score(jnp.minimum(2 * step + 2, blocks - 1))
        finish(step, 1, s_odd)
        return carry

    lax.fori_loop(0, blocks // 2, pair, 0)


def attend(place, queries, pairs):
    return pl.pallas_call(
        attend_kernel,
        in_specs=[pl.BlockSpec(memory_space=pltpu.SMEM)] + [HERE] * 8,
        out_specs=HERE,
        out_shape=jax.ShapeDtypeStruct((4, ROWS_BLOCK, MSG, HD), jnp.bfloat16),
        scratch_shapes=[
            pltpu.VMEM((FRAME, HD), jnp.bfloat16),
            pltpu.VMEM((KEYS_PART, HD), jnp.bfloat16),
            pltpu.VMEM((KEYS_PART, HD), jnp.bfloat16),
            pltpu.VMEM((SUB, KEYS_PART), jnp.float32),
            pltpu.VMEM((SUB, KEYS_PART), jnp.float32),
        ],
        compiler_params=pltpu.CompilerParams(vmem_limit_bytes=28 * MIB),
        cost_estimate=pl.CostEstimate(flops=4 * FRAME * KEYS_PART * HD, bytes_accessed=2000000, transcendentals=0),
        name="attend",
    )(place, *queries, *pairs)


def combine_kernel(r_ref, o_ref):
    shares = r_ref.shape[0]
    lane = lax.broadcasted_iota(jnp.int32, (HALF_W, HD), 1)
    row = lax.broadcasted_iota(jnp.int32, (HALF_W, HD), 0)
    zeros = jnp.zeros((16, HD), jnp.float32)
    low_lane = lax.broadcasted_iota(jnp.int32, (16, HD), 1) < MIX
    for patch_row in range(ROWS_BLOCK):
        blocks = [r_ref[share, patch_row].astype(jnp.float32) for share in range(shares)]
        levels = [b[HALF_W : HALF_W + 1] + b[HALF_W + 1 : HALF_W + 2] + b[HALF_W + 2 : HALF_W + 3] for b in blocks]
        top = levels[0]
        for level in levels[1:]:
            top = jnp.maximum(top, level)
        powers = [jnp.exp2(level - top) for level in levels]
        total = powers[0]
        for power in powers[1:]:
            total = total + power
        result = jnp.zeros((HALF_W, HD), jnp.float32)
        for block, power in zip(blocks, powers):
            weight = power / total
            low = jnp.sum(jnp.where(lane == row, weight, 0.0), axis=1, keepdims=True)
            high = jnp.sum(jnp.where(lane == row + HALF_W, weight, 0.0), axis=1, keepdims=True)
            result = result + jnp.where(lane < MIX, low, high) * block[:HALF_W]
        line = jnp.concatenate([zeros[:1], result, pltpu.roll(result, MIX, 1), zeros], axis=0)
        moved = pltpu.roll(line[: 2 * HALF_W + 16], MIX, 1)
        for tile in range(4):
            at = tile * TILE_W
            piece = jnp.where(low_lane, line[at : at + 16], moved[at + 11 : at + 27])
            o_ref[tile * ROWS_BLOCK + patch_row] = piece.astype(jnp.bfloat16)


def combine(received):
    return pl.pallas_call(
        combine_kernel,
        in_specs=[HERE],
        out_specs=HERE,
        out_shape=jax.ShapeDtypeStruct((4 * ROWS_BLOCK, 16, HD), jnp.bfloat16),
        compiler_params=pltpu.CompilerParams(vmem_limit_bytes=8 * MIB),
        cost_estimate=pl.CostEstimate(flops=1000000, bytes_accessed=900000, transcendentals=0),
        name="combine",
    )(received)


def shifted(value, axes, steps, count):
    first, last = (max(0, -steps), min(count, count - steps))
    return lax.ppermute(value, axes, [(source, source + steps) for source in range(first, last)])


def from_ahead(value, axis, steps):
    return lax.ppermute(value, axis, [((spot + steps) % 4, spot) for spot in range(4)])


def cache_tile(cache, tile_col):
    lat_ch = cache.shape[4]
    wide = cache.reshape(2, 2, -1)
    left = shifted(wide[:, :, -lat_ch:], SP, 1, 128)
    right = shifted(wide[:, :, :lat_ch], SP, -1, 128)
    left = jnp.where(tile_col > 0, left, jnp.zeros_like(left))
    right = jnp.where(tile_col < 3, right, jnp.zeros_like(right))
    sides = jnp.concatenate([left, wide, right], axis=2)
    above = shifted(sides[:, -1:], SP, 4, 128)
    below = shifted(sides[:, :1], SP, -4, 128)
    return jnp.concatenate([above, sides, below], axis=1).reshape(2, 4, -1, lat_ch)


def on_device(queries, keys, values, query_positions, key_positions, mixing, kernel, bias, cache):
    sp_index = lax.axis_index(SP)
    section = lax.axis_index("sec")
    tile_col = sp_index % 4
    tile_row = sp_index // 4
    q_own = lax.all_to_all(prepare_queries(query_positions, queries), "y", 0, 0)
    kv_own = lax.all_to_all(prepare_pairs(key_positions, keys, values, mixing), "y", 0, 0)
    query_all = [q_own] + [from_ahead(q_own, "zh", step) for step in (1, 2, 3)]
    cached = cache_tile(cache, tile_col)
    query_all, kv_own, cached = lax.optimization_barrier((query_all, kv_own, cached))
    pairs = [kv_own] + [from_ahead(kv_own, "x", step) for step in (1, 2, 3)]
    parts = attend(lax.axis_index("zh").reshape(1), query_all, pairs)
    shares = lax.all_to_all(parts, "zh", 0, 0)
    tiles = lax.all_to_all(combine(shares), ("sec", "y"), 0, 0)
    strip = jnp.sum(tiles.astype(jnp.float32), axis=0).astype(jnp.bfloat16)
    strip = jnp.stack([shifted(strip, ("zh", "y"), 1, 32), strip, shifted(strip, ("zh", "y"), -1, 32)])
    moved = []
    for step in range(3):
        pairs_at = [
            (((s * 4 + f) * 4 + z) * 8 + y, (f + step) * 128 + (8 * z + y) * 4 + s)
            for s in range(4)
            for f in range(4 - step)
            for z in range(4)
            for y in range(8)
        ]
        moved.append(lax.ppermute(strip, ALL, pairs_at))
    frames = jnp.stack([moved[2], moved[1], moved[0]])
    frames = frames.reshape(3, 3, 16, 2, MIX)[:, :, :11].transpose(0, 1, 3, 2, 4)
    frames = frames.reshape(3, 3, 22, 2, 2, 16).transpose(0, 1, 3, 2, 4, 5).reshape(3, 6, 44, 16)
    frames = frames[:, 1:5, 1:43]
    line = jnp.arange(4)[:, None, None]
    spot = jnp.arange(42)[None, :, None]
    outside = (
        ((tile_row == 0) & (line == 0))
        | ((tile_row == 31) & (line == 3))
        | ((tile_col == 0) & (spot == 0))
        | ((tile_col == 3) & (spot == 41))
    )
    frames = jnp.where(outside[None], jnp.zeros_like(frames), frames)
    minus_two = jnp.where(section >= 2, frames[0], jnp.where(section == 1, cached[1], cached[0]))
    minus_one = jnp.where(section >= 1, frames[1], cached[1])
    frames = jnp.stack([minus_two, minus_one, frames[2]])
    windows = [
        frames[step_t, step_y : step_y + 2, step_x : step_x + 40, :]
        for step_t in range(3)
        for step_y in range(3)
        for step_x in range(3)
    ]
    columns = jnp.stack(windows, axis=2).reshape(80, 27 * 16)
    output = jnp.dot(columns, kernel, preferred_element_type=jnp.float32) + bias[None, :]
    return output.reshape(1, 1, 2, 40, kernel.shape[1]).astype(jnp.bfloat16)


def solution(mesh):
    fine = Mesh(mesh.devices.reshape(4, 4, 4, 8), ALL)
    placed = (
        P(SP, "sec"),
        P(SP, "sec"),
        P(SP, "sec"),
        P(None, SP),
        P(None, SP),
        P("sec", None),
        P(),
        P(),
        P(None, SP, None, None, None),
    )
    return jax.shard_map(
        on_device,
        mesh=fine,
        in_specs=placed,
        out_specs=P("sec", SP, None, None, None),
        check_vma=False,
    )
```

```python
import math

import jax
import jax.numpy as jnp
import numpy as np
from jax import lax
from jax.experimental import pallas as pl
from jax.experimental.pallas import tpu as pltpu
from jax.sharding import Mesh
from jax.sharding import PartitionSpec as P

HD = 128
HEADS_SEC = 8
Q_OWN = 80
Q_ROWS = Q_OWN + 32
K_OWN = 96
V_ROWS = K_OWN // 2
KV_ROWS = K_OWN + V_ROWS
MIX = 64
GRID_W = 80
HALF_W = GRID_W // 2
FRAME = 2560
KEYS_PART = 3072
Q_BLOCK = 640
ROWS_BLOCK = Q_BLOCK // GRID_W
SUB = 320
MSG = HALF_W + 8
TILE_W = 20
ALL = ("sec", "x", "zh", "y")
SP = ("x", "zh", "y")
MIB = 1024 * 1024
HERE = pl.BlockSpec(memory_space=pltpu.VMEM)


def frequency_row():
    sixth = HD // 6
    time_pairs = (HD - 4 * sixth) // 2
    time = 10000.0 ** (-np.arange(time_pairs) / time_pairs)
    space = 10000.0 ** (-np.arange(sixth) / sixth)
    pairs = np.concatenate([time, space, space])
    return np.repeat(pairs, 2).astype(np.float32)[None, :]


def row_order():
    order = np.zeros((2, 2 * MIX, MIX), np.float32)
    for ch in range(16):
        for ab in range(4):
            for side in range(2):
                order[side, side * MIX + ab * 16 + ch, ch * 4 + ab] = 1.0
    return order


def turn_tables(positions, freq):
    count = positions.shape[1]
    spot = positions.astype(jnp.float32)
    same = lax.broadcasted_iota(jnp.int32, (count, count), 0) == lax.broadcasted_iota(jnp.int32, (count, count), 1)
    column = [jnp.sum(jnp.where(same, spot[i : i + 1], 0.0), axis=1, keepdims=True) for i in range(3)]
    lane = lax.broadcasted_iota(jnp.int32, (count, HD), 1)
    base = jnp.where(lane < 44, column[0], jnp.where(lane < 86, column[1], column[2]))
    angle = base * freq
    cosine = jnp.cos(angle)
    sine = jnp.sin(angle)
    even = lax.rem(lane, 2) == 0
    zero = jnp.zeros_like(sine)
    return cosine, jnp.where(even, -sine, zero), jnp.where(even, zero, sine)


def turn(vectors, tables):
    cosine, from_next, from_last = tables
    wide = vectors.astype(jnp.float32)
    out = wide * cosine + pltpu.roll(wide, HD - 1, 1) * from_next + pltpu.roll(wide, 1, 1) * from_last
    return out.astype(jnp.bfloat16)


def prepare_queries_kernel(qpos, freq, queries, cache, q_out):
    tables = turn_tables(qpos[...], freq[...])
    spots = jnp.concatenate([cache[...].astype(jnp.float32), jnp.zeros((MIX, HD - 40), jnp.float32)], axis=1)
    spots = jnp.transpose(spots)
    low = jnp.concatenate([spots[0:32], jnp.zeros((32, MIX), jnp.float32)], axis=1)
    high = jnp.concatenate([jnp.zeros((32, MIX), jnp.float32), spots[32:64]], axis=1)
    tile = (low + high).astype(jnp.bfloat16)
    for head in range(HEADS_SEC):
        q_out[head, 0:Q_OWN, :] = turn(queries[:, head * HD : (head + 1) * HD], tables)
        q_out[head, Q_OWN:Q_ROWS, :] = tile


def prepare_queries(qpos, queries, cache):
    return pl.pallas_call(
        prepare_queries_kernel,
        in_specs=[HERE] * 4,
        out_specs=HERE,
        out_shape=jax.ShapeDtypeStruct((HEADS_SEC, Q_ROWS, HD), jnp.bfloat16),
        compiler_params=pltpu.CompilerParams(vmem_limit_bytes=56 * MIB),
        cost_estimate=pl.CostEstimate(flops=1000000, bytes_accessed=400000, transcendentals=0),
        name="prepare_queries",
    )(qpos, jnp.asarray(frequency_row()), queries, cache.transpose(0, 1, 2, 4, 3).reshape(MIX, 40))


def prepare_pairs_kernel(kpos, freq, order, keys, values, mixing, kv_out):
    tables = turn_tables(kpos[...], freq[...])
    mixed = [
        jnp.dot(order[side], mixing[...], preferred_element_type=jnp.float32).astype(jnp.bfloat16)
        for side in range(2)
    ]
    for head in range(HEADS_SEC):
        cols = slice(head * HD, (head + 1) * HD)
        kv_out[head, 0:K_OWN, :] = turn(keys[:, cols], tables)
        value = values[:, cols]
        low = value[:V_ROWS]
        high = value[V_ROWS:]
        out = lax.dot_general(
            low, mixed[0][:, cols], (((1,), (1,)), ((), ())), preferred_element_type=jnp.float32
        )
        out = out + lax.dot_general(
            high, mixed[1][:, cols], (((1,), (1,)), ((), ())), preferred_element_type=jnp.float32
        )
        kv_out[head, K_OWN:KV_ROWS, :] = out.astype(jnp.bfloat16)


def prepare_pairs(kpos, keys, values, mixing):
    return pl.pallas_call(
        prepare_pairs_kernel,
        in_specs=[HERE] * 6,
        out_specs=HERE,
        out_shape=jax.ShapeDtypeStruct((HEADS_SEC, KV_ROWS, HD), jnp.bfloat16),
        compiler_params=pltpu.CompilerParams(vmem_limit_bytes=56 * MIB),
        cost_estimate=pl.CostEstimate(flops=50000000, bytes_accessed=900000, transcendentals=0),
        name="prepare_pairs",
    )(
        kpos,
        jnp.asarray(frequency_row()),
        jnp.asarray(row_order(), jnp.bfloat16),
        keys,
        values,
        mixing.T,
    )


def attend_kernel(*refs):
    place, q_refs, kv_refs, o_ref = refs[0], refs[1:5], refs[5:9], refs[9]
    q_buf, k_buf, v_buf, s_even, s_odd = refs[10:]
    lane = lax.broadcasted_iota(jnp.int32, (V_ROWS, HD), 1)
    ones = jnp.where(lane == MIX, 1.0, 0.0)
    for piece in range(4):
        for part in range(8):
            q_buf[piece * Q_BLOCK + part * Q_OWN : piece * Q_BLOCK + (part + 1) * Q_OWN] = q_refs[piece][part]

        def unpack(part, carry, piece=piece):
            at = pl.multiple_of(piece * 8 * K_OWN + part * K_OWN, 16)
            k_buf[pl.ds(at, K_OWN), :] = kv_refs[piece][part, 0:K_OWN, :]
            both = kv_refs[piece][part, K_OWN:KV_ROWS, :].astype(jnp.float32)
            v_buf[pl.ds(at, V_ROWS), :] = jnp.where(lane < MIX, both, ones).astype(jnp.bfloat16)
            other = pltpu.roll(both, MIX, 1)
            at = pl.multiple_of(piece * 8 * K_OWN + part * K_OWN + V_ROWS, 16)
            v_buf[pl.ds(at, V_ROWS), :] = jnp.where(lane < MIX, other, ones).astype(jnp.bfloat16)
            return carry

        lax.fori_loop(0, 8, unpack, 0)

    scale = jnp.float32(math.log2(math.e) / math.sqrt(HD))
    diagonal = lax.broadcasted_iota(jnp.int32, (GRID_W, HD), 1) == lax.broadcasted_iota(jnp.int32, (GRID_W, HD), 0)
    low_lane = lax.broadcasted_iota(jnp.int32, (HALF_W, HD), 1) < MIX

    def score(block):
        at = pl.multiple_of(block * SUB, 16)
        return lax.dot_general(
            q_buf[pl.ds(at, SUB), :], k_buf[...], (((1,), (1,)), ((), ())), preferred_element_type=jnp.float32
        )

    def finish(piece, block, s_ref):
        scores = s_ref[...]
        top = jnp.max(scores, axis=1, keepdims=True)
        weights = jnp.exp2((scores - top) * scale).astype(jnp.bfloat16)
        sums = jnp.dot(weights, v_buf[...], preferred_element_type=jnp.float32)
        total = sums[:, MIX : MIX + 1]
        mean = sums / total
        level = top * scale + jnp.log2(total)
        for patch_row in range(SUB // GRID_W):
            at = patch_row * GRID_W
            low = mean[at : at + HALF_W]
            high = pltpu.roll(mean[at + HALF_W : at + GRID_W], MIX, 1)
            packed = jnp.where(low_lane, low, high)
            line = jnp.sum(jnp.where(diagonal, level[at : at + GRID_W], 0.0), axis=0, keepdims=True)
            first = line.astype(jnp.bfloat16).astype(jnp.float32)
            line = line - first
            second = line.astype(jnp.bfloat16).astype(jnp.float32)
            third = line - second
            message = jnp.concatenate([packed, first, second, third, jnp.zeros((5, HD), jnp.float32)], axis=0)
            spot = block * (SUB // GRID_W) + patch_row
            o_ref[spot // 2, lax.rem(place[0] + piece, 4) * 2 + spot % 2] = message.astype(jnp.bfloat16)

    s_even[...] = score(0)
    blocks = FRAME // SUB

    def pair(step, carry):
        s_odd[...] = score(2 * step + 1)
        finish(step, 0, s_even)
        s_even[...] = score(jnp.minimum(2 * step + 2, blocks - 1))
        finish(step, 1, s_odd)
        return carry

    lax.fori_loop(0, blocks // 2, pair, 0)


def attend(place, queries, pairs):
    return pl.pallas_call(
        attend_kernel,
        in_specs=[pl.BlockSpec(memory_space=pltpu.SMEM)] + [HERE] * 8,
        out_specs=HERE,
        out_shape=jax.ShapeDtypeStruct((4, ROWS_BLOCK, MSG, HD), jnp.bfloat16),
        scratch_shapes=[
            pltpu.VMEM((FRAME, HD), jnp.bfloat16),
            pltpu.VMEM((KEYS_PART, HD), jnp.bfloat16),
            pltpu.VMEM((KEYS_PART, HD), jnp.bfloat16),
            pltpu.VMEM((SUB, KEYS_PART), jnp.float32),
            pltpu.VMEM((SUB, KEYS_PART), jnp.float32),
        ],
        compiler_params=pltpu.CompilerParams(vmem_limit_bytes=28 * MIB),
        cost_estimate=pl.CostEstimate(flops=4 * FRAME * KEYS_PART * HD, bytes_accessed=2000000, transcendentals=0),
        name="attend",
    )(place, *queries, *pairs)


def combine_kernel(r_ref, o_ref):
    shares = r_ref.shape[0]
    lane = lax.broadcasted_iota(jnp.int32, (HALF_W, HD), 1)
    row = lax.broadcasted_iota(jnp.int32, (HALF_W, HD), 0)
    zeros = jnp.zeros((16, HD), jnp.float32)
    low_lane = lax.broadcasted_iota(jnp.int32, (16, HD), 1) < MIX
    for patch_row in range(ROWS_BLOCK):
        blocks = [r_ref[share, patch_row].astype(jnp.float32) for share in range(shares)]
        levels = [b[HALF_W : HALF_W + 1] + b[HALF_W + 1 : HALF_W + 2] + b[HALF_W + 2 : HALF_W + 3] for b in blocks]
        top = levels[0]
        for level in levels[1:]:
            top = jnp.maximum(top, level)
        powers = [jnp.exp2(level - top) for level in levels]
        total = powers[0]
        for power in powers[1:]:
            total = total + power
        result = jnp.zeros((HALF_W, HD), jnp.float32)
        for block, power in zip(blocks, powers):
            weight = power / total
            low = jnp.sum(jnp.where(lane == row, weight, 0.0), axis=1, keepdims=True)
            high = jnp.sum(jnp.where(lane == row + HALF_W, weight, 0.0), axis=1, keepdims=True)
            result = result + jnp.where(lane < MIX, low, high) * block[:HALF_W]
        line = jnp.concatenate([zeros[:1], result, pltpu.roll(result, MIX, 1), zeros], axis=0)
        moved = pltpu.roll(line[: 2 * HALF_W + 16], MIX, 1)
        for tile in range(4):
            at = tile * TILE_W
            piece = jnp.where(low_lane, line[at : at + 16], moved[at + 11 : at + 27])
            piece = piece.astype(jnp.bfloat16)
            for copy in range(2):
                o_ref[patch_row // 2 * 8 + copy * 4 + tile, patch_row % 2] = piece


def combine(received):
    return pl.pallas_call(
        combine_kernel,
        in_specs=[HERE],
        out_specs=HERE,
        out_shape=jax.ShapeDtypeStruct((4 * ROWS_BLOCK, 2, 16, HD), jnp.bfloat16),
        compiler_params=pltpu.CompilerParams(vmem_limit_bytes=8 * MIB),
        cost_estimate=pl.CostEstimate(flops=1000000, bytes_accessed=900000, transcendentals=0),
        name="combine",
    )(received)


def from_ahead(value, axis, steps):
    return lax.ppermute(value, axis, [((spot + steps) % 4, spot) for spot in range(4)])


def outer_row(pair, axes, half):
    pairs = [(i, i + 8) for i in range(120) if i % 8 < 4] + [(i, i - 8) for i in range(8, 128) if i % 8 >= 4]
    return lax.ppermute(jnp.where(half == 0, pair[1], pair[0]), axes, pairs)


def cache_tile(tiles, half, tile_col):
    wide = jnp.concatenate([tiles[:, :, :MIX], tiles[:, :8, MIX:]], axis=1).reshape(2, 160, MIX)
    wide = jnp.pad(wide, ((0, 0), (1, 1), (0, 0)))
    wide = lax.dynamic_slice_in_dim(wide, tile_col * 40, 42, 1).reshape(2, 42, 2, 2, 16)
    wide = wide.transpose(0, 2, 3, 1, 4)
    near = outer_row(jnp.stack([wide[0, :, 0], wide[1, :, 1]]), SP, half)
    first = jnp.where(half == 0, near, wide[0, :, 1])
    last = jnp.where(half == 0, wide[1, :, 0], near)
    middle = jnp.where(half == 0, wide[0], wide[1])
    return jnp.concatenate([first[:, None], middle, last[:, None]], axis=1)


def on_device(queries, keys, values, query_positions, key_positions, mixing, kernel, bias, cache):
    sp_index = lax.axis_index(SP)
    section = lax.axis_index("sec")
    half = lax.axis_index("y") // 4
    tile_col = sp_index % 4
    tile_row = sp_index // 4
    own = lax.all_to_all(prepare_queries(query_positions, queries, cache), "y", 0, 0)
    q_own = own[:, :Q_OWN]
    kv_own = lax.all_to_all(prepare_pairs(key_positions, keys, values, mixing), "y", 0, 0)
    query_all = [q_own] + [from_ahead(q_own, "zh", step) for step in (1, 2, 3)]
    cached = cache_tile(own[:, Q_OWN:], half, tile_col)
    query_all, kv_own, cached = lax.optimization_barrier((query_all, kv_own, cached))
    pairs = [kv_own] + [from_ahead(kv_own, "x", step) for step in (1, 2, 3)]
    parts = attend(lax.axis_index("zh").reshape(1), query_all, pairs)
    shares = lax.all_to_all(parts, "zh", 0, 0)
    tiles = lax.all_to_all(combine(shares), ("sec", "y"), 0, 0)
    strip = jnp.sum(tiles.astype(jnp.float32), axis=0).astype(jnp.bfloat16)
    near = outer_row(strip, ("sec", "zh", "y"), half)
    strip = jnp.where(
        half == 0, jnp.stack([near, strip[0], strip[1]]), jnp.stack([strip[0], strip[1], near])
    )
    moved = []
    for step in range(3):
        pairs_at = [
            (((s * 4 + f) * 4 + z) * 8 + y, (((f + step) * 4 + s) * 4 + z) * 8 + y)
            for s in range(4)
            for f in range(4 - step)
            for z in range(4)
            for y in range(8)
        ]
        moved.append(lax.ppermute(strip, ALL, pairs_at))
    frames = jnp.stack([moved[2], moved[1], moved[0]])
    frames = frames.reshape(3, 3, 16, 2, MIX)[:, :, :11].transpose(0, 1, 3, 2, 4)
    frames = frames.reshape(3, 3, 22, 2, 2, 16).transpose(0, 1, 3, 2, 4, 5).reshape(3, 6, 44, 16)
    frames = frames[:, 1:5, 1:43]
    line = jnp.arange(4)[:, None, None]
    spot = jnp.arange(42)[None, :, None]
    outside = (
        ((tile_row == 0) & (line == 0))
        | ((tile_row == 31) & (line == 3))
        | ((tile_col == 0) & (spot == 0))
        | ((tile_col == 3) & (spot == 41))
    )
    frames = jnp.where(outside[None], jnp.zeros_like(frames), frames)
    minus_two = jnp.where(section >= 2, frames[0], jnp.where(section == 1, cached[1], cached[0]))
    minus_one = jnp.where(section >= 1, frames[1], cached[1])
    frames = jnp.stack([minus_two, minus_one, frames[2]])
    windows = [
        frames[step_t, step_y : step_y + 2, step_x : step_x + 40, :]
        for step_t in range(3)
        for step_y in range(3)
        for step_x in range(3)
    ]
    columns = jnp.stack(windows, axis=2).reshape(80, 27 * 16)
    output = jnp.dot(columns, kernel, preferred_element_type=jnp.float32) + bias[None, :]
    return output.reshape(1, 1, 2, 40, kernel.shape[1]).astype(jnp.bfloat16)


def solution(mesh):
    fine = Mesh(mesh.devices.reshape(4, 4, 4, 8), ALL)
    placed = (
        P(SP, "sec"),
        P(SP, "sec"),
        P(SP, "sec"),
        P(None, SP),
        P(None, SP),
        P("sec", None),
        P(),
        P(),
        P(None, SP, None, None, None),
    )
    return jax.shard_map(
        on_device,
        mesh=fine,
        in_specs=placed,
        out_specs=P("sec", SP, None, None, None),
        check_vma=False,
    )
```

```python
import math

import jax
import jax.numpy as jnp
import numpy as np
from jax import lax
from jax.experimental import pallas as pl
from jax.experimental.pallas import tpu as pltpu
from jax.sharding import Mesh
from jax.sharding import PartitionSpec as P

HD = 128
HEADS_SEC = 8
Q_OWN = 80
Q_ROWS = Q_OWN + 32
K_OWN = 96
V_ROWS = K_OWN // 2
KV_ROWS = K_OWN + V_ROWS
MIX = 64
GRID_W = 80
HALF_W = GRID_W // 2
FRAME = 2560
KEYS_PART = 3072
Q_BLOCK = 640
ROWS_BLOCK = Q_BLOCK // GRID_W
SUB = 320
STRIP = 24
MSG = HALF_W + 8
TILE_W = 20
ALL = ("sec", "x", "zh", "y")
SP = ("x", "zh", "y")
MIB = 1024 * 1024
HERE = pl.BlockSpec(memory_space=pltpu.VMEM)


def frequency_row():
    sixth = HD // 6
    time_pairs = (HD - 4 * sixth) // 2
    time = 10000.0 ** (-np.arange(time_pairs) / time_pairs)
    space = 10000.0 ** (-np.arange(sixth) / sixth)
    pairs = np.concatenate([time, space, space])
    return np.repeat(pairs, 2).astype(np.float32)[None, :]


def row_order():
    order = np.zeros((2, 2 * MIX, MIX), np.float32)
    for ch in range(16):
        for ab in range(4):
            for side in range(2):
                order[side, side * MIX + ab * 16 + ch, ch * 4 + ab] = 1.0
    return order


def turn_tables(positions, freq):
    count = positions.shape[1]
    spot = positions.astype(jnp.float32)
    same = lax.broadcasted_iota(jnp.int32, (count, count), 0) == lax.broadcasted_iota(jnp.int32, (count, count), 1)
    column = [jnp.sum(jnp.where(same, spot[i : i + 1], 0.0), axis=1, keepdims=True) for i in range(3)]
    lane = lax.broadcasted_iota(jnp.int32, (count, HD), 1)
    base = jnp.where(lane < 44, column[0], jnp.where(lane < 86, column[1], column[2]))
    angle = base * freq
    cosine = jnp.cos(angle)
    sine = jnp.sin(angle)
    even = lax.rem(lane, 2) == 0
    zero = jnp.zeros_like(sine)
    return cosine, jnp.where(even, -sine, zero), jnp.where(even, zero, sine)


def turn(vectors, tables):
    cosine, from_next, from_last = tables
    wide = vectors.astype(jnp.float32)
    out = wide * cosine + pltpu.roll(wide, HD - 1, 1) * from_next + pltpu.roll(wide, 1, 1) * from_last
    return out.astype(jnp.bfloat16)


def prepare_queries_kernel(qpos, freq, queries, cache, q_out):
    tables = turn_tables(qpos[...], freq[...])
    spots = jnp.concatenate([cache[...].astype(jnp.float32), jnp.zeros((MIX, HD - 40), jnp.float32)], axis=1)
    spots = jnp.transpose(spots)
    low = jnp.concatenate([spots[0:32], jnp.zeros((32, MIX), jnp.float32)], axis=1)
    high = jnp.concatenate([jnp.zeros((32, MIX), jnp.float32), spots[32:64]], axis=1)
    tile = (low + high).astype(jnp.bfloat16)
    for head in range(HEADS_SEC):
        q_out[head, 0:Q_OWN, :] = turn(queries[:, head * HD : (head + 1) * HD], tables)
        q_out[head, Q_OWN:Q_ROWS, :] = tile


def prepare_queries(qpos, queries, cache):
    return pl.pallas_call(
        prepare_queries_kernel,
        in_specs=[HERE] * 4,
        out_specs=HERE,
        out_shape=jax.ShapeDtypeStruct((HEADS_SEC, Q_ROWS, HD), jnp.bfloat16),
        compiler_params=pltpu.CompilerParams(vmem_limit_bytes=56 * MIB),
        cost_estimate=pl.CostEstimate(flops=1000000, bytes_accessed=400000, transcendentals=0),
        name="prepare_queries",
    )(qpos, jnp.asarray(frequency_row()), queries, cache.transpose(0, 1, 2, 4, 3).reshape(MIX, 40))


def prepare_pairs_kernel(kpos, freq, order, keys, values, mixing, kv_out):
    tables = turn_tables(kpos[...], freq[...])
    mixed = [
        jnp.dot(order[side], mixing[...], preferred_element_type=jnp.float32).astype(jnp.bfloat16)
        for side in range(2)
    ]
    for head in range(HEADS_SEC):
        cols = slice(head * HD, (head + 1) * HD)
        kv_out[head, 0:K_OWN, :] = turn(keys[:, cols], tables)
        value = values[:, cols]
        low = value[:V_ROWS]
        high = value[V_ROWS:]
        out = lax.dot_general(
            low, mixed[0][:, cols], (((1,), (1,)), ((), ())), preferred_element_type=jnp.float32
        )
        out = out + lax.dot_general(
            high, mixed[1][:, cols], (((1,), (1,)), ((), ())), preferred_element_type=jnp.float32
        )
        kv_out[head, K_OWN:KV_ROWS, :] = out.astype(jnp.bfloat16)


def prepare_pairs(kpos, keys, values, mixing):
    return pl.pallas_call(
        prepare_pairs_kernel,
        in_specs=[HERE] * 6,
        out_specs=HERE,
        out_shape=jax.ShapeDtypeStruct((HEADS_SEC, KV_ROWS, HD), jnp.bfloat16),
        compiler_params=pltpu.CompilerParams(vmem_limit_bytes=56 * MIB),
        cost_estimate=pl.CostEstimate(flops=50000000, bytes_accessed=900000, transcendentals=0),
        name="prepare_pairs",
    )(
        kpos,
        jnp.asarray(frequency_row()),
        jnp.asarray(row_order(), jnp.bfloat16),
        keys,
        values,
        mixing.T,
    )


def attend_kernel(*refs):
    place, q_refs, kv_refs, o_ref = refs[0], refs[1:6], refs[6:10], refs[10]
    q_buf, k_buf, v_buf, s_even, s_odd = refs[11:]
    lane = lax.broadcasted_iota(jnp.int32, (V_ROWS, HD), 1)
    ones = jnp.where(lane == MIX, 1.0, 0.0)
    spot = 0
    for q_ref in q_refs:
        for part in range(q_ref.shape[0]):
            q_buf[spot : spot + Q_OWN] = q_ref[part]
            spot += Q_OWN
    for piece in range(4):

        def unpack(part, carry, piece=piece):
            at = pl.multiple_of(piece * 8 * K_OWN + part * K_OWN, 16)
            k_buf[pl.ds(at, K_OWN), :] = kv_refs[piece][part, 0:K_OWN, :]
            both = kv_refs[piece][part, K_OWN:KV_ROWS, :].astype(jnp.float32)
            v_buf[pl.ds(at, V_ROWS), :] = jnp.where(lane < MIX, both, ones).astype(jnp.bfloat16)
            other = pltpu.roll(both, MIX, 1)
            at = pl.multiple_of(piece * 8 * K_OWN + part * K_OWN + V_ROWS, 16)
            v_buf[pl.ds(at, V_ROWS), :] = jnp.where(lane < MIX, other, ones).astype(jnp.bfloat16)
            return carry

        lax.fori_loop(0, 8, unpack, 0)

    scale = jnp.float32(math.log2(math.e) / math.sqrt(HD))
    diagonal = lax.broadcasted_iota(jnp.int32, (GRID_W, HD), 1) == lax.broadcasted_iota(jnp.int32, (GRID_W, HD), 0)
    low_lane = lax.broadcasted_iota(jnp.int32, (HALF_W, HD), 1) < MIX

    def score(block):
        at = pl.multiple_of(block * SUB, 16)
        return lax.dot_general(
            q_buf[pl.ds(at, SUB), :], k_buf[...], (((1,), (1,)), ((), ())), preferred_element_type=jnp.float32
        )

    def finish(piece, block, s_ref):
        scores = s_ref[...]
        top = jnp.max(scores, axis=1, keepdims=True)
        weights = jnp.exp2((scores - top) * scale).astype(jnp.bfloat16)
        sums = jnp.dot(weights, v_buf[...], preferred_element_type=jnp.float32)
        total = sums[:, MIX : MIX + 1]
        mean = sums / total
        level = top * scale + jnp.log2(total)
        for patch_row in range(SUB // GRID_W):
            at = patch_row * GRID_W
            low = mean[at : at + HALF_W]
            high = pltpu.roll(mean[at + HALF_W : at + GRID_W], MIX, 1)
            packed = jnp.where(low_lane, low, high)
            line = jnp.sum(jnp.where(diagonal, level[at : at + GRID_W], 0.0), axis=0, keepdims=True)
            first = line.astype(jnp.bfloat16).astype(jnp.float32)
            line = line - first
            second = line.astype(jnp.bfloat16).astype(jnp.float32)
            third = line - second
            message = jnp.concatenate([packed, first, second, third, jnp.zeros((5, HD), jnp.float32)], axis=0)
            spot = block * (SUB // GRID_W) + patch_row
            o_ref[spot // 2, lax.rem(place[0] + piece, 4) * 2 + spot % 2] = message.astype(jnp.bfloat16)

    s_even[...] = score(0)
    blocks = FRAME // SUB

    def pair(step, carry):
        s_odd[...] = score(2 * step + 1)
        finish(step, 0, s_even)
        s_even[...] = score(jnp.minimum(2 * step + 2, blocks - 1))
        finish(step, 1, s_odd)
        return carry

    lax.fori_loop(0, blocks // 2, pair, 0)


def attend(place, queries, pairs):
    return pl.pallas_call(
        attend_kernel,
        in_specs=[pl.BlockSpec(memory_space=pltpu.SMEM)] + [HERE] * 9,
        out_specs=HERE,
        out_shape=jax.ShapeDtypeStruct((4, ROWS_BLOCK, MSG, HD), jnp.bfloat16),
        scratch_shapes=[
            pltpu.VMEM((FRAME, HD), jnp.bfloat16),
            pltpu.VMEM((KEYS_PART, HD), jnp.bfloat16),
            pltpu.VMEM((KEYS_PART, HD), jnp.bfloat16),
            pltpu.VMEM((SUB, KEYS_PART), jnp.float32),
            pltpu.VMEM((SUB, KEYS_PART), jnp.float32),
        ],
        compiler_params=pltpu.CompilerParams(vmem_limit_bytes=28 * MIB),
        cost_estimate=pl.CostEstimate(flops=4 * FRAME * KEYS_PART * HD, bytes_accessed=2000000, transcendentals=0),
        name="attend",
    )(place, *queries, *pairs)


def combine_kernel(r_ref, o_ref):
    shares = r_ref.shape[0]
    lane = lax.broadcasted_iota(jnp.int32, (HALF_W, HD), 1)
    row = lax.broadcasted_iota(jnp.int32, (HALF_W, HD), 0)
    zeros = jnp.zeros((16, HD), jnp.float32)
    low_lane = lax.broadcasted_iota(jnp.int32, (STRIP, HD), 1) < MIX
    lines = []
    for patch_row in range(ROWS_BLOCK):
        blocks = [r_ref[share, patch_row].astype(jnp.float32) for share in range(shares)]
        levels = [b[HALF_W : HALF_W + 1] + b[HALF_W + 1 : HALF_W + 2] + b[HALF_W + 2 : HALF_W + 3] for b in blocks]
        top = levels[0]
        for level in levels[1:]:
            top = jnp.maximum(top, level)
        powers = [jnp.exp2(level - top) for level in levels]
        total = powers[0]
        for power in powers[1:]:
            total = total + power
        result = jnp.zeros((HALF_W, HD), jnp.float32)
        for block, power in zip(blocks, powers):
            weight = power / total
            low = jnp.sum(jnp.where(lane == row, weight, 0.0), axis=1, keepdims=True)
            high = jnp.sum(jnp.where(lane == row + HALF_W, weight, 0.0), axis=1, keepdims=True)
            result = result + jnp.where(lane < MIX, low, high) * block[:HALF_W]
        line = jnp.concatenate([zeros[:1], result, pltpu.roll(result, MIX, 1), zeros], axis=0)
        line = line[: 2 * HALF_W + 16]
        lines.append(line if patch_row % 2 == 0 else pltpu.roll(line, MIX, 1))
    for group in range(4):
        for tile in range(4):
            at = tile * TILE_W
            piece = jnp.where(low_lane, lines[2 * group][at : at + STRIP], lines[2 * group + 1][at : at + STRIP])
            piece = piece.astype(jnp.bfloat16)
            for copy in range(2):
                o_ref[group * 8 + copy * 4 + tile] = piece


def combine(received):
    return pl.pallas_call(
        combine_kernel,
        in_specs=[HERE],
        out_specs=HERE,
        out_shape=jax.ShapeDtypeStruct((4 * ROWS_BLOCK, STRIP, HD), jnp.bfloat16),
        compiler_params=pltpu.CompilerParams(vmem_limit_bytes=8 * MIB),
        cost_estimate=pl.CostEstimate(flops=1000000, bytes_accessed=900000, transcendentals=0),
        name="combine",
    )(received)


def from_ahead(value, axis, steps):
    return lax.ppermute(value, axis, [((spot + steps) % 4, spot) for spot in range(4)])


def next_pair(value, axes):
    pairs = [(i, i + 8) for i in range(120) if i % 8 < 4] + [(i, i - 8) for i in range(8, 128) if i % 8 >= 4]
    return lax.ppermute(value, axes, pairs)


def cache_tile(tiles, half, tile_col):
    wide = jnp.concatenate([tiles[:, :, :MIX], tiles[:, :8, MIX:]], axis=1).reshape(2, 160, MIX)
    wide = jnp.pad(wide, ((0, 0), (1, 1), (0, 0)))
    wide = lax.dynamic_slice_in_dim(wide, tile_col * 40, 42, 1).reshape(2, 42, 2, 2, 16)
    wide = wide.transpose(0, 2, 3, 1, 4)
    near = next_pair(jnp.where(half == 0, wide[1, :, 1], wide[0, :, 0]), SP)
    first = jnp.where(half == 0, near, wide[0, :, 1])
    last = jnp.where(half == 0, wide[1, :, 0], near)
    middle = jnp.where(half == 0, wide[0], wide[1])
    return jnp.concatenate([first[:, None], middle, last[:, None]], axis=1)


def on_device(queries, keys, values, query_positions, key_positions, mixing, kernel, bias, cache):
    sp_index = lax.axis_index(SP)
    section = lax.axis_index("sec")
    half = lax.axis_index("y") // 4
    tile_col = sp_index % 4
    tile_row = sp_index // 4
    own = lax.all_to_all(prepare_queries(query_positions, queries, cache), "y", 0, 0)
    q_own = own[:, :Q_OWN]
    kv_own = lax.all_to_all(prepare_pairs(key_positions, keys, values, mixing), "y", 0, 0)
    q_next = from_ahead(q_own, "zh", 1)
    q_last = from_ahead(q_own, "zh", 3)
    cached = cache_tile(own[:, Q_OWN:], half, tile_col)
    kv_own, cached, q_next, q_last = lax.optimization_barrier((kv_own, cached, q_next, q_last))
    q_far = [from_ahead(q_last[:4], "zh", 3), from_ahead(q_next[4:], "zh", 1)]
    query_all = [q_own, q_next, *q_far, q_last]
    pairs = [kv_own] + [from_ahead(kv_own, "x", step) for step in (1, 2, 3)]
    parts = attend(lax.axis_index("zh").reshape(1), query_all, pairs)
    shares = lax.all_to_all(parts, "zh", 0, 0)
    tiles = lax.all_to_all(combine(shares), ("sec", "y"), 0, 0)
    strip = jnp.sum(tiles.astype(jnp.float32), axis=0).astype(jnp.bfloat16)
    strip = jnp.stack([strip, next_pair(strip, ("sec", "zh", "y"))])
    moved = []
    for step in range(3):
        pairs_at = [
            (((s * 4 + f) * 4 + z) * 8 + y, (((f + step) * 4 + s) * 4 + z) * 8 + y)
            for s in range(4)
            for f in range(4 - step)
            for z in range(4)
            for y in range(8)
        ]
        moved.append(lax.ppermute(strip, ALL, pairs_at))
    frames = jnp.stack([moved[2], moved[1], moved[0]])
    own, near = frames[:, 0, :22], frames[:, 1, :22]
    low, high = own[:, :, :MIX], own[:, :, MIX:]
    first = jnp.where(half == 0, near[:, :, MIX:], low)
    middle = jnp.where(half == 0, low, high)
    last = jnp.where(half == 0, high, near[:, :, :MIX])
    frames = jnp.stack([first, middle, last], axis=1)
    frames = frames.reshape(3, 3, 22, 2, 2, 16).transpose(0, 1, 3, 2, 4, 5).reshape(3, 6, 44, 16)
    frames = frames[:, 1:5, 1:43]
    line = jnp.arange(4)[:, None, None]
    spot = jnp.arange(42)[None, :, None]
    outside = (
        ((tile_row == 0) & (line == 0))
        | ((tile_row == 31) & (line == 3))
        | ((tile_col == 0) & (spot == 0))
        | ((tile_col == 3) & (spot == 41))
    )
    frames = jnp.where(outside[None], jnp.zeros_like(frames), frames)
    minus_two = jnp.where(section >= 2, frames[0], jnp.where(section == 1, cached[1], cached[0]))
    minus_one = jnp.where(section >= 1, frames[1], cached[1])
    frames = jnp.stack([minus_two, minus_one, frames[2]])
    windows = [
        frames[step_t, step_y : step_y + 2, step_x : step_x + 40, :]
        for step_t in range(3)
        for step_y in range(3)
        for step_x in range(3)
    ]
    columns = jnp.stack(windows, axis=2).reshape(80, 27 * 16)
    output = jnp.dot(columns, kernel, preferred_element_type=jnp.float32) + bias[None, :]
    return output.reshape(1, 1, 2, 40, kernel.shape[1]).astype(jnp.bfloat16)


def solution(mesh):
    fine = Mesh(mesh.devices.reshape(4, 4, 4, 8), ALL)
    placed = (
        P(SP, "sec"),
        P(SP, "sec"),
        P(SP, "sec"),
        P(None, SP),
        P(None, SP),
        P("sec", None),
        P(),
        P(),
        P(None, SP, None, None, None),
    )
    return jax.shard_map(
        on_device,
        mesh=fine,
        in_specs=placed,
        out_specs=P("sec", SP, None, None, None),
        check_vma=False,
    )
```

```python
import math

import jax
import jax.numpy as jnp
import numpy as np
from jax import lax
from jax.experimental import pallas as pl
from jax.experimental.pallas import tpu as pltpu
from jax.sharding import Mesh
from jax.sharding import PartitionSpec as P

HD = 128
HEADS_SEC = 8
Q_OWN = 80
K_OWN = 96
V_ROWS = K_OWN // 2
KV_ROWS = K_OWN + V_ROWS
OWN_ROWS = KV_ROWS + Q_OWN + 32
MIX = 64
GRID_W = 80
HALF_W = GRID_W // 2
FRAME = 2560
KEYS_PART = 3072
Q_BLOCK = 640
ROWS_BLOCK = Q_BLOCK // GRID_W
SUB = 320
STRIP = 24
MSG = HALF_W + 8
TILE_W = 20
ALL = ("sec", "x", "zh", "y")
SP = ("x", "zh", "y")
MIB = 1024 * 1024
HERE = pl.BlockSpec(memory_space=pltpu.VMEM)


def frequency_row():
    sixth = HD // 6
    time_pairs = (HD - 4 * sixth) // 2
    time = 10000.0 ** (-np.arange(time_pairs) / time_pairs)
    space = 10000.0 ** (-np.arange(sixth) / sixth)
    pairs = np.concatenate([time, space, space])
    return np.repeat(pairs, 2).astype(np.float32)[None, :]


def row_order():
    order = np.zeros((2, 2 * MIX, MIX), np.float32)
    for ch in range(16):
        for ab in range(4):
            for side in range(2):
                order[side, side * MIX + ab * 16 + ch, ch * 4 + ab] = 1.0
    return order


def turn_tables(positions, freq):
    count = positions.shape[1]
    spot = positions.astype(jnp.float32)
    same = lax.broadcasted_iota(jnp.int32, (count, count), 0) == lax.broadcasted_iota(jnp.int32, (count, count), 1)
    column = [jnp.sum(jnp.where(same, spot[i : i + 1], 0.0), axis=1, keepdims=True) for i in range(3)]
    lane = lax.broadcasted_iota(jnp.int32, (count, HD), 1)
    base = jnp.where(lane < 44, column[0], jnp.where(lane < 86, column[1], column[2]))
    angle = base * freq
    cosine = jnp.cos(angle)
    sine = jnp.sin(angle)
    even = lax.rem(lane, 2) == 0
    zero = jnp.zeros_like(sine)
    return cosine, jnp.where(even, -sine, zero), jnp.where(even, zero, sine)


def turn(vectors, tables):
    cosine, from_next, from_last = tables
    wide = vectors.astype(jnp.float32)
    out = wide * cosine + pltpu.roll(wide, HD - 1, 1) * from_next + pltpu.roll(wide, 1, 1) * from_last
    return out.astype(jnp.bfloat16)


def prepare_kernel(qpos, kpos, freq, order, queries, keys, values, mixing, cache, out):
    q_tables = turn_tables(qpos[...], freq[...])
    k_tables = turn_tables(kpos[...], freq[...])
    spots = jnp.concatenate([cache[...].astype(jnp.float32), jnp.zeros((MIX, HD - 40), jnp.float32)], axis=1)
    spots = jnp.transpose(spots)
    low = jnp.concatenate([spots[0:32], jnp.zeros((32, MIX), jnp.float32)], axis=1)
    high = jnp.concatenate([jnp.zeros((32, MIX), jnp.float32), spots[32:64]], axis=1)
    tile = (low + high).astype(jnp.bfloat16)
    mixed = [
        jnp.dot(order[side], mixing[...], preferred_element_type=jnp.float32).astype(jnp.bfloat16)
        for side in range(2)
    ]
    for head in range(HEADS_SEC):
        cols = slice(head * HD, (head + 1) * HD)
        out[head, 0:K_OWN, :] = turn(keys[:, cols], k_tables)
        value = values[:, cols]
        mix_low = lax.dot_general(
            value[:V_ROWS], mixed[0][:, cols], (((1,), (1,)), ((), ())), preferred_element_type=jnp.float32
        )
        mix_high = lax.dot_general(
            value[V_ROWS:], mixed[1][:, cols], (((1,), (1,)), ((), ())), preferred_element_type=jnp.float32
        )
        out[head, K_OWN:KV_ROWS, :] = (mix_low + mix_high).astype(jnp.bfloat16)
        out[head, KV_ROWS : KV_ROWS + Q_OWN, :] = turn(queries[:, cols], q_tables)
        out[head, KV_ROWS + Q_OWN : OWN_ROWS, :] = tile


def prepare(qpos, kpos, queries, keys, values, mixing, cache):
    return pl.pallas_call(
        prepare_kernel,
        in_specs=[HERE] * 9,
        out_specs=HERE,
        out_shape=jax.ShapeDtypeStruct((HEADS_SEC, OWN_ROWS, HD), jnp.bfloat16),
        compiler_params=pltpu.CompilerParams(vmem_limit_bytes=56 * MIB),
        cost_estimate=pl.CostEstimate(flops=50000000, bytes_accessed=1200000, transcendentals=0),
        name="prepare",
    )(
        qpos,
        kpos,
        jnp.asarray(frequency_row()),
        jnp.asarray(row_order(), jnp.bfloat16),
        queries,
        keys,
        values,
        mixing.T,
        cache.transpose(0, 1, 2, 4, 3).reshape(MIX, 40),
    )


def attend_kernel(*refs):
    place, q_refs, kv_refs, o_ref = refs[0], refs[1:6], refs[6:10], refs[10]
    q_buf, k_buf, v_buf, s_even, s_odd = refs[11:]
    lane = lax.broadcasted_iota(jnp.int32, (V_ROWS, HD), 1)
    ones = jnp.where(lane == MIX, 1.0, 0.0)
    spot = 0
    for q_ref in q_refs:
        for part in range(q_ref.shape[0]):
            q_buf[spot : spot + Q_OWN] = q_ref[part]
            spot += Q_OWN
    for piece in range(4):

        def unpack(part, carry, piece=piece):
            at = pl.multiple_of(piece * 8 * K_OWN + part * K_OWN, 16)
            k_buf[pl.ds(at, K_OWN), :] = kv_refs[piece][part, 0:K_OWN, :]
            both = kv_refs[piece][part, K_OWN:KV_ROWS, :].astype(jnp.float32)
            v_buf[pl.ds(at, V_ROWS), :] = jnp.where(lane < MIX, both, ones).astype(jnp.bfloat16)
            other = pltpu.roll(both, MIX, 1)
            at = pl.multiple_of(piece * 8 * K_OWN + part * K_OWN + V_ROWS, 16)
            v_buf[pl.ds(at, V_ROWS), :] = jnp.where(lane < MIX, other, ones).astype(jnp.bfloat16)
            return carry

        lax.fori_loop(0, 8, unpack, 0)

    scale = jnp.float32(math.log2(math.e) / math.sqrt(HD))
    diagonal = lax.broadcasted_iota(jnp.int32, (GRID_W, HD), 1) == lax.broadcasted_iota(jnp.int32, (GRID_W, HD), 0)
    low_lane = lax.broadcasted_iota(jnp.int32, (HALF_W, HD), 1) < MIX

    def score(block):
        at = pl.multiple_of(block * SUB, 16)
        return lax.dot_general(
            q_buf[pl.ds(at, SUB), :], k_buf[...], (((1,), (1,)), ((), ())), preferred_element_type=jnp.float32
        )

    def finish(piece, block, s_ref):
        scores = s_ref[...]
        top = jnp.max(scores, axis=1, keepdims=True)
        weights = jnp.exp2((scores - top) * scale).astype(jnp.bfloat16)
        sums = jnp.dot(weights, v_buf[...], preferred_element_type=jnp.float32)
        total = sums[:, MIX : MIX + 1]
        mean = sums / total
        level = top * scale + jnp.log2(total)
        for patch_row in range(SUB // GRID_W):
            at = patch_row * GRID_W
            low = mean[at : at + HALF_W]
            high = pltpu.roll(mean[at + HALF_W : at + GRID_W], MIX, 1)
            packed = jnp.where(low_lane, low, high)
            line = jnp.sum(jnp.where(diagonal, level[at : at + GRID_W], 0.0), axis=0, keepdims=True)
            first = line.astype(jnp.bfloat16).astype(jnp.float32)
            line = line - first
            second = line.astype(jnp.bfloat16).astype(jnp.float32)
            third = line - second
            message = jnp.concatenate([packed, first, second, third, jnp.zeros((5, HD), jnp.float32)], axis=0)
            spot = block * (SUB // GRID_W) + patch_row
            o_ref[spot // 2, lax.rem(place[0] + piece, 4) * 2 + spot % 2] = message.astype(jnp.bfloat16)

    s_even[...] = score(0)
    blocks = FRAME // SUB

    def pair(step, carry):
        s_odd[...] = score(2 * step + 1)
        finish(step, 0, s_even)
        s_even[...] = score(jnp.minimum(2 * step + 2, blocks - 1))
        finish(step, 1, s_odd)
        return carry

    lax.fori_loop(0, blocks // 2, pair, 0)


def attend(place, queries, pairs):
    return pl.pallas_call(
        attend_kernel,
        in_specs=[pl.BlockSpec(memory_space=pltpu.SMEM)] + [HERE] * 9,
        out_specs=HERE,
        out_shape=jax.ShapeDtypeStruct((4, ROWS_BLOCK, MSG, HD), jnp.bfloat16),
        scratch_shapes=[
            pltpu.VMEM((FRAME, HD), jnp.bfloat16),
            pltpu.VMEM((KEYS_PART, HD), jnp.bfloat16),
            pltpu.VMEM((KEYS_PART, HD), jnp.bfloat16),
            pltpu.VMEM((SUB, KEYS_PART), jnp.float32),
            pltpu.VMEM((SUB, KEYS_PART), jnp.float32),
        ],
        compiler_params=pltpu.CompilerParams(vmem_limit_bytes=28 * MIB),
        cost_estimate=pl.CostEstimate(flops=4 * FRAME * KEYS_PART * HD, bytes_accessed=2000000, transcendentals=0),
        name="attend",
    )(place, *queries, *pairs)


def combine_kernel(r_ref, o_ref):
    shares = r_ref.shape[0]
    lane = lax.broadcasted_iota(jnp.int32, (HALF_W, HD), 1)
    row = lax.broadcasted_iota(jnp.int32, (HALF_W, HD), 0)
    zeros = jnp.zeros((16, HD), jnp.float32)
    low_lane = lax.broadcasted_iota(jnp.int32, (STRIP, HD), 1) < MIX
    lines = []
    for patch_row in range(ROWS_BLOCK):
        blocks = [r_ref[share, patch_row].astype(jnp.float32) for share in range(shares)]
        levels = [b[HALF_W : HALF_W + 1] + b[HALF_W + 1 : HALF_W + 2] + b[HALF_W + 2 : HALF_W + 3] for b in blocks]
        top = levels[0]
        for level in levels[1:]:
            top = jnp.maximum(top, level)
        powers = [jnp.exp2(level - top) for level in levels]
        total = powers[0]
        for power in powers[1:]:
            total = total + power
        result = jnp.zeros((HALF_W, HD), jnp.float32)
        for block, power in zip(blocks, powers):
            weight = power / total
            low = jnp.sum(jnp.where(lane == row, weight, 0.0), axis=1, keepdims=True)
            high = jnp.sum(jnp.where(lane == row + HALF_W, weight, 0.0), axis=1, keepdims=True)
            result = result + jnp.where(lane < MIX, low, high) * block[:HALF_W]
        line = jnp.concatenate([zeros[:1], result, pltpu.roll(result, MIX, 1), zeros], axis=0)
        line = line[: 2 * HALF_W + 16]
        lines.append(line if patch_row % 2 == 0 else pltpu.roll(line, MIX, 1))
    for group in range(4):
        for tile in range(4):
            at = tile * TILE_W
            piece = jnp.where(low_lane, lines[2 * group][at : at + STRIP], lines[2 * group + 1][at : at + STRIP])
            piece = piece.astype(jnp.bfloat16)
            for copy in range(2):
                o_ref[group * 8 + copy * 4 + tile] = piece


def combine(received):
    return pl.pallas_call(
        combine_kernel,
        in_specs=[HERE],
        out_specs=HERE,
        out_shape=jax.ShapeDtypeStruct((4 * ROWS_BLOCK, STRIP, HD), jnp.bfloat16),
        compiler_params=pltpu.CompilerParams(vmem_limit_bytes=8 * MIB),
        cost_estimate=pl.CostEstimate(flops=1000000, bytes_accessed=900000, transcendentals=0),
        name="combine",
    )(received)


def from_ahead(value, axis, steps):
    return lax.ppermute(value, axis, [((spot + steps) % 4, spot) for spot in range(4)])


def next_pair(value, axes):
    pairs = [(i, i + 8) for i in range(120) if i % 8 < 4] + [(i, i - 8) for i in range(8, 128) if i % 8 >= 4]
    return lax.ppermute(value, axes, pairs)


def cache_tile(tiles, half, tile_col):
    wide = jnp.concatenate([tiles[:, :, :MIX], tiles[:, :8, MIX:]], axis=1).reshape(2, 160, MIX)
    wide = jnp.pad(wide, ((0, 0), (1, 1), (0, 0)))
    wide = lax.dynamic_slice_in_dim(wide, tile_col * 40, 42, 1).reshape(2, 42, 2, 2, 16)
    wide = wide.transpose(0, 2, 3, 1, 4)
    near = next_pair(jnp.where(half == 0, wide[1, :, 1], wide[0, :, 0]), SP)
    first = jnp.where(half == 0, near, wide[0, :, 1])
    last = jnp.where(half == 0, wide[1, :, 0], near)
    middle = jnp.where(half == 0, wide[0], wide[1])
    return jnp.concatenate([first[:, None], middle, last[:, None]], axis=1)


def on_device(queries, keys, values, query_positions, key_positions, mixing, kernel, bias, cache):
    sp_index = lax.axis_index(SP)
    section = lax.axis_index("sec")
    half = lax.axis_index("y") // 4
    tile_col = sp_index % 4
    tile_row = sp_index // 4
    own = prepare(query_positions, key_positions, queries, keys, values, mixing, cache)
    own = lax.all_to_all(own, "y", 0, 0)
    kv_own = own[:, :KV_ROWS]
    q_own = own[:, KV_ROWS : KV_ROWS + Q_OWN]
    q_next = from_ahead(q_own, "zh", 1)
    q_last = from_ahead(q_own, "zh", 3)
    pairs = [kv_own] + [from_ahead(kv_own, "x", step) for step in (1, 2, 3)]
    tiles, q_next, q_last = lax.optimization_barrier((own[:, KV_ROWS + Q_OWN :], q_next, q_last))
    q_far = [from_ahead(q_last[:4], "zh", 3), from_ahead(q_next[4:], "zh", 1)]
    query_all = [q_own, q_next, *q_far, q_last]
    cached = cache_tile(tiles, half, tile_col)
    query_all, pairs, cached = lax.optimization_barrier((query_all, pairs, cached))
    parts = attend(lax.axis_index("zh").reshape(1), query_all, pairs)
    shares = lax.all_to_all(parts, "zh", 0, 0)
    tiles = lax.all_to_all(combine(shares), ("sec", "y"), 0, 0)
    strip = jnp.sum(tiles.astype(jnp.float32), axis=0).astype(jnp.bfloat16)
    strip = jnp.stack([strip, next_pair(strip, ("sec", "zh", "y"))])
    moved = []
    for step in range(3):
        pairs_at = [
            (((s * 4 + f) * 4 + z) * 8 + y, (((f + step) * 4 + s) * 4 + z) * 8 + y)
            for s in range(4)
            for f in range(4 - step)
            for z in range(4)
            for y in range(8)
        ]
        moved.append(lax.ppermute(strip, ALL, pairs_at))
    frames = jnp.stack([moved[2], moved[1], moved[0]])
    own, near = frames[:, 0, :22], frames[:, 1, :22]
    low, high = own[:, :, :MIX], own[:, :, MIX:]
    first = jnp.where(half == 0, near[:, :, MIX:], low)
    middle = jnp.where(half == 0, low, high)
    last = jnp.where(half == 0, high, near[:, :, :MIX])
    frames = jnp.stack([first, middle, last], axis=1)
    frames = frames.reshape(3, 3, 22, 2, 2, 16).transpose(0, 1, 3, 2, 4, 5).reshape(3, 6, 44, 16)
    frames = frames[:, 1:5, 1:43]
    line = jnp.arange(4)[:, None, None]
    spot = jnp.arange(42)[None, :, None]
    outside = (
        ((tile_row == 0) & (line == 0))
        | ((tile_row == 31) & (line == 3))
        | ((tile_col == 0) & (spot == 0))
        | ((tile_col == 3) & (spot == 41))
    )
    frames = jnp.where(outside[None], jnp.zeros_like(frames), frames)
    minus_two = jnp.where(section >= 2, frames[0], jnp.where(section == 1, cached[1], cached[0]))
    minus_one = jnp.where(section >= 1, frames[1], cached[1])
    frames = jnp.stack([minus_two, minus_one, frames[2]])
    windows = [
        frames[step_t, step_y : step_y + 2, step_x : step_x + 40, :]
        for step_t in range(3)
        for step_y in range(3)
        for step_x in range(3)
    ]
    columns = jnp.stack(windows, axis=2).reshape(80, 27 * 16)
    output = jnp.dot(columns, kernel, preferred_element_type=jnp.float32) + bias[None, :]
    return output.reshape(1, 1, 2, 40, kernel.shape[1]).astype(jnp.bfloat16)


def solution(mesh):
    fine = Mesh(mesh.devices.reshape(4, 4, 4, 8), ALL)
    placed = (
        P(SP, "sec"),
        P(SP, "sec"),
        P(SP, "sec"),
        P(None, SP),
        P(None, SP),
        P("sec", None),
        P(),
        P(),
        P(None, SP, None, None, None),
    )
    return jax.shard_map(
        on_device,
        mesh=fine,
        in_specs=placed,
        out_specs=P("sec", SP, None, None, None),
        check_vma=False,
    )
```

```python
import math

import jax
import jax.numpy as jnp
import numpy as np
from jax import lax
from jax.experimental import pallas as pl
from jax.experimental.pallas import tpu as pltpu
from jax.sharding import Mesh
from jax.sharding import PartitionSpec as P

HD = 128
HEADS_SEC = 8
Q_OWN = 80
K_OWN = 96
V_ROWS = K_OWN // 2
KV_ROWS = K_OWN + V_ROWS
OWN_ROWS = KV_ROWS + Q_OWN + 32
MIX = 64
GRID_W = 80
HALF_W = GRID_W // 2
FRAME = 2560
KEYS_PART = 3072
Q_BLOCK = 640
ROWS_BLOCK = Q_BLOCK // GRID_W
SUB = 320
STRIP = 24
MSG = HALF_W + 8
TILE_W = 20
SP = ("x", "zh", "y")
MIB = 1024 * 1024
HERE = pl.BlockSpec(memory_space=pltpu.VMEM)


def frequency_row():
    sixth = HD // 6
    time_pairs = (HD - 4 * sixth) // 2
    time = 10000.0 ** (-np.arange(time_pairs) / time_pairs)
    space = 10000.0 ** (-np.arange(sixth) / sixth)
    pairs = np.concatenate([time, space, space])
    return np.repeat(pairs, 2).astype(np.float32)[None, :]


def row_order():
    order = np.zeros((2, 2 * MIX, MIX), np.float32)
    for ch in range(16):
        for ab in range(4):
            for side in range(2):
                order[side, side * MIX + ab * 16 + ch, ch * 4 + ab] = 1.0
    return order


def turn_tables(positions, freq):
    count = positions.shape[1]
    spot = positions.astype(jnp.float32)
    same = lax.broadcasted_iota(jnp.int32, (count, count), 0) == lax.broadcasted_iota(jnp.int32, (count, count), 1)
    column = [jnp.sum(jnp.where(same, spot[i : i + 1], 0.0), axis=1, keepdims=True) for i in range(3)]
    lane = lax.broadcasted_iota(jnp.int32, (count, HD), 1)
    base = jnp.where(lane < 44, column[0], jnp.where(lane < 86, column[1], column[2]))
    angle = base * freq
    cosine = jnp.cos(angle)
    sine = jnp.sin(angle)
    even = lax.rem(lane, 2) == 0
    zero = jnp.zeros_like(sine)
    return cosine, jnp.where(even, -sine, zero), jnp.where(even, zero, sine)


def turn(vectors, tables):
    cosine, from_next, from_last = tables
    wide = vectors.astype(jnp.float32)
    out = wide * cosine + pltpu.roll(wide, HD - 1, 1) * from_next + pltpu.roll(wide, 1, 1) * from_last
    return out.astype(jnp.bfloat16)


def prepare_kernel(qpos, kpos, freq, order, queries, keys, values, mixing, cache, out):
    q_tables = turn_tables(qpos[...], freq[...])
    k_tables = turn_tables(kpos[...], freq[...])
    spots = jnp.concatenate([cache[...].astype(jnp.float32), jnp.zeros((MIX, HD - 40), jnp.float32)], axis=1)
    spots = jnp.transpose(spots)
    low = jnp.concatenate([spots[0:32], jnp.zeros((32, MIX), jnp.float32)], axis=1)
    high = jnp.concatenate([jnp.zeros((32, MIX), jnp.float32), spots[32:64]], axis=1)
    tile = (low + high).astype(jnp.bfloat16)
    mixed = [
        jnp.dot(order[side], mixing[...], preferred_element_type=jnp.float32).astype(jnp.bfloat16)
        for side in range(2)
    ]
    for head in range(HEADS_SEC):
        cols = slice(head * HD, (head + 1) * HD)
        out[head, 0:K_OWN, :] = turn(keys[:, cols], k_tables)
        value = values[:, cols]
        mix_low = lax.dot_general(
            value[:V_ROWS], mixed[0][:, cols], (((1,), (1,)), ((), ())), preferred_element_type=jnp.float32
        )
        mix_high = lax.dot_general(
            value[V_ROWS:], mixed[1][:, cols], (((1,), (1,)), ((), ())), preferred_element_type=jnp.float32
        )
        out[head, K_OWN:KV_ROWS, :] = (mix_low + mix_high).astype(jnp.bfloat16)
        out[head, KV_ROWS : KV_ROWS + Q_OWN, :] = turn(queries[:, cols], q_tables)
        out[head, KV_ROWS + Q_OWN : OWN_ROWS, :] = tile


def prepare(qpos, kpos, queries, keys, values, mixing, cache):
    return pl.pallas_call(
        prepare_kernel,
        in_specs=[HERE] * 9,
        out_specs=HERE,
        out_shape=jax.ShapeDtypeStruct((HEADS_SEC, OWN_ROWS, HD), jnp.bfloat16),
        compiler_params=pltpu.CompilerParams(vmem_limit_bytes=56 * MIB),
        cost_estimate=pl.CostEstimate(flops=50000000, bytes_accessed=1200000, transcendentals=0),
        name="prepare",
    )(
        qpos,
        kpos,
        jnp.asarray(frequency_row()),
        jnp.asarray(row_order(), jnp.bfloat16),
        queries,
        keys,
        values,
        mixing.T,
        cache.transpose(0, 1, 2, 4, 3).reshape(MIX, 40),
    )


def attend_kernel(*refs):
    q_ref, kv_refs, o_ref = refs[0], refs[1:5], refs[5]
    q_buf, k_buf, v_buf, s_even, s_odd = refs[6:]
    lane = lax.broadcasted_iota(jnp.int32, (V_ROWS, HD), 1)
    ones = jnp.where(lane == MIX, 1.0, 0.0)
    for part in range(q_ref.shape[0]):
        q_buf[part * Q_OWN : (part + 1) * Q_OWN] = q_ref[part]
    for piece in range(4):

        def unpack(part, carry, piece=piece):
            at = pl.multiple_of(piece * 8 * K_OWN + part * K_OWN, 16)
            k_buf[pl.ds(at, K_OWN), :] = kv_refs[piece][part, 0:K_OWN, :]
            both = kv_refs[piece][part, K_OWN:KV_ROWS, :].astype(jnp.float32)
            v_buf[pl.ds(at, V_ROWS), :] = jnp.where(lane < MIX, both, ones).astype(jnp.bfloat16)
            other = pltpu.roll(both, MIX, 1)
            at = pl.multiple_of(piece * 8 * K_OWN + part * K_OWN + V_ROWS, 16)
            v_buf[pl.ds(at, V_ROWS), :] = jnp.where(lane < MIX, other, ones).astype(jnp.bfloat16)
            return carry

        lax.fori_loop(0, 8, unpack, 0)

    scale = jnp.float32(math.log2(math.e) / math.sqrt(HD))
    diagonal = lax.broadcasted_iota(jnp.int32, (GRID_W, HD), 1) == lax.broadcasted_iota(jnp.int32, (GRID_W, HD), 0)
    low_lane = lax.broadcasted_iota(jnp.int32, (HALF_W, HD), 1) < MIX

    def score(block):
        at = pl.multiple_of(block * SUB, 16)
        return lax.dot_general(
            q_buf[pl.ds(at, SUB), :], k_buf[...], (((1,), (1,)), ((), ())), preferred_element_type=jnp.float32
        )

    def finish(piece, block, s_ref):
        scores = s_ref[...]
        top = jnp.max(scores, axis=1, keepdims=True)
        weights = jnp.exp2((scores - top) * scale).astype(jnp.bfloat16)
        sums = jnp.dot(weights, v_buf[...], preferred_element_type=jnp.float32)
        total = sums[:, MIX : MIX + 1]
        mean = sums / total
        level = top * scale + jnp.log2(total)
        for patch_row in range(SUB // GRID_W):
            at = patch_row * GRID_W
            low = mean[at : at + HALF_W]
            high = pltpu.roll(mean[at + HALF_W : at + GRID_W], MIX, 1)
            packed = jnp.where(low_lane, low, high)
            line = jnp.sum(jnp.where(diagonal, level[at : at + GRID_W], 0.0), axis=0, keepdims=True)
            first = line.astype(jnp.bfloat16).astype(jnp.float32)
            line = line - first
            second = line.astype(jnp.bfloat16).astype(jnp.float32)
            third = line - second
            message = jnp.concatenate([packed, first, second, third, jnp.zeros((5, HD), jnp.float32)], axis=0)
            spot = block * (SUB // GRID_W) + patch_row
            o_ref[spot // 2, piece * 2 + spot % 2] = message.astype(jnp.bfloat16)

    s_even[...] = score(0)
    blocks = FRAME // SUB

    def pair(step, carry):
        s_odd[...] = score(2 * step + 1)
        finish(step, 0, s_even)
        s_even[...] = score(2 * step + 2)
        finish(step, 1, s_odd)
        return carry

    lax.fori_loop(0, blocks // 2 - 1, pair, 0)
    s_odd[...] = score(blocks - 1)
    finish(blocks // 2 - 1, 0, s_even)
    finish(blocks // 2 - 1, 1, s_odd)


def attend(queries, pairs):
    return pl.pallas_call(
        attend_kernel,
        in_specs=[HERE] * 5,
        out_specs=HERE,
        out_shape=jax.ShapeDtypeStruct((4, ROWS_BLOCK, MSG, HD), jnp.bfloat16),
        scratch_shapes=[
            pltpu.VMEM((FRAME, HD), jnp.bfloat16),
            pltpu.VMEM((KEYS_PART, HD), jnp.bfloat16),
            pltpu.VMEM((KEYS_PART, HD), jnp.bfloat16),
            pltpu.VMEM((SUB, KEYS_PART), jnp.float32),
            pltpu.VMEM((SUB, KEYS_PART), jnp.float32),
        ],
        compiler_params=pltpu.CompilerParams(vmem_limit_bytes=28 * MIB),
        cost_estimate=pl.CostEstimate(flops=4 * FRAME * KEYS_PART * HD, bytes_accessed=2000000, transcendentals=0),
        name="attend",
    )(queries.reshape(FRAME // Q_OWN, Q_OWN, HD), *pairs)


def combine_kernel(r_ref, o_ref):
    shares = r_ref.shape[0]
    lane = lax.broadcasted_iota(jnp.int32, (HALF_W, HD), 1)
    row = lax.broadcasted_iota(jnp.int32, (HALF_W, HD), 0)
    zeros = jnp.zeros((16, HD), jnp.float32)
    low_lane = lax.broadcasted_iota(jnp.int32, (STRIP, HD), 1) < MIX
    lines = []
    for patch_row in range(ROWS_BLOCK):
        blocks = [r_ref[share, patch_row].astype(jnp.float32) for share in range(shares)]
        levels = [b[HALF_W : HALF_W + 1] + b[HALF_W + 1 : HALF_W + 2] + b[HALF_W + 2 : HALF_W + 3] for b in blocks]
        top = levels[0]
        for level in levels[1:]:
            top = jnp.maximum(top, level)
        powers = [jnp.exp2(level - top) for level in levels]
        total = powers[0]
        for power in powers[1:]:
            total = total + power
        result = jnp.zeros((HALF_W, HD), jnp.float32)
        for block, power in zip(blocks, powers):
            weight = power / total
            low = jnp.sum(jnp.where(lane == row, weight, 0.0), axis=1, keepdims=True)
            high = jnp.sum(jnp.where(lane == row + HALF_W, weight, 0.0), axis=1, keepdims=True)
            result = result + jnp.where(lane < MIX, low, high) * block[:HALF_W]
        line = jnp.concatenate([zeros[:1], result, pltpu.roll(result, MIX, 1), zeros], axis=0)
        line = line[: 2 * HALF_W + 16]
        lines.append(line if patch_row % 2 == 0 else pltpu.roll(line, MIX, 1))
    for group in range(4):
        for tile in range(4):
            at = tile * TILE_W
            piece = jnp.where(low_lane, lines[2 * group][at : at + STRIP], lines[2 * group + 1][at : at + STRIP])
            piece = piece.astype(jnp.bfloat16)
            for copy in range(2):
                o_ref[copy * 4 + tile, group] = piece


def combine(received):
    return pl.pallas_call(
        combine_kernel,
        in_specs=[HERE],
        out_specs=HERE,
        out_shape=jax.ShapeDtypeStruct((8, 4, STRIP, HD), jnp.bfloat16),
        compiler_params=pltpu.CompilerParams(vmem_limit_bytes=8 * MIB),
        cost_estimate=pl.CostEstimate(flops=1000000, bytes_accessed=900000, transcendentals=0),
        name="combine",
    )(received)


def from_ahead(value, axis, steps):
    return lax.ppermute(value, axis, [((spot + steps) % 4, spot) for spot in range(4)])


def next_pair(value, axes):
    pairs = [(i, i + 8) for i in range(120) if i % 8 < 4] + [(i, i - 8) for i in range(8, 128) if i % 8 >= 4]
    return lax.ppermute(value, axes, pairs)


def cache_tile(tiles, half, tile_col):
    wide = jnp.concatenate([tiles[:, :, :MIX], tiles[:, :8, MIX:]], axis=1).reshape(2, 160, MIX)
    wide = jnp.pad(wide, ((0, 0), (1, 1), (0, 0)))
    wide = lax.dynamic_slice_in_dim(wide, tile_col * 40, 42, 1).reshape(2, 42, 2, 2, 16)
    wide = wide.transpose(0, 2, 3, 1, 4)
    near = next_pair(jnp.where(half == 0, wide[1, :, 1], wide[0, :, 0]), SP)
    first = jnp.where(half == 0, near, wide[0, :, 1])
    last = jnp.where(half == 0, wide[1, :, 0], near)
    middle = jnp.where(half == 0, wide[0], wide[1])
    return jnp.concatenate([first[:, None], middle, last[:, None]], axis=1)


def on_device(queries, keys, values, query_positions, key_positions, mixing, kernel, bias, cache):
    sp_index = lax.axis_index(SP)
    section = lax.axis_index("sec")
    half = lax.axis_index("y") // 4
    tile_col = sp_index % 4
    tile_row = sp_index // 4
    own = prepare(query_positions, key_positions, queries, keys, values, mixing, cache)
    own = lax.all_to_all(own, "y", 0, 0)
    kv_own = own[:, :KV_ROWS]
    q_own = own[:, KV_ROWS : KV_ROWS + Q_OWN]
    query_all = lax.all_to_all(jnp.broadcast_to(q_own[None], (4, *q_own.shape)), "zh", 0, 0)
    pairs = [kv_own] + [from_ahead(kv_own, "x", step) for step in (1, 2, 3)]
    tiles, pairs[1] = lax.optimization_barrier((own[:, KV_ROWS + Q_OWN :], pairs[1]))
    cached = cache_tile(tiles, half, tile_col)
    query_all, pairs, cached = lax.optimization_barrier((query_all, pairs, cached))
    parts = attend(query_all, pairs)
    shares = lax.all_to_all(parts, "zh", 0, 0)
    tiles = lax.all_to_all(combine(shares), "y", 0, 0)
    strip = jnp.sum(tiles.astype(jnp.float32), axis=0).astype(jnp.bfloat16)
    strip = lax.all_to_all(jnp.broadcast_to(strip[None], (4, *strip.shape)).reshape(16, STRIP, HD), ("sec", "x"), 0, 0)
    strip = jnp.sum(strip.reshape(4, 4, STRIP, HD).astype(jnp.float32), axis=0).astype(jnp.bfloat16)
    strip = jnp.concatenate([jnp.zeros((2, STRIP, HD), jnp.bfloat16), strip], axis=0)
    frames = lax.dynamic_slice_in_dim(strip, section, 3, 0)
    own, near = frames[:, :22], next_pair(frames, SP)[:, :22]
    low, high = own[:, :, :MIX], own[:, :, MIX:]
    first = jnp.where(half == 0, near[:, :, MIX:], low)
    middle = jnp.where(half == 0, low, high)
    last = jnp.where(half == 0, high, near[:, :, :MIX])
    frames = jnp.stack([first, middle, last], axis=1)
    frames = frames.reshape(3, 3, 22, 2, 2, 16).transpose(0, 1, 3, 2, 4, 5).reshape(3, 6, 44, 16)
    frames = frames[:, 1:5, 1:43]
    line = jnp.arange(4)[:, None, None]
    spot = jnp.arange(42)[None, :, None]
    outside = (
        ((tile_row == 0) & (line == 0))
        | ((tile_row == 31) & (line == 3))
        | ((tile_col == 0) & (spot == 0))
        | ((tile_col == 3) & (spot == 41))
    )
    frames = jnp.where(outside[None], jnp.zeros_like(frames), frames)
    minus_two = jnp.where(section >= 2, frames[0], jnp.where(section == 1, cached[1], cached[0]))
    minus_one = jnp.where(section >= 1, frames[1], cached[1])
    frames = jnp.stack([minus_two, minus_one, frames[2]])
    windows = [
        frames[step_t, step_y : step_y + 2, step_x : step_x + 40, :]
        for step_t in range(3)
        for step_y in range(3)
        for step_x in range(3)
    ]
    columns = jnp.stack(windows, axis=2).reshape(80, 27 * 16)
    output = jnp.dot(columns, kernel, preferred_element_type=jnp.float32) + bias[None, :]
    return output.reshape(1, 1, 2, 40, kernel.shape[1]).astype(jnp.bfloat16)


def solution(mesh):
    fine = Mesh(mesh.devices.reshape(4, 4, 4, 8), ("sec", *SP))
    placed = (
        P(SP, "sec"),
        P(SP, "sec"),
        P(SP, "sec"),
        P(None, SP),
        P(None, SP),
        P("sec", None),
        P(),
        P(),
        P(None, SP, None, None, None),
    )
    return jax.shard_map(
        on_device,
        mesh=fine,
        in_specs=placed,
        out_specs=P("sec", SP, None, None, None),
        check_vma=False,
    )
```

```python
import math

import jax
import jax.numpy as jnp
import numpy as np
from jax import lax
from jax.experimental import pallas as pl
from jax.experimental.pallas import tpu as pltpu
from jax.sharding import Mesh
from jax.sharding import PartitionSpec as P

HD = 128
HEADS_SEC = 8
Q_OWN = 80
K_OWN = 96
V_ROWS = K_OWN // 2
KV_ROWS = K_OWN + V_ROWS
OWN_ROWS = KV_ROWS + Q_OWN + 32
MIX = 64
GRID_W = 80
HALF_W = GRID_W // 2
FRAME = 2560
KEYS_PART = 3072
Q_BLOCK = 640
ROWS_BLOCK = Q_BLOCK // GRID_W
SUB = 640
STRIP = 24
MSG = HALF_W + 8
TILE_W = 20
SP = ("x", "zh", "y")
MIB = 1024 * 1024
HERE = pl.BlockSpec(memory_space=pltpu.VMEM)


def frequency_row():
    sixth = HD // 6
    time_pairs = (HD - 4 * sixth) // 2
    time = 10000.0 ** (-np.arange(time_pairs) / time_pairs)
    space = 10000.0 ** (-np.arange(sixth) / sixth)
    pairs = np.concatenate([time, space, space])
    return np.repeat(pairs, 2).astype(np.float32)[None, :]


def row_order():
    order = np.zeros((2, 2 * MIX, MIX), np.float32)
    for ch in range(16):
        for ab in range(4):
            for side in range(2):
                order[side, side * MIX + ab * 16 + ch, ch * 4 + ab] = 1.0
    return order


def patch_order():
    pick = np.zeros((2, 32, 40), np.float32)
    place = np.zeros((2, MIX, HD), np.float32)
    for side in range(2):
        for patch in range(TILE_W):
            pick[side, patch, 2 * patch + side] = 1.0
        for line in range(4):
            for ch in range(16):
                place[side, line * 16 + ch, line * 32 + side * 16 + ch] = 1.0
    return pick, place


def turn_tables(positions, freq):
    count = positions.shape[1]
    spot = positions.astype(jnp.float32)
    same = lax.broadcasted_iota(jnp.int32, (count, count), 0) == lax.broadcasted_iota(jnp.int32, (count, count), 1)
    column = [jnp.sum(jnp.where(same, spot[i : i + 1], 0.0), axis=1, keepdims=True) for i in range(3)]
    lane = lax.broadcasted_iota(jnp.int32, (count, HD), 1)
    base = jnp.where(lane < 44, column[0], jnp.where(lane < 86, column[1], column[2]))
    angle = base * freq
    cosine = jnp.cos(angle)
    sine = jnp.sin(angle)
    even = lax.rem(lane, 2) == 0
    zero = jnp.zeros_like(sine)
    return cosine, jnp.where(even, -sine, zero), jnp.where(even, zero, sine)


def turn(vectors, tables):
    cosine, from_next, from_last = tables
    wide = vectors.astype(jnp.float32)
    out = wide * cosine + pltpu.roll(wide, HD - 1, 1) * from_next + pltpu.roll(wide, 1, 1) * from_last
    return out.astype(jnp.bfloat16)


def prepare_kernel(qpos, kpos, freq, order, pick, place, queries, keys, values, mixing, cache, out):
    q_tables = turn_tables(qpos[...], freq[...])
    k_tables = turn_tables(kpos[...], freq[...])
    tile = jnp.zeros((32, HD), jnp.float32)
    for side in range(2):
        column = lax.dot_general(
            pick[side], cache[...], (((1,), (1,)), ((), ())), preferred_element_type=jnp.float32
        )
        tile = tile + jnp.dot(column.astype(jnp.bfloat16), place[side], preferred_element_type=jnp.float32)
    tile = tile.astype(jnp.bfloat16)
    mixed = [
        jnp.dot(order[side], mixing[...], preferred_element_type=jnp.float32).astype(jnp.bfloat16)
        for side in range(2)
    ]
    for head in range(HEADS_SEC):
        cols = slice(head * HD, (head + 1) * HD)
        out[head, 0:K_OWN, :] = turn(keys[:, cols], k_tables)
        value = values[:, cols]
        mix_low = lax.dot_general(
            value[:V_ROWS], mixed[0][:, cols], (((1,), (1,)), ((), ())), preferred_element_type=jnp.float32
        )
        mix_high = lax.dot_general(
            value[V_ROWS:], mixed[1][:, cols], (((1,), (1,)), ((), ())), preferred_element_type=jnp.float32
        )
        out[head, K_OWN:KV_ROWS, :] = (mix_low + mix_high).astype(jnp.bfloat16)
        out[head, KV_ROWS : KV_ROWS + Q_OWN, :] = turn(queries[:, cols], q_tables)
        out[head, KV_ROWS + Q_OWN : OWN_ROWS, :] = tile


def prepare(qpos, kpos, queries, keys, values, mixing, cache):
    return pl.pallas_call(
        prepare_kernel,
        in_specs=[HERE] * 11,
        out_specs=HERE,
        out_shape=jax.ShapeDtypeStruct((HEADS_SEC, OWN_ROWS, HD), jnp.bfloat16),
        compiler_params=pltpu.CompilerParams(vmem_limit_bytes=56 * MIB),
        cost_estimate=pl.CostEstimate(flops=50000000, bytes_accessed=1200000, transcendentals=0),
        name="prepare",
    )(
        qpos,
        kpos,
        jnp.asarray(frequency_row()),
        jnp.asarray(row_order(), jnp.bfloat16),
        *(jnp.asarray(part, jnp.bfloat16) for part in patch_order()),
        queries,
        keys,
        values,
        mixing.T,
        cache.transpose(0, 1, 2, 4, 3).reshape(MIX, 40),
    )


def attend_kernel(*refs):
    q_ref, kv_refs, o_ref = refs[0], refs[1:5], refs[5]
    q_buf, k_buf, v_buf, s_even, s_odd = refs[6:]
    lane = lax.broadcasted_iota(jnp.int32, (V_ROWS, HD), 1)
    ones = jnp.where(lane == MIX, 1.0, 0.0)
    for part in range(q_ref.shape[0]):
        q_buf[part * Q_OWN : (part + 1) * Q_OWN] = q_ref[part]
    for piece in range(4):
        for part in range(8):
            at = (piece * 8 + part) * K_OWN
            k_buf[at : at + K_OWN] = kv_refs[piece][part, 0:K_OWN, :]
            both = kv_refs[piece][part, K_OWN:KV_ROWS, :].astype(jnp.float32)
            v_buf[at : at + V_ROWS] = jnp.where(lane < MIX, both, ones).astype(jnp.bfloat16)
            other = pltpu.roll(both, MIX, 1)
            v_buf[at + V_ROWS : at + K_OWN] = jnp.where(lane < MIX, other, ones).astype(jnp.bfloat16)

    scale = jnp.float32(math.log2(math.e) / math.sqrt(HD))
    diagonal = lax.broadcasted_iota(jnp.int32, (GRID_W, HD), 1) == lax.broadcasted_iota(jnp.int32, (GRID_W, HD), 0)
    low_lane = lax.broadcasted_iota(jnp.int32, (HALF_W, HD), 1) < MIX

    def score(block):
        at = pl.multiple_of(block * SUB, 16)
        return lax.dot_general(
            q_buf[pl.ds(at, SUB), :], k_buf[...], (((1,), (1,)), ((), ())), preferred_element_type=jnp.float32
        )

    def finish(piece, s_ref):
        scores = s_ref[...]
        top = jnp.max(scores, axis=1, keepdims=True)
        weights = jnp.exp2((scores - top) * scale).astype(jnp.bfloat16)
        sums = jnp.dot(weights, v_buf[...], preferred_element_type=jnp.float32)
        total = sums[:, MIX : MIX + 1]
        mean = sums / total
        level = top * scale + jnp.log2(total)
        for patch_row in range(SUB // GRID_W):
            at = patch_row * GRID_W
            low = mean[at : at + HALF_W]
            high = pltpu.roll(mean[at + HALF_W : at + GRID_W], MIX, 1)
            packed = jnp.where(low_lane, low, high)
            line = jnp.sum(jnp.where(diagonal, level[at : at + GRID_W], 0.0), axis=0, keepdims=True)
            first = line.astype(jnp.bfloat16).astype(jnp.float32)
            line = line - first
            second = line.astype(jnp.bfloat16).astype(jnp.float32)
            third = line - second
            message = jnp.concatenate([packed, first, second, third, jnp.zeros((5, HD), jnp.float32)], axis=0)
            spot = patch_row
            o_ref[spot // 2, piece * 2 + spot % 2] = message.astype(jnp.bfloat16)

    s_even[...] = score(0)

    def pair(step, carry):
        s_odd[...] = score(2 * step + 1)
        finish(2 * step, s_even)
        s_even[...] = score(2 * step + 2)
        finish(2 * step + 1, s_odd)
        return carry

    lax.fori_loop(0, 1, pair, 0)
    s_odd[...] = score(3)
    finish(2, s_even)
    finish(3, s_odd)


def attend(queries, pairs):
    return pl.pallas_call(
        attend_kernel,
        in_specs=[HERE] * 5,
        out_specs=HERE,
        out_shape=jax.ShapeDtypeStruct((4, ROWS_BLOCK, MSG, HD), jnp.bfloat16),
        scratch_shapes=[
            pltpu.VMEM((FRAME, HD), jnp.bfloat16),
            pltpu.VMEM((KEYS_PART, HD), jnp.bfloat16),
            pltpu.VMEM((KEYS_PART, HD), jnp.bfloat16),
            pltpu.VMEM((SUB, KEYS_PART), jnp.float32),
            pltpu.VMEM((SUB, KEYS_PART), jnp.float32),
        ],
        compiler_params=pltpu.CompilerParams(vmem_limit_bytes=42 * MIB),
        cost_estimate=pl.CostEstimate(flops=4 * FRAME * KEYS_PART * HD, bytes_accessed=2000000, transcendentals=0),
        name="attend",
    )(queries.reshape(FRAME // Q_OWN, Q_OWN, HD), *pairs)


def combine_kernel(r_ref, o_ref):
    shares = r_ref.shape[0]
    lane = lax.broadcasted_iota(jnp.int32, (HALF_W, HD), 1)
    row = lax.broadcasted_iota(jnp.int32, (HALF_W, HD), 0)
    zeros = jnp.zeros((16, HD), jnp.float32)
    low_lane = lax.broadcasted_iota(jnp.int32, (STRIP, HD), 1) < MIX
    lines = []
    for patch_row in range(ROWS_BLOCK):
        blocks = [r_ref[share, patch_row].astype(jnp.float32) for share in range(shares)]
        levels = [b[HALF_W : HALF_W + 1] + b[HALF_W + 1 : HALF_W + 2] + b[HALF_W + 2 : HALF_W + 3] for b in blocks]
        top = levels[0]
        for level in levels[1:]:
            top = jnp.maximum(top, level)
        powers = [jnp.exp2(level - top) for level in levels]
        total = powers[0]
        for power in powers[1:]:
            total = total + power
        result = jnp.zeros((HALF_W, HD), jnp.float32)
        for block, power in zip(blocks, powers):
            weight = power / total
            low = jnp.sum(jnp.where(lane == row, weight, 0.0), axis=1, keepdims=True)
            high = jnp.sum(jnp.where(lane == row + HALF_W, weight, 0.0), axis=1, keepdims=True)
            result = result + jnp.where(lane < MIX, low, high) * block[:HALF_W]
        line = jnp.concatenate([zeros[:1], result, pltpu.roll(result, MIX, 1), zeros], axis=0)
        line = line[: 2 * HALF_W + 16]
        lines.append(line if patch_row % 2 == 0 else pltpu.roll(line, MIX, 1))
    for group in range(4):
        for tile in range(4):
            at = tile * TILE_W
            piece = jnp.where(low_lane, lines[2 * group][at : at + STRIP], lines[2 * group + 1][at : at + STRIP])
            piece = piece.astype(jnp.bfloat16)
            for copy in range(2):
                o_ref[copy * 4 + tile, group] = piece


def combine(received):
    return pl.pallas_call(
        combine_kernel,
        in_specs=[HERE],
        out_specs=HERE,
        out_shape=jax.ShapeDtypeStruct((8, 4, STRIP, HD), jnp.bfloat16),
        compiler_params=pltpu.CompilerParams(vmem_limit_bytes=8 * MIB),
        cost_estimate=pl.CostEstimate(flops=1000000, bytes_accessed=900000, transcendentals=0),
        name="combine",
    )(received)


def from_ahead(value, axis, steps):
    return lax.ppermute(value, axis, [((spot + steps) % 4, spot) for spot in range(4)])


def next_pair(value, axes):
    pairs = [(i, i + 8) for i in range(120) if i % 8 < 4] + [(i, i - 8) for i in range(8, 128) if i % 8 >= 4]
    return lax.ppermute(value, axes, pairs)


def cache_strips(tiles, tile_col):
    wide = tiles.reshape(2, 4, 32, HD)[:, :, :TILE_W].reshape(2, GRID_W, HD)
    wide = jnp.pad(wide, ((0, 0), (1, 3), (0, 0)))
    wide = lax.dynamic_slice_in_dim(wide, tile_col * TILE_W, STRIP, 1)
    return wide.reshape(2, STRIP, 2, MIX).transpose(2, 1, 0, 3).reshape(2, STRIP, HD)


def on_device(queries, keys, values, query_positions, key_positions, mixing, kernel, bias, cache):
    sp_index = lax.axis_index(SP)
    section = lax.axis_index("sec")
    half = lax.axis_index("y") // 4
    tile_col = sp_index % 4
    tile_row = sp_index // 4
    own = prepare(query_positions, key_positions, queries, keys, values, mixing, cache)
    own = lax.all_to_all(own, "y", 0, 0)
    kv_own = own[:, :KV_ROWS]
    q_own = own[:, KV_ROWS : KV_ROWS + Q_OWN]
    query_all = lax.all_to_all(jnp.broadcast_to(q_own[None], (4, *q_own.shape)), "zh", 0, 0)
    pairs = [kv_own] + [from_ahead(kv_own, "x", step) for step in (1, 2, 3)]
    cached = cache_strips(own[:, KV_ROWS + Q_OWN :], tile_col)
    query_all, pairs, cached = lax.optimization_barrier((query_all, pairs, cached))
    parts = attend(query_all, pairs)
    shares = lax.all_to_all(parts, "zh", 0, 0)
    tiles = lax.all_to_all(combine(shares), "y", 0, 0)
    strip = jnp.sum(tiles.astype(jnp.float32), axis=0).astype(jnp.bfloat16)
    strip = lax.all_to_all(jnp.broadcast_to(strip[None], (4, *strip.shape)).reshape(16, STRIP, HD), ("sec", "x"), 0, 0)
    strip = jnp.sum(strip.reshape(4, 4, STRIP, HD).astype(jnp.float32), axis=0).astype(jnp.bfloat16)
    strip = jnp.concatenate([cached, strip], axis=0)
    frames = lax.dynamic_slice_in_dim(strip, section, 3, 0)
    own, near = frames[:, :22], next_pair(frames, SP)[:, :22]
    low, high = own[:, :, :MIX], own[:, :, MIX:]
    first = jnp.where(half == 0, near[:, :, MIX:], low)
    middle = jnp.where(half == 0, low, high)
    last = jnp.where(half == 0, high, near[:, :, :MIX])
    frames = jnp.stack([first, middle, last], axis=1)
    frames = frames.reshape(3, 3, 22, 2, 2, 16).transpose(0, 1, 3, 2, 4, 5).reshape(3, 6, 44, 16)
    frames = frames[:, 1:5, 1:43]
    line = jnp.arange(4)[:, None, None]
    spot = jnp.arange(42)[None, :, None]
    outside = (
        ((tile_row == 0) & (line == 0))
        | ((tile_row == 31) & (line == 3))
        | ((tile_col == 0) & (spot == 0))
        | ((tile_col == 3) & (spot == 41))
    )
    frames = jnp.where(outside[None], jnp.zeros_like(frames), frames)
    windows = [
        frames[step_t, step_y : step_y + 2, step_x : step_x + 40, :]
        for step_t in range(3)
        for step_y in range(3)
        for step_x in range(3)
    ]
    columns = jnp.stack(windows, axis=2).reshape(80, 27 * 16)
    output = jnp.dot(columns, kernel, preferred_element_type=jnp.float32) + bias[None, :]
    return output.reshape(1, 1, 2, 40, kernel.shape[1]).astype(jnp.bfloat16)


def solution(mesh):
    fine = Mesh(mesh.devices.reshape(4, 4, 4, 8), ("sec", *SP))
    placed = (
        P(SP, "sec"),
        P(SP, "sec"),
        P(SP, "sec"),
        P(None, SP),
        P(None, SP),
        P("sec", None),
        P(),
        P(),
        P(None, SP, None, None, None),
    )
    return jax.shard_map(
        on_device,
        mesh=fine,
        in_specs=placed,
        out_specs=P("sec", SP, None, None, None),
        check_vma=False,
    )
```

```python
import math

import jax
import jax.numpy as jnp
import numpy as np
from jax import lax
from jax.experimental import pallas as pl
from jax.experimental.pallas import tpu as pltpu
from jax.sharding import Mesh
from jax.sharding import PartitionSpec as P

HD = 128
HEADS_SEC = 8
Q_OWN = 80
K_OWN = 96
V_ROWS = K_OWN // 2
KV_ROWS = K_OWN + V_ROWS
OWN_ROWS = KV_ROWS + Q_OWN + 32
MIX = 64
GRID_W = 80
HALF_W = GRID_W // 2
FRAME = 2560
KEYS_PART = 3072
Q_BLOCK = 640
ROWS_BLOCK = Q_BLOCK // GRID_W
SUB = 640
STRIP = 24
MSG = HALF_W + 8
TILE_W = 20
SP = ("x", "zh", "y")
MIB = 1024 * 1024
HERE = pl.BlockSpec(memory_space=pltpu.VMEM)


def frequency_row():
    sixth = HD // 6
    time_pairs = (HD - 4 * sixth) // 2
    time = 10000.0 ** (-np.arange(time_pairs) / time_pairs)
    space = 10000.0 ** (-np.arange(sixth) / sixth)
    pairs = np.concatenate([time, space, space])
    return np.repeat(pairs, 2).astype(np.float32)[None, :]


def row_order():
    order = np.zeros((2, 2 * MIX, MIX), np.float32)
    for ch in range(16):
        for ab in range(4):
            for side in range(2):
                order[side, side * MIX + ab * 16 + ch, ch * 4 + ab] = 1.0
    return order


def patch_order():
    pick = np.zeros((2, 32, 40), np.float32)
    place = np.zeros((2, MIX, HD), np.float32)
    for side in range(2):
        for patch in range(TILE_W):
            pick[side, patch, 2 * patch + side] = 1.0
        for line in range(4):
            for ch in range(16):
                place[side, line * 16 + ch, line * 32 + side * 16 + ch] = 1.0
    return pick, place


def turn_tables(positions, freq):
    count = positions.shape[1]
    spot = positions.astype(jnp.float32)
    same = lax.broadcasted_iota(jnp.int32, (count, count), 0) == lax.broadcasted_iota(jnp.int32, (count, count), 1)
    column = [jnp.sum(jnp.where(same, spot[i : i + 1], 0.0), axis=1, keepdims=True) for i in range(3)]
    lane = lax.broadcasted_iota(jnp.int32, (count, HD), 1)
    base = jnp.where(lane < 44, column[0], jnp.where(lane < 86, column[1], column[2]))
    angle = base * freq
    cosine = jnp.cos(angle)
    sine = jnp.sin(angle)
    even = lax.rem(lane, 2) == 0
    zero = jnp.zeros_like(sine)
    return cosine, jnp.where(even, -sine, zero), jnp.where(even, zero, sine)


def turn(vectors, tables):
    cosine, from_next, from_last = tables
    wide = vectors.astype(jnp.float32)
    out = wide * cosine + pltpu.roll(wide, HD - 1, 1) * from_next + pltpu.roll(wide, 1, 1) * from_last
    return out.astype(jnp.bfloat16)


def prepare_kernel(qpos, kpos, freq, order, pick, place, queries, keys, values, mixing, cache, out):
    q_tables = turn_tables(qpos[...], freq[...])
    k_tables = turn_tables(kpos[...], freq[...])
    tile = jnp.zeros((32, HD), jnp.float32)
    for side in range(2):
        column = lax.dot_general(
            pick[side], cache[...], (((1,), (1,)), ((), ())), preferred_element_type=jnp.float32
        )
        tile = tile + jnp.dot(column.astype(jnp.bfloat16), place[side], preferred_element_type=jnp.float32)
    tile = tile.astype(jnp.bfloat16)
    mixed = [
        jnp.dot(order[side], mixing[...], preferred_element_type=jnp.float32).astype(jnp.bfloat16)
        for side in range(2)
    ]
    for head in range(HEADS_SEC):
        cols = slice(head * HD, (head + 1) * HD)
        out[head, 0:K_OWN, :] = turn(keys[:, cols], k_tables)
        value = values[:, cols]
        mix_low = lax.dot_general(
            value[:V_ROWS], mixed[0][:, cols], (((1,), (1,)), ((), ())), preferred_element_type=jnp.float32
        )
        mix_high = lax.dot_general(
            value[V_ROWS:], mixed[1][:, cols], (((1,), (1,)), ((), ())), preferred_element_type=jnp.float32
        )
        out[head, K_OWN:KV_ROWS, :] = (mix_low + mix_high).astype(jnp.bfloat16)
        out[head, KV_ROWS : KV_ROWS + Q_OWN, :] = turn(queries[:, cols], q_tables)
        out[head, KV_ROWS + Q_OWN : OWN_ROWS, :] = tile


def prepare(qpos, kpos, queries, keys, values, mixing, cache):
    return pl.pallas_call(
        prepare_kernel,
        in_specs=[HERE] * 11,
        out_specs=HERE,
        out_shape=jax.ShapeDtypeStruct((HEADS_SEC, OWN_ROWS, HD), jnp.bfloat16),
        compiler_params=pltpu.CompilerParams(vmem_limit_bytes=56 * MIB),
        cost_estimate=pl.CostEstimate(flops=50000000, bytes_accessed=1200000, transcendentals=0),
        name="prepare",
    )(
        qpos,
        kpos,
        jnp.asarray(frequency_row()),
        jnp.asarray(row_order(), jnp.bfloat16),
        *(jnp.asarray(part, jnp.bfloat16) for part in patch_order()),
        queries,
        keys,
        values,
        mixing.T,
        cache.transpose(0, 1, 2, 4, 3).reshape(MIX, 40),
    )


def attend_kernel(*refs):
    q_ref, kv_refs, o_ref = refs[0], refs[1:6], refs[6]
    q_buf, k_buf, v_buf, s_even, s_odd = refs[7:]
    lane = lax.broadcasted_iota(jnp.int32, (V_ROWS, HD), 1)
    ones = jnp.where(lane == MIX, 1.0, 0.0)
    for part in range(q_ref.shape[0]):
        q_buf[part * Q_OWN : (part + 1) * Q_OWN] = q_ref[part]
    at = 0
    for kv_ref in kv_refs:
        for part in range(kv_ref.shape[0]):
            k_buf[at : at + K_OWN] = kv_ref[part, 0:K_OWN, :]
            both = kv_ref[part, K_OWN:KV_ROWS, :].astype(jnp.float32)
            v_buf[at : at + V_ROWS] = jnp.where(lane < MIX, both, ones).astype(jnp.bfloat16)
            other = pltpu.roll(both, MIX, 1)
            v_buf[at + V_ROWS : at + K_OWN] = jnp.where(lane < MIX, other, ones).astype(jnp.bfloat16)
            at += K_OWN

    scale = jnp.float32(math.log2(math.e) / math.sqrt(HD))
    diagonal = lax.broadcasted_iota(jnp.int32, (GRID_W, HD), 1) == lax.broadcasted_iota(jnp.int32, (GRID_W, HD), 0)
    low_lane = lax.broadcasted_iota(jnp.int32, (HALF_W, HD), 1) < MIX

    def score(block):
        at = pl.multiple_of(block * SUB, 16)
        return lax.dot_general(
            q_buf[pl.ds(at, SUB), :], k_buf[...], (((1,), (1,)), ((), ())), preferred_element_type=jnp.float32
        )

    def finish(piece, s_ref):
        scores = s_ref[...]
        top = jnp.max(scores, axis=1, keepdims=True)
        weights = jnp.exp2((scores - top) * scale).astype(jnp.bfloat16)
        sums = jnp.dot(weights, v_buf[...], preferred_element_type=jnp.float32)
        total = sums[:, MIX : MIX + 1]
        mean = sums / total
        level = top * scale + jnp.log2(total)
        for patch_row in range(SUB // GRID_W):
            at = patch_row * GRID_W
            low = mean[at : at + HALF_W]
            high = pltpu.roll(mean[at + HALF_W : at + GRID_W], MIX, 1)
            packed = jnp.where(low_lane, low, high)
            line = jnp.sum(jnp.where(diagonal, level[at : at + GRID_W], 0.0), axis=0, keepdims=True)
            first = line.astype(jnp.bfloat16).astype(jnp.float32)
            line = line - first
            second = line.astype(jnp.bfloat16).astype(jnp.float32)
            third = line - second
            message = jnp.concatenate([packed, first, second, third, jnp.zeros((5, HD), jnp.float32)], axis=0)
            spot = patch_row
            o_ref[spot // 2, piece * 2 + spot % 2] = message.astype(jnp.bfloat16)

    s_even[...] = score(0)

    def pair(step, carry):
        s_odd[...] = score(2 * step + 1)
        finish(2 * step, s_even)
        s_even[...] = score(2 * step + 2)
        finish(2 * step + 1, s_odd)
        return carry

    lax.fori_loop(0, 1, pair, 0)
    s_odd[...] = score(3)
    finish(2, s_even)
    finish(3, s_odd)


def attend(queries, pairs):
    return pl.pallas_call(
        attend_kernel,
        in_specs=[HERE] * 6,
        out_specs=HERE,
        out_shape=jax.ShapeDtypeStruct((4, ROWS_BLOCK, MSG, HD), jnp.bfloat16),
        scratch_shapes=[
            pltpu.VMEM((FRAME, HD), jnp.bfloat16),
            pltpu.VMEM((KEYS_PART, HD), jnp.bfloat16),
            pltpu.VMEM((KEYS_PART, HD), jnp.bfloat16),
            pltpu.VMEM((SUB, KEYS_PART), jnp.float32),
            pltpu.VMEM((SUB, KEYS_PART), jnp.float32),
        ],
        compiler_params=pltpu.CompilerParams(vmem_limit_bytes=42 * MIB),
        cost_estimate=pl.CostEstimate(flops=4 * FRAME * KEYS_PART * HD, bytes_accessed=2000000, transcendentals=0),
        name="attend",
    )(queries.reshape(FRAME // Q_OWN, Q_OWN, HD), *pairs)


def combine_kernel(r_ref, o_ref):
    shares = r_ref.shape[0]
    lane = lax.broadcasted_iota(jnp.int32, (HALF_W, HD), 1)
    row = lax.broadcasted_iota(jnp.int32, (HALF_W, HD), 0)
    zeros = jnp.zeros((16, HD), jnp.float32)
    low_lane = lax.broadcasted_iota(jnp.int32, (STRIP, HD), 1) < MIX
    lines = []
    for patch_row in range(ROWS_BLOCK):
        blocks = [r_ref[share, patch_row].astype(jnp.float32) for share in range(shares)]
        levels = [b[HALF_W : HALF_W + 1] + b[HALF_W + 1 : HALF_W + 2] + b[HALF_W + 2 : HALF_W + 3] for b in blocks]
        top = levels[0]
        for level in levels[1:]:
            top = jnp.maximum(top, level)
        powers = [jnp.exp2(level - top) for level in levels]
        total = powers[0]
        for power in powers[1:]:
            total = total + power
        result = jnp.zeros((HALF_W, HD), jnp.float32)
        for block, power in zip(blocks, powers):
            weight = power / total
            low = jnp.sum(jnp.where(lane == row, weight, 0.0), axis=1, keepdims=True)
            high = jnp.sum(jnp.where(lane == row + HALF_W, weight, 0.0), axis=1, keepdims=True)
            result = result + jnp.where(lane < MIX, low, high) * block[:HALF_W]
        line = jnp.concatenate([zeros[:1], result, pltpu.roll(result, MIX, 1), zeros], axis=0)
        line = line[: 2 * HALF_W + 16]
        lines.append(line if patch_row % 2 == 0 else pltpu.roll(line, MIX, 1))
    for group in range(4):
        for tile in range(4):
            at = tile * TILE_W
            piece = jnp.where(low_lane, lines[2 * group][at : at + STRIP], lines[2 * group + 1][at : at + STRIP])
            piece = piece.astype(jnp.bfloat16)
            for copy in range(2):
                o_ref[copy * 4 + tile, group] = piece


def combine(received):
    return pl.pallas_call(
        combine_kernel,
        in_specs=[HERE],
        out_specs=HERE,
        out_shape=jax.ShapeDtypeStruct((8, 4, STRIP, HD), jnp.bfloat16),
        compiler_params=pltpu.CompilerParams(vmem_limit_bytes=8 * MIB),
        cost_estimate=pl.CostEstimate(flops=1000000, bytes_accessed=900000, transcendentals=0),
        name="combine",
    )(received)


def from_ahead(value, axis, steps):
    return lax.ppermute(value, axis, [((spot + steps) % 4, spot) for spot in range(4)])


def next_pairs(turned):
    links = []
    for pair in range(16):
        for y in range(8):
            other = pair - 1 if y < 4 else pair + 1
            if 0 <= other < 16:
                place = other % 4 * 4 + other // 4 if turned else other
                links.append((place * 8 + y, pair * 8 + y))
    return links


def cache_strips(tiles, tile_col):
    wide = tiles.reshape(2, 4, 32, HD)[:, :, :TILE_W].reshape(2, GRID_W, HD)
    wide = jnp.pad(wide, ((0, 0), (1, 3), (0, 0)))
    wide = lax.dynamic_slice_in_dim(wide, tile_col * TILE_W, STRIP, 1)
    return wide.reshape(2, STRIP, 2, MIX).transpose(2, 1, 0, 3).reshape(2, STRIP, HD)


def on_device(queries, keys, values, query_positions, key_positions, mixing, kernel, bias, cache):
    sp_index = lax.axis_index(SP)
    section = lax.axis_index("sec")
    half = lax.axis_index("y") // 4
    tile_col = sp_index % 4
    tile_row = sp_index // 4
    own = prepare(query_positions, key_positions, queries, keys, values, mixing, cache)
    own = lax.all_to_all(own, "y", 0, 0)
    kv_own = own[:, :KV_ROWS]
    q_own = own[:, KV_ROWS : KV_ROWS + Q_OWN]
    query_all = lax.all_to_all(jnp.broadcast_to(q_own[None], (4, *q_own.shape)), "x", 0, 0)
    kv_next = from_ahead(kv_own, "zh", 1)
    kv_last = from_ahead(kv_own, "zh", 3)
    tiles, kv_next, kv_last = lax.optimization_barrier((own[:, KV_ROWS + Q_OWN :], kv_next, kv_last))
    kv_far = [from_ahead(kv_last[:4], "zh", 3), from_ahead(kv_next[4:], "zh", 1)]
    pairs = [kv_own, kv_next, kv_last, *kv_far]
    cached = jnp.pad(cache_strips(tiles, tile_col), ((0, 4), (0, 0), (0, 0)))
    cached = lax.dynamic_slice_in_dim(cached, section, 3, 0)
    cached_near = lax.ppermute(cached, SP, next_pairs(False))
    query_all, pairs, cached, cached_near = lax.optimization_barrier((query_all, pairs, cached, cached_near))
    parts = attend(query_all, pairs)
    shares = lax.all_to_all(parts, "x", 0, 0)
    tiles = lax.all_to_all(combine(shares), "y", 0, 0)
    strip = jnp.sum(tiles.astype(jnp.float32), axis=0).astype(jnp.bfloat16)
    strip = jnp.pad(strip, ((2, 0), (0, 0), (0, 0)))
    strip = lax.all_to_all(jnp.stack([strip[frame : frame + 3] for frame in range(4)]), "sec", 0, 0)
    strip = jnp.sum(strip.astype(jnp.float32), axis=0).astype(jnp.bfloat16)
    turned = [(p * 4 + g, g * 4 + p) for p in range(4) for g in range(4)]
    near = lax.ppermute(strip, SP, next_pairs(True)) + cached_near
    own = lax.ppermute(strip, ("x", "zh"), turned) + cached
    own, near = own[:, :22], near[:, :22]
    low, high = own[:, :, :MIX], own[:, :, MIX:]
    first = jnp.where(half == 0, near[:, :, MIX:], low)
    middle = jnp.where(half == 0, low, high)
    last = jnp.where(half == 0, high, near[:, :, :MIX])
    frames = jnp.stack([first, middle, last], axis=1)
    frames = frames.reshape(3, 3, 22, 2, 2, 16).transpose(0, 1, 3, 2, 4, 5).reshape(3, 6, 44, 16)
    frames = frames[:, 1:5, 1:43]
    line = jnp.arange(4)[:, None, None]
    spot = jnp.arange(42)[None, :, None]
    outside = (
        ((tile_row == 0) & (line == 0))
        | ((tile_row == 31) & (line == 3))
        | ((tile_col == 0) & (spot == 0))
        | ((tile_col == 3) & (spot == 41))
    )
    frames = jnp.where(outside[None], jnp.zeros_like(frames), frames)
    windows = [
        frames[step_t, step_y : step_y + 2, step_x : step_x + 40, :]
        for step_t in range(3)
        for step_y in range(3)
        for step_x in range(3)
    ]
    columns = jnp.stack(windows, axis=2).reshape(80, 27 * 16)
    output = jnp.dot(columns, kernel, preferred_element_type=jnp.float32) + bias[None, :]
    return output.reshape(1, 1, 2, 40, kernel.shape[1]).astype(jnp.bfloat16)


def solution(mesh):
    fine = Mesh(mesh.devices.reshape(4, 4, 4, 8), ("sec", *SP))
    placed = (
        P(SP, "sec"),
        P(SP, "sec"),
        P(SP, "sec"),
        P(None, SP),
        P(None, SP),
        P("sec", None),
        P(),
        P(),
        P(None, SP, None, None, None),
    )
    return jax.shard_map(
        on_device,
        mesh=fine,
        in_specs=placed,
        out_specs=P("sec", SP, None, None, None),
        check_vma=False,
    )
```

```python
import math

import jax
import jax.numpy as jnp
import numpy as np
from jax import lax
from jax.experimental import pallas as pl
from jax.experimental.pallas import tpu as pltpu
from jax.sharding import Mesh
from jax.sharding import PartitionSpec as P

HD = 128
HEADS_SEC = 8
Q_OWN = 80
K_OWN = 96
V_ROWS = K_OWN // 2
KV_ROWS = K_OWN + V_ROWS
OWN_ROWS = KV_ROWS + Q_OWN + 32
MIX = 64
GRID_W = 80
HALF_W = GRID_W // 2
FRAME = 2560
KEYS_PART = 3072
Q_BLOCK = 640
ROWS_BLOCK = Q_BLOCK // GRID_W
SUB = 640
STRIP = 24
MSG = 4 * GRID_W + 32
TILE_W = 20
C_OUT = 384
SP = ("x", "zh", "y")
MIB = 1024 * 1024
HERE = pl.BlockSpec(memory_space=pltpu.VMEM)


def frequency_row():
    sixth = HD // 6
    time_pairs = (HD - 4 * sixth) // 2
    time = 10000.0 ** (-np.arange(time_pairs) / time_pairs)
    space = 10000.0 ** (-np.arange(sixth) / sixth)
    pairs = np.concatenate([time, space, space])
    return np.repeat(pairs, 2).astype(np.float32)[None, :]


def row_order():
    order = np.zeros((2, 2 * MIX, MIX), np.float32)
    for ch in range(16):
        for ab in range(4):
            for side in range(2):
                order[side, side * MIX + ab * 16 + ch, ch * 4 + ab] = 1.0
    return order


def patch_order():
    pick = np.zeros((2, 32, 40), np.float32)
    place = np.zeros((2, MIX, HD), np.float32)
    for side in range(2):
        for patch in range(TILE_W):
            pick[side, patch, 2 * patch + side] = 1.0
        for line in range(4):
            for ch in range(16):
                place[side, line * 16 + ch, line * 32 + side * 16 + ch] = 1.0
    return pick, place


def turn_tables(positions, freq):
    count = positions.shape[1]
    spot = positions.astype(jnp.float32)
    same = lax.broadcasted_iota(jnp.int32, (count, count), 0) == lax.broadcasted_iota(jnp.int32, (count, count), 1)
    column = [jnp.sum(jnp.where(same, spot[i : i + 1], 0.0), axis=1, keepdims=True) for i in range(3)]
    lane = lax.broadcasted_iota(jnp.int32, (count, HD), 1)
    base = jnp.where(lane < 44, column[0], jnp.where(lane < 86, column[1], column[2]))
    angle = base * freq
    cosine = jnp.cos(angle)
    sine = jnp.sin(angle)
    even = lax.rem(lane, 2) == 0
    zero = jnp.zeros_like(sine)
    return cosine, jnp.where(even, -sine, zero), jnp.where(even, zero, sine)


def turn(vectors, tables):
    cosine, from_next, from_last = tables
    wide = vectors.astype(jnp.float32)
    out = wide * cosine + pltpu.roll(wide, HD - 1, 1) * from_next + pltpu.roll(wide, 1, 1) * from_last
    return out.astype(jnp.bfloat16)


def prepare_kernel(qpos, kpos, freq, order, pick, place, queries, keys, values, mixing, cache, out):
    q_tables = turn_tables(qpos[...], freq[...])
    k_tables = turn_tables(kpos[...], freq[...])
    tile = jnp.zeros((32, HD), jnp.float32)
    for side in range(2):
        column = lax.dot_general(
            pick[side], cache[...], (((1,), (1,)), ((), ())), preferred_element_type=jnp.float32
        )
        tile = tile + jnp.dot(column.astype(jnp.bfloat16), place[side], preferred_element_type=jnp.float32)
    tile = tile.astype(jnp.bfloat16)
    mixed = [
        jnp.dot(order[side], mixing[...], preferred_element_type=jnp.float32).astype(jnp.bfloat16)
        for side in range(2)
    ]
    for head in range(HEADS_SEC):
        cols = slice(head * HD, (head + 1) * HD)
        out[head, 0:K_OWN, :] = turn(keys[:, cols], k_tables)
        value = values[:, cols]
        mix_low = lax.dot_general(
            value[:V_ROWS], mixed[0][:, cols], (((1,), (1,)), ((), ())), preferred_element_type=jnp.float32
        )
        mix_high = lax.dot_general(
            value[V_ROWS:], mixed[1][:, cols], (((1,), (1,)), ((), ())), preferred_element_type=jnp.float32
        )
        out[head, K_OWN:KV_ROWS, :] = (mix_low + mix_high).astype(jnp.bfloat16)
        out[head, KV_ROWS : KV_ROWS + Q_OWN, :] = turn(queries[:, cols], q_tables)
        out[head, KV_ROWS + Q_OWN : OWN_ROWS, :] = tile


def prepare(qpos, kpos, queries, keys, values, mixing, cache):
    return pl.pallas_call(
        prepare_kernel,
        in_specs=[HERE] * 11,
        out_specs=HERE,
        out_shape=jax.ShapeDtypeStruct((HEADS_SEC, OWN_ROWS, HD), jnp.bfloat16),
        compiler_params=pltpu.CompilerParams(vmem_limit_bytes=56 * MIB),
        cost_estimate=pl.CostEstimate(flops=50000000, bytes_accessed=1200000, transcendentals=0),
        name="prepare",
    )(
        qpos,
        kpos,
        jnp.asarray(frequency_row()),
        jnp.asarray(row_order(), jnp.bfloat16),
        *(jnp.asarray(part, jnp.bfloat16) for part in patch_order()),
        queries,
        keys,
        values,
        mixing.T,
        cache.transpose(0, 1, 2, 4, 3).reshape(MIX, 40),
    )


def attend_kernel(*refs):
    q_ref, kv_refs, o_ref = refs[0], refs[1:5], refs[5]
    q_buf, k_buf, v_buf, s_even, s_odd, levels = refs[6:]
    lane = lax.broadcasted_iota(jnp.int32, (V_ROWS, HD), 1)
    ones = jnp.where(lane == MIX, 1.0, 0.0)
    for part in range(q_ref.shape[0]):
        q_buf[part * Q_OWN : (part + 1) * Q_OWN] = q_ref[part]
    for piece in range(4):
        for part in range(8):
            at = (piece * 8 + part) * K_OWN
            k_buf[at : at + K_OWN] = kv_refs[piece][part, 0:K_OWN, :]
            both = kv_refs[piece][part, K_OWN:KV_ROWS, :].astype(jnp.float32)
            v_buf[at : at + V_ROWS] = jnp.where(lane < MIX, both, ones).astype(jnp.bfloat16)
            other = pltpu.roll(both, MIX, 1)
            v_buf[at + V_ROWS : at + K_OWN] = jnp.where(lane < MIX, other, ones).astype(jnp.bfloat16)

    scale = jnp.float32(math.log2(math.e) / math.sqrt(HD))
    diagonal = lax.broadcasted_iota(jnp.int32, (GRID_W, HD), 1) == lax.broadcasted_iota(jnp.int32, (GRID_W, HD), 0)
    low_lane = lax.broadcasted_iota(jnp.int32, (HALF_W, HD), 1) < MIX

    def score(block):
        at = pl.multiple_of(block * SUB, 16)
        return lax.dot_general(
            q_buf[pl.ds(at, SUB), :], k_buf[...], (((1,), (1,)), ((), ())), preferred_element_type=jnp.float32
        )

    def finish(piece, s_ref):
        scores = s_ref[...]
        top = jnp.max(scores, axis=1, keepdims=True)
        weights = jnp.exp2((scores - top) * scale).astype(jnp.bfloat16)
        sums = jnp.dot(weights, v_buf[...], preferred_element_type=jnp.float32)
        total = sums[:, MIX : MIX + 1]
        mean = sums / total
        level = top * scale + jnp.log2(total)
        for pair in range(4):
            lines = []
            for patch_row in (2 * pair, 2 * pair + 1):
                at = patch_row * GRID_W
                low = mean[at : at + HALF_W]
                high = pltpu.roll(mean[at + HALF_W : at + GRID_W], MIX, 1)
                lines.append(jnp.where(low_lane, low, high))
                line = jnp.sum(jnp.where(diagonal, level[at : at + GRID_W], 0.0), axis=0, keepdims=True)
                first = line.astype(jnp.bfloat16).astype(jnp.float32)
                line = line - first
                second = line.astype(jnp.bfloat16).astype(jnp.float32)
                third = line - second
                spot = patch_row % 2 * 4
                levels[pair, piece * 8 + spot : piece * 8 + spot + 4] = jnp.concatenate(
                    [first, second, third, jnp.zeros((1, HD), jnp.float32)], axis=0
                )
            o_ref[pair, piece * GRID_W : (piece + 1) * GRID_W] = jnp.concatenate(lines, axis=0).astype(jnp.bfloat16)

    s_even[...] = score(0)
    s_odd[...] = score(1)
    finish(0, s_even)
    s_even[...] = score(2)
    finish(1, s_odd)
    s_odd[...] = score(3)
    finish(2, s_even)
    finish(3, s_odd)
    o_ref[:, 4 * GRID_W : MSG] = levels[...].astype(jnp.bfloat16)


def attend(queries, pairs):
    return pl.pallas_call(
        attend_kernel,
        in_specs=[HERE] * 5,
        out_specs=HERE,
        out_shape=jax.ShapeDtypeStruct((4, MSG, HD), jnp.bfloat16),
        scratch_shapes=[
            pltpu.VMEM((FRAME, HD), jnp.bfloat16),
            pltpu.VMEM((KEYS_PART, HD), jnp.bfloat16),
            pltpu.VMEM((KEYS_PART, HD), jnp.bfloat16),
            pltpu.VMEM((SUB, KEYS_PART), jnp.float32),
            pltpu.VMEM((SUB, KEYS_PART), jnp.float32),
            pltpu.VMEM((4, 32, HD), jnp.float32),
        ],
        compiler_params=pltpu.CompilerParams(vmem_limit_bytes=42 * MIB),
        cost_estimate=pl.CostEstimate(flops=4 * FRAME * KEYS_PART * HD, bytes_accessed=2000000, transcendentals=0),
        name="attend",
    )(queries.reshape(FRAME // Q_OWN, Q_OWN, HD), *pairs)


def combine_kernel(r_ref, o_ref):
    shares = r_ref.shape[0]
    lane = lax.broadcasted_iota(jnp.int32, (HALF_W, HD), 1)
    row = lax.broadcasted_iota(jnp.int32, (HALF_W, HD), 0)
    zeros = jnp.zeros((16, HD), jnp.float32)
    low_lane = lax.broadcasted_iota(jnp.int32, (STRIP, HD), 1) < MIX
    lines = []
    asides = [r_ref[share, 4 * GRID_W : MSG].astype(jnp.float32) for share in range(shares)]
    for patch_row in range(ROWS_BLOCK):
        at, spot = patch_row % 2 * HALF_W, patch_row * 4
        blocks = [
            r_ref[share, patch_row // 2 * GRID_W : (patch_row // 2 + 1) * GRID_W].astype(jnp.float32)[at : at + HALF_W]
            for share in range(shares)
        ]
        levels = [a[spot : spot + 1] + a[spot + 1 : spot + 2] + a[spot + 2 : spot + 3] for a in asides]
        top = levels[0]
        for level in levels[1:]:
            top = jnp.maximum(top, level)
        powers = [jnp.exp2(level - top) for level in levels]
        total = powers[0]
        for power in powers[1:]:
            total = total + power
        result = jnp.zeros((HALF_W, HD), jnp.float32)
        for block, power in zip(blocks, powers):
            weight = power / total
            low = jnp.sum(jnp.where(lane == row, weight, 0.0), axis=1, keepdims=True)
            high = jnp.sum(jnp.where(lane == row + HALF_W, weight, 0.0), axis=1, keepdims=True)
            result = result + jnp.where(lane < MIX, low, high) * block
        line = jnp.concatenate([zeros[:1], result, pltpu.roll(result, MIX, 1), zeros], axis=0)
        line = line[: 2 * HALF_W + 16]
        lines.append(line if patch_row % 2 == 0 else pltpu.roll(line, MIX, 1))
    for group in range(4):
        for tile in range(4):
            at = tile * TILE_W
            piece = jnp.where(low_lane, lines[2 * group][at : at + STRIP], lines[2 * group + 1][at : at + STRIP])
            piece = piece.astype(jnp.bfloat16)
            for copy in range(2):
                o_ref[copy * 4 + tile, group] = piece


def combine(received):
    return pl.pallas_call(
        combine_kernel,
        in_specs=[HERE],
        out_specs=HERE,
        out_shape=jax.ShapeDtypeStruct((8, 4, STRIP, HD), jnp.bfloat16),
        compiler_params=pltpu.CompilerParams(vmem_limit_bytes=8 * MIB),
        cost_estimate=pl.CostEstimate(flops=1000000, bytes_accessed=900000, transcendentals=0),
        name="combine",
    )(received)


def convolve_kernel(half, own, near, kernel, bias, o_ref, weights, rows):
    tap = {(0, 0, 1): 0, (0, 1, 0): 1, (0, 1, 1): 2, (1, 0, 0): 0, (1, 0, 1): 1, (1, 1, 0): 2}
    nothing = jnp.zeros((16, C_OUT), jnp.bfloat16)
    at = 0
    for side in range(2):
        for shift in range(2):
            for frame in range(3):
                for line in range(4):
                    for b in range(2):
                        step_x = tap.get((side, shift, b))
                        if line == 0 or step_x is None:
                            weights[at : at + 16] = nothing
                        else:
                            source = ((frame * 3 + line - 1) * 3 + step_x) * 16
                            weights[at : at + 16] = kernel[source : source + 16]
                        at += 16
    lane = lax.broadcasted_iota(jnp.int32, (STRIP, HD), 1)
    low = lane < MIX
    top = half[0] == 0
    lines = ([], [])
    for frame in range(3):
        mine = own[frame].astype(jnp.float32)
        beside = near[frame].astype(jnp.float32)
        mine_turned = pltpu.roll(mine, MIX, 1)
        beside_turned = pltpu.roll(beside, MIX, 1)
        upper = jnp.where(top, jnp.where(low, beside_turned, mine_turned), mine)
        lower = jnp.where(top, mine_turned, beside)
        lines[0].append(upper)
        lines[1].append(jnp.where(lane < 96, pltpu.roll(upper, 96, 1), pltpu.roll(lower, 96, 1)))
    spare = jnp.zeros((8, HD), jnp.float32)
    lines = [[jnp.concatenate([part, spare], axis=0) for part in parts] for parts in lines]
    for side in range(2):
        taps = jnp.concatenate(
            [
                jnp.concatenate([part[side + s : side + s + STRIP] for s in range(2) for part in parts], axis=1)
                for parts in lines
            ],
            axis=0,
        ).astype(jnp.bfloat16)
        size = 6 * HD
        sums = jnp.dot(taps, weights[side * size : (side + 1) * size, :], preferred_element_type=jnp.float32)
        sums = sums + bias[...]
        for a in range(2):
            for part in range(C_OUT // HD):
                block = sums[a * STRIP : a * STRIP + TILE_W, part * HD : (part + 1) * HD]
                rows[part, pl.ds(a * 40 + side, TILE_W, 2), :] = block
    o_ref[...] = jnp.concatenate([rows[part] for part in range(C_OUT // HD)], axis=1).astype(jnp.bfloat16)


def convolve(half, own, near, kernel, bias):
    return pl.pallas_call(
        convolve_kernel,
        in_specs=[pl.BlockSpec(memory_space=pltpu.SMEM)] + [HERE] * 4,
        out_specs=HERE,
        out_shape=jax.ShapeDtypeStruct((80, C_OUT), jnp.bfloat16),
        scratch_shapes=[pltpu.VMEM((12 * HD, C_OUT), jnp.bfloat16), pltpu.VMEM((C_OUT // HD, 80, HD), jnp.float32)],
        compiler_params=pltpu.CompilerParams(vmem_limit_bytes=8 * MIB),
        cost_estimate=pl.CostEstimate(flops=100000000, bytes_accessed=500000, transcendentals=0),
        name="convolve",
    )(half, own, near, kernel, bias)


def from_ahead(value, axis, steps):
    return lax.ppermute(value, axis, [((spot + steps) % 4, spot) for spot in range(4)])


def next_pair(value, axes):
    pairs = [(i, i + 8) for i in range(120) if i % 8 < 4] + [(i, i - 8) for i in range(8, 128) if i % 8 >= 4]
    return lax.ppermute(value, axes, pairs)


def cache_strips(tiles, tile_col):
    wide = tiles.reshape(2, 4, 32, HD)[:, :, :TILE_W].reshape(2, GRID_W, HD)
    wide = jnp.pad(wide, ((0, 0), (1, 3), (0, 0)))
    wide = lax.dynamic_slice_in_dim(wide, tile_col * TILE_W, STRIP, 1)
    return wide.reshape(2, STRIP, 2, MIX).transpose(2, 1, 0, 3).reshape(2, STRIP, HD)


def on_device(queries, keys, values, query_positions, key_positions, mixing, kernel, bias, cache):
    sp_index = lax.axis_index(SP)
    section = lax.axis_index("sec")
    half = lax.axis_index("y") // 4
    tile_col = sp_index % 4
    own = prepare(query_positions, key_positions, queries, keys, values, mixing, cache)
    own = lax.all_to_all(own, "y", 0, 0)
    kv_own = own[:, :KV_ROWS]
    q_own = own[:, KV_ROWS : KV_ROWS + Q_OWN]
    query_all = lax.all_to_all(jnp.broadcast_to(q_own[None], (4, *q_own.shape)), "zh", 0, 0)
    pairs = [kv_own] + [from_ahead(kv_own, "x", step) for step in (1, 2, 3)]
    cached = cache_strips(own[:, KV_ROWS + Q_OWN :], tile_col)
    query_all, pairs, cached = lax.optimization_barrier((query_all, pairs, cached))
    parts = attend(query_all, pairs)
    shares = lax.all_to_all(parts, "zh", 0, 0)
    tiles = lax.all_to_all(combine(shares), "y", 0, 0)
    strip = jnp.sum(tiles.astype(jnp.float32), axis=0).astype(jnp.bfloat16)
    strip = lax.all_to_all(jnp.broadcast_to(strip[None], (4, *strip.shape)).reshape(16, STRIP, HD), ("sec", "x"), 0, 0)
    strip = jnp.sum(strip.reshape(4, 4, STRIP, HD).astype(jnp.float32), axis=0).astype(jnp.bfloat16)
    strip = jnp.concatenate([cached, strip], axis=0)
    frames = lax.dynamic_slice_in_dim(strip, section, 3, 0)
    output = convolve(half.reshape(1), frames, next_pair(frames, SP), kernel, bias[None])
    return output.reshape(1, 1, 2, 40, kernel.shape[1])


def solution(mesh):
    fine = Mesh(mesh.devices.reshape(4, 4, 4, 8), ("sec", *SP))
    placed = (
        P(SP, "sec"),
        P(SP, "sec"),
        P(SP, "sec"),
        P(None, SP),
        P(None, SP),
        P("sec", None),
        P(),
        P(),
        P(None, SP, None, None, None),
    )
    return jax.shard_map(
        on_device,
        mesh=fine,
        in_specs=placed,
        out_specs=P("sec", SP, None, None, None),
        check_vma=False,
    )
```

```python
import math

import jax
import jax.numpy as jnp
import numpy as np
from jax import lax
from jax.experimental import pallas as pl
from jax.experimental.pallas import tpu as pltpu
from jax.sharding import Mesh
from jax.sharding import PartitionSpec as P

HD = 128
STRIP = 24
HEADS_SEC = 8
Q_OWN = 80
K_OWN = 96
V_ROWS = K_OWN // 2
KV_ROWS = K_OWN + V_ROWS
OWN_ROWS = KV_ROWS + Q_OWN + STRIP
MIX = 64
GRID_W = 80
HALF_W = GRID_W // 2
FRAME = 2560
KEYS_PART = 3072
Q_BLOCK = 640
ROWS_BLOCK = Q_BLOCK // GRID_W
SUB = 640
MSG = 4 * GRID_W + 32
TILE_W = 20
C_OUT = 384
SP = ("x", "zh", "y")
MIB = 1024 * 1024
HERE = pl.BlockSpec(memory_space=pltpu.VMEM)


def frequency_row():
    sixth = HD // 6
    time_pairs = (HD - 4 * sixth) // 2
    time = 10000.0 ** (-np.arange(time_pairs) / time_pairs)
    space = 10000.0 ** (-np.arange(sixth) / sixth)
    pairs = np.concatenate([time, space, space])
    return np.repeat(pairs, 2).astype(np.float32)[None, :]


def row_order():
    order = np.zeros((2, 2 * MIX, MIX), np.float32)
    for ch in range(16):
        for ab in range(4):
            for side in range(2):
                order[side, side * MIX + ab * 16 + ch, ch * 4 + ab] = 1.0
    return order


def patch_order():
    pick = np.zeros((2, STRIP, 40), np.float32)
    place = np.zeros((2, MIX, HD), np.float32)
    for side in range(2):
        for patch in range(TILE_W):
            pick[side, patch, 2 * patch + side] = 1.0
        for line in range(4):
            for ch in range(16):
                place[side, line * 16 + ch, line * 32 + side * 16 + ch] = 1.0
    return pick, place


def turn_tables(positions, freq):
    count = positions.shape[1]
    spot = positions.astype(jnp.float32)
    same = lax.broadcasted_iota(jnp.int32, (count, count), 0) == lax.broadcasted_iota(jnp.int32, (count, count), 1)
    column = [jnp.sum(jnp.where(same, spot[i : i + 1], 0.0), axis=1, keepdims=True) for i in range(3)]
    lane = lax.broadcasted_iota(jnp.int32, (count, HD), 1)
    base = jnp.where(lane < 44, column[0], jnp.where(lane < 86, column[1], column[2]))
    angle = base * freq
    cosine = jnp.cos(angle)
    sine = jnp.sin(angle)
    even = lax.rem(lane, 2) == 0
    zero = jnp.zeros_like(sine)
    return cosine, jnp.where(even, -sine, zero), jnp.where(even, zero, sine)


def turn(vectors, tables):
    cosine, from_next, from_last = tables
    wide = vectors.astype(jnp.float32)
    out = wide * cosine + pltpu.roll(wide, HD - 1, 1) * from_next + pltpu.roll(wide, 1, 1) * from_last
    return out.astype(jnp.bfloat16)


def prepare_kernel(qpos, kpos, freq, order, pick, place, queries, keys, values, mixing, cache, out):
    q_tables = turn_tables(qpos[...], freq[...])
    k_tables = turn_tables(kpos[...], freq[...])
    tile = jnp.zeros((STRIP, HD), jnp.float32)
    for side in range(2):
        column = lax.dot_general(
            pick[side], cache[...], (((1,), (1,)), ((), ())), preferred_element_type=jnp.float32
        )
        tile = tile + jnp.dot(column.astype(jnp.bfloat16), place[side], preferred_element_type=jnp.float32)
    tile = tile.astype(jnp.bfloat16)
    mixed = [
        jnp.dot(order[side], mixing[...], preferred_element_type=jnp.float32).astype(jnp.bfloat16)
        for side in range(2)
    ]
    for head in range(HEADS_SEC):
        cols = slice(head * HD, (head + 1) * HD)
        out[head, 0:K_OWN, :] = turn(keys[:, cols], k_tables)
        value = values[:, cols]
        mix_low = lax.dot_general(
            value[:V_ROWS], mixed[0][:, cols], (((1,), (1,)), ((), ())), preferred_element_type=jnp.float32
        )
        mix_high = lax.dot_general(
            value[V_ROWS:], mixed[1][:, cols], (((1,), (1,)), ((), ())), preferred_element_type=jnp.float32
        )
        out[head, K_OWN:KV_ROWS, :] = (mix_low + mix_high).astype(jnp.bfloat16)
        out[head, KV_ROWS : KV_ROWS + Q_OWN, :] = turn(queries[:, cols], q_tables)
        out[head, KV_ROWS + Q_OWN : OWN_ROWS, :] = tile


def prepare(qpos, kpos, queries, keys, values, mixing, cache):
    return pl.pallas_call(
        prepare_kernel,
        in_specs=[HERE] * 11,
        out_specs=HERE,
        out_shape=jax.ShapeDtypeStruct((HEADS_SEC, OWN_ROWS, HD), jnp.bfloat16),
        compiler_params=pltpu.CompilerParams(vmem_limit_bytes=56 * MIB),
        cost_estimate=pl.CostEstimate(flops=50000000, bytes_accessed=1200000, transcendentals=0),
        name="prepare",
    )(
        qpos,
        kpos,
        jnp.asarray(frequency_row()),
        jnp.asarray(row_order(), jnp.bfloat16),
        *(jnp.asarray(part, jnp.bfloat16) for part in patch_order()),
        queries,
        keys,
        values,
        mixing.T,
        cache.transpose(0, 1, 2, 4, 3).reshape(MIX, 40),
    )


def attend_kernel(*refs):
    q_ref, kv_refs, o_ref = refs[0], refs[1:6], refs[6]
    q_buf, k_buf, v_buf, s_even, s_odd, levels = refs[7:]
    lane = lax.broadcasted_iota(jnp.int32, (V_ROWS, HD), 1)
    ones = jnp.where(lane == MIX, 1.0, 0.0)
    for part in range(q_ref.shape[0]):
        q_buf[part * Q_OWN : (part + 1) * Q_OWN] = q_ref[part]
    at = 0
    for kv_ref in kv_refs:
        for part in range(kv_ref.shape[0]):
            k_buf[at : at + K_OWN] = kv_ref[part, 0:K_OWN, :]
            both = kv_ref[part, K_OWN:KV_ROWS, :].astype(jnp.float32)
            v_buf[at : at + V_ROWS] = jnp.where(lane < MIX, both, ones).astype(jnp.bfloat16)
            other = pltpu.roll(both, MIX, 1)
            v_buf[at + V_ROWS : at + K_OWN] = jnp.where(lane < MIX, other, ones).astype(jnp.bfloat16)
            at += K_OWN

    scale = jnp.float32(math.log2(math.e) / math.sqrt(HD))
    diagonal = lax.broadcasted_iota(jnp.int32, (GRID_W, HD), 1) == lax.broadcasted_iota(jnp.int32, (GRID_W, HD), 0)
    low_lane = lax.broadcasted_iota(jnp.int32, (HALF_W, HD), 1) < MIX

    def score(block):
        at = pl.multiple_of(block * SUB, 16)
        return lax.dot_general(
            q_buf[pl.ds(at, SUB), :], k_buf[...], (((1,), (1,)), ((), ())), preferred_element_type=jnp.float32
        )

    def finish(piece, s_ref):
        scores = s_ref[...]
        top = jnp.max(scores, axis=1, keepdims=True)
        weights = jnp.exp2((scores - top) * scale).astype(jnp.bfloat16)
        sums = jnp.dot(weights, v_buf[...], preferred_element_type=jnp.float32)
        total = sums[:, MIX : MIX + 1]
        mean = sums / total
        level = top * scale + jnp.log2(total)
        for pair in range(4):
            lines = []
            for patch_row in (2 * pair, 2 * pair + 1):
                at = patch_row * GRID_W
                low = mean[at : at + HALF_W]
                high = pltpu.roll(mean[at + HALF_W : at + GRID_W], MIX, 1)
                lines.append(jnp.where(low_lane, low, high))
                line = jnp.sum(jnp.where(diagonal, level[at : at + GRID_W], 0.0), axis=0, keepdims=True)
                first = line.astype(jnp.bfloat16).astype(jnp.float32)
                line = line - first
                second = line.astype(jnp.bfloat16).astype(jnp.float32)
                third = line - second
                spot = patch_row % 2 * 4
                levels[pair, piece * 8 + spot : piece * 8 + spot + 4] = jnp.concatenate(
                    [first, second, third, jnp.zeros((1, HD), jnp.float32)], axis=0
                )
            o_ref[pair, piece * GRID_W : (piece + 1) * GRID_W] = jnp.concatenate(lines, axis=0).astype(jnp.bfloat16)

    s_even[...] = score(0)
    s_odd[...] = score(1)
    finish(0, s_even)
    s_even[...] = score(2)
    finish(1, s_odd)
    s_odd[...] = score(3)
    finish(2, s_even)
    finish(3, s_odd)
    o_ref[:, 4 * GRID_W : MSG] = levels[...].astype(jnp.bfloat16)


def attend(queries, pairs):
    return pl.pallas_call(
        attend_kernel,
        in_specs=[HERE] * 6,
        out_specs=HERE,
        out_shape=jax.ShapeDtypeStruct((4, MSG, HD), jnp.bfloat16),
        scratch_shapes=[
            pltpu.VMEM((FRAME, HD), jnp.bfloat16),
            pltpu.VMEM((KEYS_PART, HD), jnp.bfloat16),
            pltpu.VMEM((KEYS_PART, HD), jnp.bfloat16),
            pltpu.VMEM((SUB, KEYS_PART), jnp.float32),
            pltpu.VMEM((SUB, KEYS_PART), jnp.float32),
            pltpu.VMEM((4, 32, HD), jnp.float32),
        ],
        compiler_params=pltpu.CompilerParams(vmem_limit_bytes=42 * MIB),
        cost_estimate=pl.CostEstimate(flops=4 * FRAME * KEYS_PART * HD, bytes_accessed=2000000, transcendentals=0),
        name="attend",
    )(queries.reshape(FRAME // Q_OWN, Q_OWN, HD), *pairs)


def combine_kernel(r_ref, o_ref):
    shares = r_ref.shape[0]
    lane = lax.broadcasted_iota(jnp.int32, (HALF_W, HD), 1)
    row = lax.broadcasted_iota(jnp.int32, (HALF_W, HD), 0)
    zeros = jnp.zeros((16, HD), jnp.float32)
    low_lane = lax.broadcasted_iota(jnp.int32, (STRIP, HD), 1) < MIX
    lines = []
    asides = [r_ref[share, 4 * GRID_W : MSG].astype(jnp.float32) for share in range(shares)]
    for patch_row in range(ROWS_BLOCK):
        at, spot = patch_row % 2 * HALF_W, patch_row * 4
        blocks = [
            r_ref[share, patch_row // 2 * GRID_W : (patch_row // 2 + 1) * GRID_W].astype(jnp.float32)[at : at + HALF_W]
            for share in range(shares)
        ]
        levels = [a[spot : spot + 1] + a[spot + 1 : spot + 2] + a[spot + 2 : spot + 3] for a in asides]
        top = levels[0]
        for level in levels[1:]:
            top = jnp.maximum(top, level)
        powers = [jnp.exp2(level - top) for level in levels]
        total = powers[0]
        for power in powers[1:]:
            total = total + power
        result = jnp.zeros((HALF_W, HD), jnp.float32)
        for block, power in zip(blocks, powers):
            weight = power / total
            low = jnp.sum(jnp.where(lane == row, weight, 0.0), axis=1, keepdims=True)
            high = jnp.sum(jnp.where(lane == row + HALF_W, weight, 0.0), axis=1, keepdims=True)
            result = result + jnp.where(lane < MIX, low, high) * block
        line = jnp.concatenate([zeros[:1], result, pltpu.roll(result, MIX, 1), zeros], axis=0)
        line = line[: 2 * HALF_W + 16]
        lines.append(line if patch_row % 2 == 0 else pltpu.roll(line, MIX, 1))
    for group in range(4):
        for tile in range(4):
            at = tile * TILE_W
            piece = jnp.where(low_lane, lines[2 * group][at : at + STRIP], lines[2 * group + 1][at : at + STRIP])
            piece = piece.astype(jnp.bfloat16)
            for copy in range(2):
                o_ref[copy * 4 + tile, group] = piece


def combine(received):
    return pl.pallas_call(
        combine_kernel,
        in_specs=[HERE],
        out_specs=HERE,
        out_shape=jax.ShapeDtypeStruct((8, 4, STRIP, HD), jnp.bfloat16),
        compiler_params=pltpu.CompilerParams(vmem_limit_bytes=8 * MIB),
        cost_estimate=pl.CostEstimate(flops=1000000, bytes_accessed=900000, transcendentals=0),
        name="combine",
    )(received)


def convolve_kernel(half, own, near, kernel, bias, o_ref, weights, rows):
    tap = {(0, 0, 1): 0, (0, 1, 0): 1, (0, 1, 1): 2, (1, 0, 0): 0, (1, 0, 1): 1, (1, 1, 0): 2}
    nothing = jnp.zeros((16, C_OUT), jnp.bfloat16)
    at = 0
    for side in range(2):
        for shift in range(2):
            for frame in range(3):
                for line in range(4):
                    for b in range(2):
                        step_x = tap.get((side, shift, b))
                        if line == 0 or step_x is None:
                            weights[at : at + 16] = nothing
                        else:
                            source = ((frame * 3 + line - 1) * 3 + step_x) * 16
                            weights[at : at + 16] = kernel[source : source + 16]
                        at += 16
    lane = lax.broadcasted_iota(jnp.int32, (STRIP, HD), 1)
    low = lane < MIX
    top = half[0] == 0
    lines = ([], [])
    for frame in range(3):
        mine = own[frame].astype(jnp.float32)
        beside = near[frame].astype(jnp.float32)
        mine_turned = pltpu.roll(mine, MIX, 1)
        beside_turned = pltpu.roll(beside, MIX, 1)
        upper = jnp.where(top, jnp.where(low, beside_turned, mine_turned), mine)
        lower = jnp.where(top, mine_turned, beside)
        lines[0].append(upper)
        lines[1].append(jnp.where(lane < 96, pltpu.roll(upper, 96, 1), pltpu.roll(lower, 96, 1)))
    spare = jnp.zeros((8, HD), jnp.float32)
    lines = [[jnp.concatenate([part, spare], axis=0) for part in parts] for parts in lines]
    for side in range(2):
        taps = jnp.concatenate(
            [
                jnp.concatenate([part[side + s : side + s + STRIP] for s in range(2) for part in parts], axis=1)
                for parts in lines
            ],
            axis=0,
        ).astype(jnp.bfloat16)
        size = 6 * HD
        sums = jnp.dot(taps, weights[side * size : (side + 1) * size, :], preferred_element_type=jnp.float32)
        sums = sums + bias[...]
        for a in range(2):
            for part in range(C_OUT // HD):
                block = sums[a * STRIP : a * STRIP + TILE_W, part * HD : (part + 1) * HD]
                rows[part, pl.ds(a * 40 + side, TILE_W, 2), :] = block
    o_ref[...] = jnp.concatenate([rows[part] for part in range(C_OUT // HD)], axis=1).astype(jnp.bfloat16)


def convolve(half, own, near, kernel, bias):
    return pl.pallas_call(
        convolve_kernel,
        in_specs=[pl.BlockSpec(memory_space=pltpu.SMEM)] + [HERE] * 4,
        out_specs=HERE,
        out_shape=jax.ShapeDtypeStruct((80, C_OUT), jnp.bfloat16),
        scratch_shapes=[pltpu.VMEM((12 * HD, C_OUT), jnp.bfloat16), pltpu.VMEM((C_OUT // HD, 80, HD), jnp.float32)],
        compiler_params=pltpu.CompilerParams(vmem_limit_bytes=8 * MIB),
        cost_estimate=pl.CostEstimate(flops=100000000, bytes_accessed=500000, transcendentals=0),
        name="convolve",
    )(half, own, near, kernel, bias)


def from_ahead(value, axis, steps):
    return lax.ppermute(value, axis, [((spot + steps) % 4, spot) for spot in range(4)])


def next_pair(value, axes):
    pairs = [(i, i + 8) for i in range(120) if i % 8 < 4] + [(i, i - 8) for i in range(8, 128) if i % 8 >= 4]
    return lax.ppermute(value, axes, pairs)


def cache_strips(tiles, tile_col):
    wide = tiles.reshape(2, 4, STRIP, HD)[:, :, :TILE_W].reshape(2, GRID_W, HD)
    wide = jnp.pad(wide, ((0, 0), (1, 3), (0, 0)))
    wide = lax.dynamic_slice_in_dim(wide, tile_col * TILE_W, STRIP, 1)
    return wide.reshape(2, STRIP, 2, MIX).transpose(2, 1, 0, 3).reshape(2, STRIP, HD)


def on_device(queries, keys, values, query_positions, key_positions, mixing, kernel, bias, cache):
    sp_index = lax.axis_index(SP)
    section = lax.axis_index("sec")
    half = lax.axis_index("y") // 4
    tile_col = sp_index % 4
    own = prepare(query_positions, key_positions, queries, keys, values, mixing, cache)
    own = lax.all_to_all(own, "y", 0, 0)
    kv_own = own[:, :KV_ROWS]
    q_own = own[:, KV_ROWS : KV_ROWS + Q_OWN]
    query_all = lax.all_to_all(jnp.broadcast_to(q_own[None], (4, *q_own.shape)), "zh", 0, 0)
    kv_next = from_ahead(kv_own, "x", 1)
    pairs = [kv_own, kv_next, from_ahead(kv_own, "x", 3), from_ahead(kv_own[:4], "x", 2), from_ahead(kv_next[4:], "x", 1)]
    cached = cache_strips(own[:, KV_ROWS + Q_OWN :], tile_col)
    query_all, pairs, cached = lax.optimization_barrier((query_all, pairs, cached))
    parts = attend(query_all, pairs)
    shares = lax.all_to_all(parts, "zh", 0, 0)
    tiles = lax.all_to_all(combine(shares), "y", 0, 0)
    strip = jnp.sum(tiles.astype(jnp.float32), axis=0).astype(jnp.bfloat16)
    strip = lax.all_to_all(jnp.broadcast_to(strip[None], (4, *strip.shape)).reshape(16, STRIP, HD), ("sec", "x"), 0, 0)
    strip = jnp.sum(strip.reshape(4, 4, STRIP, HD).astype(jnp.float32), axis=0).astype(jnp.bfloat16)
    strip = jnp.concatenate([cached, strip], axis=0)
    frames = lax.dynamic_slice_in_dim(strip, section, 3, 0)
    output = convolve(half.reshape(1), frames, next_pair(frames, SP), kernel, bias[None])
    return output.reshape(1, 1, 2, 40, kernel.shape[1])


def solution(mesh):
    fine = Mesh(mesh.devices.reshape(4, 4, 4, 8), ("sec", *SP))
    placed = (
        P(SP, "sec"),
        P(SP, "sec"),
        P(SP, "sec"),
        P(None, SP),
        P(None, SP),
        P("sec", None),
        P(),
        P(),
        P(None, SP, None, None, None),
    )
    return jax.shard_map(
        on_device,
        mesh=fine,
        in_specs=placed,
        out_specs=P("sec", SP, None, None, None),
        check_vma=False,
    )
```

```python
import math

import jax
import jax.numpy as jnp
import numpy as np
from jax import lax
from jax.experimental import pallas as pl
from jax.experimental.pallas import tpu as pltpu
from jax.sharding import Mesh
from jax.sharding import PartitionSpec as P

HD = 128
STRIP = 24
HEADS_SEC = 8
Q_OWN = 80
K_OWN = 96
V_ROWS = K_OWN // 2
KV_ROWS = K_OWN + V_ROWS
OWN_ROWS = KV_ROWS + Q_OWN + STRIP
MIX = 64
GRID_W = 80
HALF_W = GRID_W // 2
FRAME = 2560
KEYS_PART = 3072
Q_BLOCK = 640
ROWS_BLOCK = Q_BLOCK // GRID_W
SUB = 640
MSG = 4 * GRID_W + 32
TILE_W = 20
C_OUT = 384
SP = ("x", "zh", "y")
MIB = 1024 * 1024
HERE = pl.BlockSpec(memory_space=pltpu.VMEM)


def frequency_row():
    sixth = HD // 6
    time_pairs = (HD - 4 * sixth) // 2
    time = 10000.0 ** (-np.arange(time_pairs) / time_pairs)
    space = 10000.0 ** (-np.arange(sixth) / sixth)
    pairs = np.concatenate([time, space, space])
    return np.repeat(pairs, 2).astype(np.float32)[None, :]


def row_order():
    order = np.zeros((2, 2 * MIX, MIX), np.float32)
    for ch in range(16):
        for ab in range(4):
            for side in range(2):
                order[side, side * MIX + ab * 16 + ch, ch * 4 + ab] = 1.0
    return order


def patch_order():
    pick = np.zeros((2, STRIP, 40), np.float32)
    place = np.zeros((2, MIX, HD), np.float32)
    for side in range(2):
        for patch in range(TILE_W):
            pick[side, patch, 2 * patch + side] = 1.0
        for line in range(4):
            for ch in range(16):
                place[side, line * 16 + ch, line * 32 + side * 16 + ch] = 1.0
    return pick, place


def cosine_sine(angle):
    turns = jnp.floor(angle * jnp.float32(2.0 / math.pi) + 0.5)
    rest = angle - turns * jnp.float32(1.5703125)
    rest = rest - turns * jnp.float32(4.837512969970703e-4)
    rest = rest - turns * jnp.float32(7.549789948768648e-8)
    square = rest * rest
    sine = rest + rest * square * (
        jnp.float32(-1.6666654611e-1) + square * (jnp.float32(8.3321608736e-3) - square * jnp.float32(1.9515295891e-4))
    )
    cosine = 1.0 - 0.5 * square + square * square * (
        jnp.float32(4.166664568298827e-2)
        + square * (jnp.float32(-1.388731625493765e-3) + square * jnp.float32(2.443315711809948e-5))
    )
    quarter = turns.astype(jnp.int32)
    odd = (quarter & 1) == 1
    first, second = jnp.where(odd, sine, cosine), jnp.where(odd, cosine, sine)
    first = jnp.where(((quarter + 1) & 2) == 2, -first, first)
    return first, jnp.where((quarter & 2) == 2, -second, second)


def turn_tables(positions, freq):
    count = positions.shape[1]
    spot = positions.astype(jnp.float32)
    same = lax.broadcasted_iota(jnp.int32, (count, count), 0) == lax.broadcasted_iota(jnp.int32, (count, count), 1)
    column = [jnp.sum(jnp.where(same, spot[i : i + 1], 0.0), axis=1, keepdims=True) for i in range(3)]
    lane = lax.broadcasted_iota(jnp.int32, (count, HD), 1)
    base = jnp.where(lane < 44, column[0], jnp.where(lane < 86, column[1], column[2]))
    angle = base * freq
    cosine, sine = cosine_sine(angle)
    even = lax.rem(lane, 2) == 0
    zero = jnp.zeros_like(sine)
    return cosine, jnp.where(even, -sine, zero), jnp.where(even, zero, sine)


def turn(vectors, tables):
    cosine, from_next, from_last = tables
    wide = vectors.astype(jnp.float32)
    out = wide * cosine + pltpu.roll(wide, HD - 1, 1) * from_next + pltpu.roll(wide, 1, 1) * from_last
    return out.astype(jnp.bfloat16)


def prepare_kernel(qpos, kpos, freq, order, pick, place, queries, keys, values, mixing, cache, out):
    q_tables = turn_tables(qpos[...], freq[...])
    k_tables = turn_tables(kpos[...], freq[...])
    tile = jnp.zeros((STRIP, HD), jnp.float32)
    for side in range(2):
        column = lax.dot_general(
            pick[side], cache[...], (((1,), (1,)), ((), ())), preferred_element_type=jnp.float32
        )
        tile = tile + jnp.dot(column.astype(jnp.bfloat16), place[side], preferred_element_type=jnp.float32)
    tile = tile.astype(jnp.bfloat16)
    mixed = [
        jnp.dot(order[side], mixing[...], preferred_element_type=jnp.float32).astype(jnp.bfloat16)
        for side in range(2)
    ]
    for head in range(HEADS_SEC):
        cols = slice(head * HD, (head + 1) * HD)
        out[head, 0:K_OWN, :] = turn(keys[:, cols], k_tables)
        value = values[:, cols]
        mix_low = lax.dot_general(
            value[:V_ROWS], mixed[0][:, cols], (((1,), (1,)), ((), ())), preferred_element_type=jnp.float32
        )
        mix_high = lax.dot_general(
            value[V_ROWS:], mixed[1][:, cols], (((1,), (1,)), ((), ())), preferred_element_type=jnp.float32
        )
        out[head, K_OWN:KV_ROWS, :] = (mix_low + mix_high).astype(jnp.bfloat16)
        out[head, KV_ROWS : KV_ROWS + Q_OWN, :] = turn(queries[:, cols], q_tables)
        out[head, KV_ROWS + Q_OWN : OWN_ROWS, :] = tile


def prepare(qpos, kpos, queries, keys, values, mixing, cache):
    return pl.pallas_call(
        prepare_kernel,
        in_specs=[HERE] * 11,
        out_specs=HERE,
        out_shape=jax.ShapeDtypeStruct((HEADS_SEC, OWN_ROWS, HD), jnp.bfloat16),
        compiler_params=pltpu.CompilerParams(vmem_limit_bytes=56 * MIB),
        cost_estimate=pl.CostEstimate(flops=50000000, bytes_accessed=1200000, transcendentals=0),
        name="prepare",
    )(
        qpos,
        kpos,
        jnp.asarray(frequency_row()),
        jnp.asarray(row_order(), jnp.bfloat16),
        *(jnp.asarray(part, jnp.bfloat16) for part in patch_order()),
        queries,
        keys,
        values,
        mixing.T,
        cache.transpose(0, 1, 2, 4, 3).reshape(MIX, 40),
    )


def spread_kernel(own, queries, pairs, tiles):
    for part in range(HEADS_SEC):
        lines = own[part, KV_ROWS : KV_ROWS + Q_OWN, :]
        for copy in range(4):
            queries[copy, part] = lines
        pairs[part] = own[part, 0:KV_ROWS, :]
        tiles[part] = own[part, KV_ROWS + Q_OWN : OWN_ROWS, :]


def spread(own):
    return pl.pallas_call(
        spread_kernel,
        in_specs=[HERE],
        out_specs=[HERE] * 3,
        out_shape=[
            jax.ShapeDtypeStruct((4, HEADS_SEC, Q_OWN, HD), jnp.bfloat16),
            jax.ShapeDtypeStruct((HEADS_SEC, KV_ROWS, HD), jnp.bfloat16),
            jax.ShapeDtypeStruct((HEADS_SEC, STRIP, HD), jnp.bfloat16),
        ],
        compiler_params=pltpu.CompilerParams(vmem_limit_bytes=4 * MIB),
        cost_estimate=pl.CostEstimate(flops=0, bytes_accessed=800000, transcendentals=0),
        name="spread",
    )(own)


def add_heads_kernel(parts, out):
    total = parts[0].astype(jnp.float32)
    for part in range(1, 8):
        total = total + parts[part].astype(jnp.float32)
    total = total.astype(jnp.bfloat16)
    for copy in range(4):
        out[copy] = total


def add_heads(parts):
    return pl.pallas_call(
        add_heads_kernel,
        in_specs=[HERE],
        out_specs=HERE,
        out_shape=jax.ShapeDtypeStruct((4, 4, STRIP, HD), jnp.bfloat16),
        compiler_params=pltpu.CompilerParams(vmem_limit_bytes=4 * MIB),
        cost_estimate=pl.CostEstimate(flops=100000, bytes_accessed=300000, transcendentals=0),
        name="add_heads",
    )(parts)


def attend_kernel(*refs):
    q_ref, kv_refs, o_ref = refs[0], refs[1:6], refs[6]
    k_buf, v_buf, s_even, s_odd, levels = refs[7:]
    lane = lax.broadcasted_iota(jnp.int32, (V_ROWS, HD), 1)
    ones = jnp.where(lane == MIX, 1.0, 0.0)
    at = 0
    for kv_ref in kv_refs:
        for part in range(kv_ref.shape[0]):
            k_buf[at : at + K_OWN] = kv_ref[part, 0:K_OWN, :]
            both = kv_ref[part, K_OWN:KV_ROWS, :].astype(jnp.float32)
            v_buf[at : at + V_ROWS] = jnp.where(lane < MIX, both, ones).astype(jnp.bfloat16)
            other = pltpu.roll(both, MIX, 1)
            v_buf[at + V_ROWS : at + K_OWN] = jnp.where(lane < MIX, other, ones).astype(jnp.bfloat16)
            at += K_OWN

    scale = jnp.float32(math.log2(math.e) / math.sqrt(HD))
    diagonal = lax.broadcasted_iota(jnp.int32, (GRID_W, HD), 1) == lax.broadcasted_iota(jnp.int32, (GRID_W, HD), 0)
    low_lane = lax.broadcasted_iota(jnp.int32, (HALF_W, HD), 1) < MIX

    def score(block):
        return lax.dot_general(
            q_ref[block * SUB : (block + 1) * SUB, :],
            k_buf[...],
            (((1,), (1,)), ((), ())),
            preferred_element_type=jnp.float32,
        )

    def finish(piece, s_ref):
        scores = s_ref[...]
        top = jnp.max(scores, axis=1, keepdims=True)
        weights = jnp.exp2((scores - top) * scale).astype(jnp.bfloat16)
        sums = jnp.dot(weights, v_buf[...], preferred_element_type=jnp.float32)
        total = sums[:, MIX : MIX + 1]
        mean = sums / total
        level = top * scale + jnp.log2(total)
        for pair in range(4):
            lines = []
            for patch_row in (2 * pair, 2 * pair + 1):
                at = patch_row * GRID_W
                low = mean[at : at + HALF_W]
                high = pltpu.roll(mean[at + HALF_W : at + GRID_W], MIX, 1)
                lines.append(jnp.where(low_lane, low, high))
                line = jnp.sum(jnp.where(diagonal, level[at : at + GRID_W], 0.0), axis=0, keepdims=True)
                first = line.astype(jnp.bfloat16).astype(jnp.float32)
                line = line - first
                second = line.astype(jnp.bfloat16).astype(jnp.float32)
                third = line - second
                spot = patch_row % 2 * 4
                levels[pair, piece * 8 + spot : piece * 8 + spot + 4] = jnp.concatenate(
                    [first, second, third, jnp.zeros((1, HD), jnp.float32)], axis=0
                )
            o_ref[pair, piece * GRID_W : (piece + 1) * GRID_W] = jnp.concatenate(lines, axis=0).astype(jnp.bfloat16)

    s_even[...] = score(0)
    s_odd[...] = score(1)
    finish(0, s_even)
    s_even[...] = score(2)
    finish(1, s_odd)
    s_odd[...] = score(3)
    finish(2, s_even)
    finish(3, s_odd)
    o_ref[:, 4 * GRID_W : MSG] = levels[...].astype(jnp.bfloat16)


def attend(queries, pairs):
    return pl.pallas_call(
        attend_kernel,
        in_specs=[HERE] * 6,
        out_specs=HERE,
        out_shape=jax.ShapeDtypeStruct((4, MSG, HD), jnp.bfloat16),
        scratch_shapes=[
            pltpu.VMEM((KEYS_PART, HD), jnp.bfloat16),
            pltpu.VMEM((KEYS_PART, HD), jnp.bfloat16),
            pltpu.VMEM((SUB, KEYS_PART), jnp.float32),
            pltpu.VMEM((SUB, KEYS_PART), jnp.float32),
            pltpu.VMEM((4, 32, HD), jnp.float32),
        ],
        compiler_params=pltpu.CompilerParams(vmem_limit_bytes=42 * MIB),
        cost_estimate=pl.CostEstimate(flops=4 * FRAME * KEYS_PART * HD, bytes_accessed=2000000, transcendentals=0),
        name="attend",
    )(queries.reshape(FRAME, HD), *pairs)


def combine_kernel(r_ref, o_ref):
    shares = r_ref.shape[0]
    lane = lax.broadcasted_iota(jnp.int32, (HALF_W, HD), 1)
    row = lax.broadcasted_iota(jnp.int32, (HALF_W, HD), 0)
    zeros = jnp.zeros((16, HD), jnp.float32)
    low_lane = lax.broadcasted_iota(jnp.int32, (STRIP, HD), 1) < MIX
    lines = []
    asides = [r_ref[share, 4 * GRID_W : MSG].astype(jnp.float32) for share in range(shares)]
    for patch_row in range(ROWS_BLOCK):
        at, spot = patch_row % 2 * HALF_W, patch_row * 4
        blocks = [
            r_ref[share, patch_row // 2 * GRID_W : (patch_row // 2 + 1) * GRID_W].astype(jnp.float32)[at : at + HALF_W]
            for share in range(shares)
        ]
        levels = [a[spot : spot + 1] + a[spot + 1 : spot + 2] + a[spot + 2 : spot + 3] for a in asides]
        top = levels[0]
        for level in levels[1:]:
            top = jnp.maximum(top, level)
        powers = [jnp.exp2(level - top) for level in levels]
        total = powers[0]
        for power in powers[1:]:
            total = total + power
        result = jnp.zeros((HALF_W, HD), jnp.float32)
        for block, power in zip(blocks, powers):
            weight = power / total
            low = jnp.sum(jnp.where(lane == row, weight, 0.0), axis=1, keepdims=True)
            high = jnp.sum(jnp.where(lane == row + HALF_W, weight, 0.0), axis=1, keepdims=True)
            result = result + jnp.where(lane < MIX, low, high) * block
        line = jnp.concatenate([zeros[:1], result, pltpu.roll(result, MIX, 1), zeros], axis=0)
        line = line[: 2 * HALF_W + 16]
        lines.append(line if patch_row % 2 == 0 else pltpu.roll(line, MIX, 1))
    for group in range(4):
        for tile in range(4):
            at = tile * TILE_W
            piece = jnp.where(low_lane, lines[2 * group][at : at + STRIP], lines[2 * group + 1][at : at + STRIP])
            piece = piece.astype(jnp.bfloat16)
            for copy in range(2):
                o_ref[copy * 4 + tile, group] = piece


def combine(received):
    return pl.pallas_call(
        combine_kernel,
        in_specs=[HERE],
        out_specs=HERE,
        out_shape=jax.ShapeDtypeStruct((8, 4, STRIP, HD), jnp.bfloat16),
        compiler_params=pltpu.CompilerParams(vmem_limit_bytes=8 * MIB),
        cost_estimate=pl.CostEstimate(flops=1000000, bytes_accessed=900000, transcendentals=0),
        name="combine",
    )(received)


def convolve_kernel(half, own, near, kernel, bias, o_ref, weights, rows):
    tap = {(0, 0, 1): 0, (0, 1, 0): 1, (0, 1, 1): 2, (1, 0, 0): 0, (1, 0, 1): 1, (1, 1, 0): 2}
    nothing = jnp.zeros((16, C_OUT), jnp.bfloat16)
    at = 0
    for side in range(2):
        for shift in range(2):
            for frame in range(3):
                for line in range(4):
                    for b in range(2):
                        step_x = tap.get((side, shift, b))
                        if line == 0 or step_x is None:
                            weights[at : at + 16] = nothing
                        else:
                            source = ((frame * 3 + line - 1) * 3 + step_x) * 16
                            weights[at : at + 16] = kernel[source : source + 16]
                        at += 16
    lane = lax.broadcasted_iota(jnp.int32, (STRIP, HD), 1)
    low = lane < MIX
    top = half[0] == 0
    lines = ([], [])
    for frame in range(3):
        mine = own[frame].astype(jnp.float32)
        beside = near[frame].astype(jnp.float32)
        mine_turned = pltpu.roll(mine, MIX, 1)
        beside_turned = pltpu.roll(beside, MIX, 1)
        upper = jnp.where(top, jnp.where(low, beside_turned, mine_turned), mine)
        lower = jnp.where(top, mine_turned, beside)
        lines[0].append(upper)
        lines[1].append(jnp.where(lane < 96, pltpu.roll(upper, 96, 1), pltpu.roll(lower, 96, 1)))
    spare = jnp.zeros((8, HD), jnp.float32)
    lines = [[jnp.concatenate([part, spare], axis=0) for part in parts] for parts in lines]
    for side in range(2):
        taps = jnp.concatenate(
            [
                jnp.concatenate([part[side + s : side + s + STRIP] for s in range(2) for part in parts], axis=1)
                for parts in lines
            ],
            axis=0,
        ).astype(jnp.bfloat16)
        size = 6 * HD
        sums = jnp.dot(taps, weights[side * size : (side + 1) * size, :], preferred_element_type=jnp.float32)
        sums = sums + bias[...]
        for a in range(2):
            for part in range(C_OUT // HD):
                block = sums[a * STRIP : a * STRIP + TILE_W, part * HD : (part + 1) * HD]
                rows[part, pl.ds(a * 40 + side, TILE_W, 2), :] = block
    o_ref[...] = jnp.concatenate([rows[part] for part in range(C_OUT // HD)], axis=1).astype(jnp.bfloat16)


def convolve(half, own, near, kernel, bias):
    return pl.pallas_call(
        convolve_kernel,
        in_specs=[pl.BlockSpec(memory_space=pltpu.SMEM)] + [HERE] * 4,
        out_specs=HERE,
        out_shape=jax.ShapeDtypeStruct((80, C_OUT), jnp.bfloat16),
        scratch_shapes=[pltpu.VMEM((12 * HD, C_OUT), jnp.bfloat16), pltpu.VMEM((C_OUT // HD, 80, HD), jnp.float32)],
        compiler_params=pltpu.CompilerParams(vmem_limit_bytes=8 * MIB),
        cost_estimate=pl.CostEstimate(flops=100000000, bytes_accessed=500000, transcendentals=0),
        name="convolve",
    )(half, own, near, kernel, bias)


def from_ahead(value, axis, steps):
    return lax.ppermute(value, axis, [((spot + steps) % 4, spot) for spot in range(4)])


def next_pair(value, axes):
    pairs = [(i, i + 8) for i in range(120) if i % 8 < 4] + [(i, i - 8) for i in range(8, 128) if i % 8 >= 4]
    return lax.ppermute(value, axes, pairs)


def cache_strips(tiles, tile_col):
    wide = tiles.reshape(2, 4, STRIP, HD)[:, :, :TILE_W].reshape(2, GRID_W, HD)
    wide = jnp.pad(wide, ((0, 0), (1, 3), (0, 0)))
    wide = lax.dynamic_slice_in_dim(wide, tile_col * TILE_W, STRIP, 1)
    return wide.reshape(2, STRIP, 2, MIX).transpose(2, 1, 0, 3).reshape(2, STRIP, HD)


def on_device(queries, keys, values, query_positions, key_positions, mixing, kernel, bias, cache):
    sp_index = lax.axis_index(SP)
    section = lax.axis_index("sec")
    half = lax.axis_index("y") // 4
    tile_col = sp_index % 4
    own = prepare(query_positions, key_positions, queries, keys, values, mixing, cache)
    own = lax.all_to_all(own, "y", 0, 0)
    q_copies, kv_own, tiles = spread(own)
    query_all = lax.all_to_all(q_copies, "zh", 0, 0)
    kv_next = from_ahead(kv_own, "x", 1)
    pairs = [kv_own, kv_next, from_ahead(kv_own, "x", 3), from_ahead(kv_own[:4], "x", 2), from_ahead(kv_next[4:], "x", 1)]
    cached = cache_strips(tiles, tile_col)
    query_all, pairs, cached = lax.optimization_barrier((query_all, pairs, cached))
    parts = attend(query_all, pairs)
    shares = lax.all_to_all(parts, "zh", 0, 0)
    tiles = lax.all_to_all(combine(shares), "y", 0, 0)
    strip = lax.all_to_all(add_heads(tiles).reshape(16, STRIP, HD), ("sec", "x"), 0, 0)
    strip = jnp.sum(strip.reshape(4, 4, STRIP, HD).astype(jnp.float32), axis=0).astype(jnp.bfloat16)
    strip = jnp.concatenate([cached, strip], axis=0)
    frames = lax.dynamic_slice_in_dim(strip, section, 3, 0)
    output = convolve(half.reshape(1), frames, next_pair(frames, SP), kernel, bias[None])
    return output.reshape(1, 1, 2, 40, kernel.shape[1])


def solution(mesh):
    fine = Mesh(mesh.devices.reshape(4, 4, 4, 8), ("sec", *SP))
    placed = (
        P(SP, "sec"),
        P(SP, "sec"),
        P(SP, "sec"),
        P(None, SP),
        P(None, SP),
        P("sec", None),
        P(),
        P(),
        P(None, SP, None, None, None),
    )
    return jax.shard_map(
        on_device,
        mesh=fine,
        in_specs=placed,
        out_specs=P("sec", SP, None, None, None),
        check_vma=False,
    )
```

```python
import math

import jax
import jax.numpy as jnp
import numpy as np
from jax import lax
from jax.experimental import pallas as pl
from jax.experimental.pallas import tpu as pltpu
from jax.sharding import Mesh
from jax.sharding import PartitionSpec as P

HD = 128
STRIP = 24
HEADS_SEC = 8
Q_OWN = 80
K_OWN = 96
V_ROWS = K_OWN // 2
KV_ROWS = K_OWN + V_ROWS
OWN_ROWS = KV_ROWS + Q_OWN + STRIP
MIX = 64
GRID_W = 80
HALF_W = GRID_W // 2
FRAME = 2560
KEYS_PART = 3072
Q_BLOCK = 640
ROWS_BLOCK = Q_BLOCK // GRID_W
SUB = 640
MSG = 4 * GRID_W + 32
TILE_W = 20
C_OUT = 384
SP = ("x", "zh", "y")
MIB = 1024 * 1024
HERE = pl.BlockSpec(memory_space=pltpu.VMEM)


def frequency_row():
    sixth = HD // 6
    time_pairs = (HD - 4 * sixth) // 2
    time = 10000.0 ** (-np.arange(time_pairs) / time_pairs)
    space = 10000.0 ** (-np.arange(sixth) / sixth)
    pairs = np.concatenate([time, space, space])
    return np.repeat(pairs, 2).astype(np.float32)[None, :]


def row_order():
    order = np.zeros((2, 2 * MIX, MIX), np.float32)
    for ch in range(16):
        for ab in range(4):
            for side in range(2):
                order[side, side * MIX + ab * 16 + ch, ch * 4 + ab] = 1.0
    return order


def patch_order():
    pick = np.zeros((2, STRIP, 40), np.float32)
    place = np.zeros((2, MIX, HD), np.float32)
    for side in range(2):
        for patch in range(TILE_W):
            pick[side, patch, 2 * patch + side] = 1.0
        for line in range(4):
            for ch in range(16):
                place[side, line * 16 + ch, line * 32 + side * 16 + ch] = 1.0
    return pick, place


def cosine_sine(angle):
    turns = jnp.floor(angle * jnp.float32(2.0 / math.pi) + 0.5)
    rest = angle - turns * jnp.float32(1.5703125)
    rest = rest - turns * jnp.float32(4.837512969970703e-4)
    rest = rest - turns * jnp.float32(7.549789948768648e-8)
    square = rest * rest
    sine = rest + rest * square * (
        jnp.float32(-1.6666654611e-1) + square * (jnp.float32(8.3321608736e-3) - square * jnp.float32(1.9515295891e-4))
    )
    cosine = 1.0 - 0.5 * square + square * square * (
        jnp.float32(4.166664568298827e-2)
        + square * (jnp.float32(-1.388731625493765e-3) + square * jnp.float32(2.443315711809948e-5))
    )
    quarter = turns.astype(jnp.int32)
    odd = (quarter & 1) == 1
    first, second = jnp.where(odd, sine, cosine), jnp.where(odd, cosine, sine)
    first = jnp.where(((quarter + 1) & 2) == 2, -first, first)
    return first, jnp.where((quarter & 2) == 2, -second, second)


def turn_tables(positions, freq):
    count = positions.shape[1]
    spot = positions.astype(jnp.float32)
    same = lax.broadcasted_iota(jnp.int32, (count, count), 0) == lax.broadcasted_iota(jnp.int32, (count, count), 1)
    column = [jnp.sum(jnp.where(same, spot[i : i + 1], 0.0), axis=1, keepdims=True) for i in range(3)]
    lane = lax.broadcasted_iota(jnp.int32, (count, HD), 1)
    base = jnp.where(lane < 44, column[0], jnp.where(lane < 86, column[1], column[2]))
    angle = base * freq
    cosine, sine = cosine_sine(angle)
    even = lax.rem(lane, 2) == 0
    zero = jnp.zeros_like(sine)
    return cosine, jnp.where(even, -sine, zero), jnp.where(even, zero, sine)


def turn(vectors, tables):
    cosine, from_next, from_last = tables
    wide = vectors.astype(jnp.float32)
    out = wide * cosine + pltpu.roll(wide, HD - 1, 1) * from_next + pltpu.roll(wide, 1, 1) * from_last
    return out.astype(jnp.bfloat16)


def prepare_kernel(qpos, kpos, freq, order, pick, place, queries, keys, values, mixing, cache, out):
    q_tables = turn_tables(qpos[...], freq[...])
    k_tables = turn_tables(kpos[...], freq[...])
    tile = jnp.zeros((STRIP, HD), jnp.float32)
    for side in range(2):
        column = lax.dot_general(
            pick[side], cache[...], (((1,), (1,)), ((), ())), preferred_element_type=jnp.float32
        )
        tile = tile + jnp.dot(column.astype(jnp.bfloat16), place[side], preferred_element_type=jnp.float32)
    tile = tile.astype(jnp.bfloat16)
    mixed = [
        jnp.dot(order[side], mixing[...], preferred_element_type=jnp.float32).astype(jnp.bfloat16)
        for side in range(2)
    ]
    for head in range(HEADS_SEC):
        cols = slice(head * HD, (head + 1) * HD)
        out[head, 0:K_OWN, :] = turn(keys[:, cols], k_tables)
        value = values[:, cols]
        mix_low = lax.dot_general(
            value[:V_ROWS], mixed[0][:, cols], (((1,), (1,)), ((), ())), preferred_element_type=jnp.float32
        )
        mix_high = lax.dot_general(
            value[V_ROWS:], mixed[1][:, cols], (((1,), (1,)), ((), ())), preferred_element_type=jnp.float32
        )
        out[head, K_OWN:KV_ROWS, :] = (mix_low + mix_high).astype(jnp.bfloat16)
        out[head, KV_ROWS : KV_ROWS + Q_OWN, :] = turn(queries[:, cols], q_tables)
        out[head, KV_ROWS + Q_OWN : OWN_ROWS, :] = tile


def prepare(qpos, kpos, queries, keys, values, mixing, cache):
    return pl.pallas_call(
        prepare_kernel,
        in_specs=[HERE] * 11,
        out_specs=HERE,
        out_shape=jax.ShapeDtypeStruct((HEADS_SEC, OWN_ROWS, HD), jnp.bfloat16),
        compiler_params=pltpu.CompilerParams(vmem_limit_bytes=56 * MIB),
        cost_estimate=pl.CostEstimate(flops=50000000, bytes_accessed=1200000, transcendentals=0),
        name="prepare",
    )(
        qpos,
        kpos,
        jnp.asarray(frequency_row()),
        jnp.asarray(row_order(), jnp.bfloat16),
        *(jnp.asarray(part, jnp.bfloat16) for part in patch_order()),
        queries,
        keys,
        values,
        mixing.T,
        cache.transpose(0, 1, 2, 4, 3).reshape(MIX, 40),
    )


def spread_kernel(own, queries, pairs, tiles):
    for part in range(HEADS_SEC):
        lines = own[part, KV_ROWS : KV_ROWS + Q_OWN, :]
        for copy in range(4):
            queries[copy, part] = lines
        pairs[part] = own[part, 0:KV_ROWS, :]
        tiles[part] = own[part, KV_ROWS + Q_OWN : OWN_ROWS, :]


def spread(own):
    return pl.pallas_call(
        spread_kernel,
        in_specs=[HERE],
        out_specs=[HERE] * 3,
        out_shape=[
            jax.ShapeDtypeStruct((4, HEADS_SEC, Q_OWN, HD), jnp.bfloat16),
            jax.ShapeDtypeStruct((HEADS_SEC, KV_ROWS, HD), jnp.bfloat16),
            jax.ShapeDtypeStruct((HEADS_SEC, STRIP, HD), jnp.bfloat16),
        ],
        compiler_params=pltpu.CompilerParams(vmem_limit_bytes=4 * MIB),
        cost_estimate=pl.CostEstimate(flops=0, bytes_accessed=800000, transcendentals=0),
        name="spread",
    )(own)


def add_heads_kernel(parts, out):
    total = parts[0].astype(jnp.float32)
    for part in range(1, 8):
        total = total + parts[part].astype(jnp.float32)
    total = total.astype(jnp.bfloat16)
    for copy in range(4):
        out[copy] = total


def add_heads(parts):
    return pl.pallas_call(
        add_heads_kernel,
        in_specs=[HERE],
        out_specs=HERE,
        out_shape=jax.ShapeDtypeStruct((4, 4, STRIP, HD), jnp.bfloat16),
        compiler_params=pltpu.CompilerParams(vmem_limit_bytes=4 * MIB),
        cost_estimate=pl.CostEstimate(flops=100000, bytes_accessed=300000, transcendentals=0),
        name="add_heads",
    )(parts)


def attend_kernel(*refs):
    q_ref, kv_refs, o_ref = refs[0], refs[1:6], refs[6]
    k_buf, v_buf, s_even, s_odd, levels = refs[7:]
    lane = lax.broadcasted_iota(jnp.int32, (V_ROWS, HD), 1)
    ones = jnp.where(lane == MIX, 1.0, 0.0)
    at = 0
    for kv_ref in kv_refs:
        for part in range(kv_ref.shape[0]):
            k_buf[at : at + K_OWN] = kv_ref[part, 0:K_OWN, :]
            both = kv_ref[part, K_OWN:KV_ROWS, :].astype(jnp.float32)
            v_buf[at : at + V_ROWS] = jnp.where(lane < MIX, both, ones).astype(jnp.bfloat16)
            other = pltpu.roll(both, MIX, 1)
            v_buf[at + V_ROWS : at + K_OWN] = jnp.where(lane < MIX, other, ones).astype(jnp.bfloat16)
            at += K_OWN

    scale = jnp.float32(math.log2(math.e) / math.sqrt(HD))
    diagonal = lax.broadcasted_iota(jnp.int32, (GRID_W, HD), 1) == lax.broadcasted_iota(jnp.int32, (GRID_W, HD), 0)
    low_lane = lax.broadcasted_iota(jnp.int32, (HALF_W, HD), 1) < MIX

    def score(start, rows):
        return lax.dot_general(
            q_ref[start : start + rows, :],
            k_buf[...],
            (((1,), (1,)), ((), ())),
            preferred_element_type=jnp.float32,
        )

    def finish(start, rows, s_ref):
        scores = s_ref[0:rows]
        top = jnp.max(scores, axis=1, keepdims=True)
        weights = jnp.exp2((scores - top) * scale).astype(jnp.bfloat16)
        sums = jnp.dot(weights, v_buf[...], preferred_element_type=jnp.float32)
        total = sums[:, MIX : MIX + 1]
        mean = sums / total
        level = top * scale + jnp.log2(total)
        for block in range(rows // (2 * GRID_W)):
            piece, pair = divmod(start // (2 * GRID_W) + block, 4)
            lines = []
            for half in range(2):
                at = (2 * block + half) * GRID_W
                low = mean[at : at + HALF_W]
                high = pltpu.roll(mean[at + HALF_W : at + GRID_W], MIX, 1)
                lines.append(jnp.where(low_lane, low, high))
                line = jnp.sum(jnp.where(diagonal, level[at : at + GRID_W], 0.0), axis=0, keepdims=True)
                first = line.astype(jnp.bfloat16).astype(jnp.float32)
                line = line - first
                second = line.astype(jnp.bfloat16).astype(jnp.float32)
                third = line - second
                spot = piece * 8 + half * 4
                levels[pair, spot : spot + 4] = jnp.concatenate(
                    [first, second, third, jnp.zeros((1, HD), jnp.float32)], axis=0
                )
            o_ref[pair, piece * GRID_W : (piece + 1) * GRID_W] = jnp.concatenate(lines, axis=0).astype(jnp.bfloat16)

    blocks = [(0, 320), (320, 640), (960, 640), (1600, 640), (2240, 320)]
    buffers = [s_even, s_odd]
    s_even[0:320] = score(0, 320)
    for index, (start, rows) in enumerate(blocks):
        if index + 1 < len(blocks):
            after, count = blocks[index + 1]
            buffers[(index + 1) % 2][0:count] = score(after, count)
        finish(start, rows, buffers[index % 2])
    o_ref[:, 4 * GRID_W : MSG] = levels[...].astype(jnp.bfloat16)


def attend(queries, pairs):
    return pl.pallas_call(
        attend_kernel,
        in_specs=[HERE] * 6,
        out_specs=HERE,
        out_shape=jax.ShapeDtypeStruct((4, MSG, HD), jnp.bfloat16),
        scratch_shapes=[
            pltpu.VMEM((KEYS_PART, HD), jnp.bfloat16),
            pltpu.VMEM((KEYS_PART, HD), jnp.bfloat16),
            pltpu.VMEM((SUB, KEYS_PART), jnp.float32),
            pltpu.VMEM((SUB, KEYS_PART), jnp.float32),
            pltpu.VMEM((4, 32, HD), jnp.float32),
        ],
        compiler_params=pltpu.CompilerParams(vmem_limit_bytes=42 * MIB),
        cost_estimate=pl.CostEstimate(flops=4 * FRAME * KEYS_PART * HD, bytes_accessed=2000000, transcendentals=0),
        name="attend",
    )(queries.reshape(FRAME, HD), *pairs)


def combine_kernel(r_ref, o_ref):
    shares = r_ref.shape[0]
    lane = lax.broadcasted_iota(jnp.int32, (HALF_W, HD), 1)
    row = lax.broadcasted_iota(jnp.int32, (HALF_W, HD), 0)
    zeros = jnp.zeros((16, HD), jnp.float32)
    low_lane = lax.broadcasted_iota(jnp.int32, (STRIP, HD), 1) < MIX
    lines = []
    asides = [r_ref[share, 4 * GRID_W : MSG].astype(jnp.float32) for share in range(shares)]
    for patch_row in range(ROWS_BLOCK):
        at, spot = patch_row % 2 * HALF_W, patch_row * 4
        blocks = [
            r_ref[share, patch_row // 2 * GRID_W : (patch_row // 2 + 1) * GRID_W].astype(jnp.float32)[at : at + HALF_W]
            for share in range(shares)
        ]
        levels = [a[spot : spot + 1] + a[spot + 1 : spot + 2] + a[spot + 2 : spot + 3] for a in asides]
        top = levels[0]
        for level in levels[1:]:
            top = jnp.maximum(top, level)
        powers = [jnp.exp2(level - top) for level in levels]
        total = powers[0]
        for power in powers[1:]:
            total = total + power
        result = jnp.zeros((HALF_W, HD), jnp.float32)
        for block, power in zip(blocks, powers):
            weight = power / total
            low = jnp.sum(jnp.where(lane == row, weight, 0.0), axis=1, keepdims=True)
            high = jnp.sum(jnp.where(lane == row + HALF_W, weight, 0.0), axis=1, keepdims=True)
            result = result + jnp.where(lane < MIX, low, high) * block
        line = jnp.concatenate([zeros[:1], result, pltpu.roll(result, MIX, 1), zeros], axis=0)
        line = line[: 2 * HALF_W + 16]
        lines.append(line if patch_row % 2 == 0 else pltpu.roll(line, MIX, 1))
    for group in range(4):
        for tile in range(4):
            at = tile * TILE_W
            piece = jnp.where(low_lane, lines[2 * group][at : at + STRIP], lines[2 * group + 1][at : at + STRIP])
            piece = piece.astype(jnp.bfloat16)
            for copy in range(2):
                o_ref[copy * 4 + tile, group] = piece


def combine(received):
    return pl.pallas_call(
        combine_kernel,
        in_specs=[HERE],
        out_specs=HERE,
        out_shape=jax.ShapeDtypeStruct((8, 4, STRIP, HD), jnp.bfloat16),
        compiler_params=pltpu.CompilerParams(vmem_limit_bytes=8 * MIB),
        cost_estimate=pl.CostEstimate(flops=1000000, bytes_accessed=900000, transcendentals=0),
        name="combine",
    )(received)


def convolve_kernel(half, own, near, kernel, bias, o_ref, weights, rows):
    tap = {(0, 0, 1): 0, (0, 1, 0): 1, (0, 1, 1): 2, (1, 0, 0): 0, (1, 0, 1): 1, (1, 1, 0): 2}
    nothing = jnp.zeros((16, C_OUT), jnp.bfloat16)
    at = 0
    for side in range(2):
        for shift in range(2):
            for frame in range(3):
                for line in range(4):
                    for b in range(2):
                        step_x = tap.get((side, shift, b))
                        if line == 0 or step_x is None:
                            weights[at : at + 16] = nothing
                        else:
                            source = ((frame * 3 + line - 1) * 3 + step_x) * 16
                            weights[at : at + 16] = kernel[source : source + 16]
                        at += 16
    lane = lax.broadcasted_iota(jnp.int32, (STRIP, HD), 1)
    low = lane < MIX
    top = half[0] == 0
    lines = ([], [])
    for frame in range(3):
        mine = own[frame].astype(jnp.float32)
        beside = near[frame].astype(jnp.float32)
        mine_turned = pltpu.roll(mine, MIX, 1)
        beside_turned = pltpu.roll(beside, MIX, 1)
        upper = jnp.where(top, jnp.where(low, beside_turned, mine_turned), mine)
        lower = jnp.where(top, mine_turned, beside)
        lines[0].append(upper)
        lines[1].append(jnp.where(lane < 96, pltpu.roll(upper, 96, 1), pltpu.roll(lower, 96, 1)))
    spare = jnp.zeros((8, HD), jnp.float32)
    lines = [[jnp.concatenate([part, spare], axis=0) for part in parts] for parts in lines]
    for side in range(2):
        taps = jnp.concatenate(
            [
                jnp.concatenate([part[side + s : side + s + STRIP] for s in range(2) for part in parts], axis=1)
                for parts in lines
            ],
            axis=0,
        ).astype(jnp.bfloat16)
        size = 6 * HD
        sums = jnp.dot(taps, weights[side * size : (side + 1) * size, :], preferred_element_type=jnp.float32)
        sums = sums + bias[...]
        for a in range(2):
            for part in range(C_OUT // HD):
                block = sums[a * STRIP : a * STRIP + TILE_W, part * HD : (part + 1) * HD]
                rows[part, pl.ds(a * 40 + side, TILE_W, 2), :] = block
    o_ref[...] = jnp.concatenate([rows[part] for part in range(C_OUT // HD)], axis=1).astype(jnp.bfloat16)


def convolve(half, own, near, kernel, bias):
    return pl.pallas_call(
        convolve_kernel,
        in_specs=[pl.BlockSpec(memory_space=pltpu.SMEM)] + [HERE] * 4,
        out_specs=HERE,
        out_shape=jax.ShapeDtypeStruct((80, C_OUT), jnp.bfloat16),
        scratch_shapes=[pltpu.VMEM((12 * HD, C_OUT), jnp.bfloat16), pltpu.VMEM((C_OUT // HD, 80, HD), jnp.float32)],
        compiler_params=pltpu.CompilerParams(vmem_limit_bytes=8 * MIB),
        cost_estimate=pl.CostEstimate(flops=100000000, bytes_accessed=500000, transcendentals=0),
        name="convolve",
    )(half, own, near, kernel, bias)


def from_ahead(value, axis, steps):
    return lax.ppermute(value, axis, [((spot + steps) % 4, spot) for spot in range(4)])


def next_pair(value, axes):
    pairs = [(i, i + 8) for i in range(120) if i % 8 < 4] + [(i, i - 8) for i in range(8, 128) if i % 8 >= 4]
    return lax.ppermute(value, axes, pairs)


def cache_strips(tiles, tile_col):
    wide = tiles.reshape(2, 4, STRIP, HD)[:, :, :TILE_W].reshape(2, GRID_W, HD)
    wide = jnp.pad(wide, ((0, 0), (1, 3), (0, 0)))
    wide = lax.dynamic_slice_in_dim(wide, tile_col * TILE_W, STRIP, 1)
    return wide.reshape(2, STRIP, 2, MIX).transpose(2, 1, 0, 3).reshape(2, STRIP, HD)


def on_device(queries, keys, values, query_positions, key_positions, mixing, kernel, bias, cache):
    sp_index = lax.axis_index(SP)
    section = lax.axis_index("sec")
    half = lax.axis_index("y") // 4
    tile_col = sp_index % 4
    own = prepare(query_positions, key_positions, queries, keys, values, mixing, cache)
    own = lax.all_to_all(own, "y", 0, 0)
    q_copies, kv_own, tiles = spread(own)
    query_all = lax.all_to_all(q_copies, "zh", 0, 0)
    kv_next = from_ahead(kv_own, "x", 1)
    pairs = [kv_own, kv_next, from_ahead(kv_own, "x", 3), from_ahead(kv_own[:4], "x", 2), from_ahead(kv_next[4:], "x", 1)]
    cached = cache_strips(tiles, tile_col)
    query_all, pairs, cached = lax.optimization_barrier((query_all, pairs, cached))
    parts = attend(query_all, pairs)
    shares = lax.all_to_all(parts, "zh", 0, 0)
    tiles = lax.all_to_all(combine(shares), "y", 0, 0)
    strip = lax.all_to_all(add_heads(tiles).reshape(16, STRIP, HD), ("sec", "x"), 0, 0)
    strip = jnp.sum(strip.reshape(4, 4, STRIP, HD).astype(jnp.float32), axis=0).astype(jnp.bfloat16)
    strip = jnp.concatenate([cached, strip], axis=0)
    frames = lax.dynamic_slice_in_dim(strip, section, 3, 0)
    output = convolve(half.reshape(1), frames, next_pair(frames, SP), kernel, bias[None])
    return output.reshape(1, 1, 2, 40, kernel.shape[1])


def solution(mesh):
    fine = Mesh(mesh.devices.reshape(4, 4, 4, 8), ("sec", *SP))
    placed = (
        P(SP, "sec"),
        P(SP, "sec"),
        P(SP, "sec"),
        P(None, SP),
        P(None, SP),
        P("sec", None),
        P(),
        P(),
        P(None, SP, None, None, None),
    )
    return jax.shard_map(
        on_device,
        mesh=fine,
        in_specs=placed,
        out_specs=P("sec", SP, None, None, None),
        check_vma=False,
    )
```

```python
import math

import jax
import jax.numpy as jnp
import numpy as np
from jax import lax
from jax.experimental import pallas as pl
from jax.experimental.pallas import tpu as pltpu
from jax.sharding import Mesh
from jax.sharding import PartitionSpec as P

HD = 128
STRIP = 24
HEADS_SEC = 8
Q_OWN = 80
K_OWN = 96
V_ROWS = K_OWN // 2
KV_ROWS = K_OWN + V_ROWS
OWN_ROWS = KV_ROWS + Q_OWN + STRIP
MIX = 64
GRID_W = 80
HALF_W = GRID_W // 2
FRAME = 2560
KEYS_PART = 3072
Q_BLOCK = 640
ROWS_BLOCK = Q_BLOCK // GRID_W
SUB = 640
MSG = 4 * GRID_W + 32
TILE_W = 20
C_OUT = 384
SP = ("x", "zh", "y")
MIB = 1024 * 1024
HERE = pl.BlockSpec(memory_space=pltpu.VMEM)


def frequency_row():
    sixth = HD // 6
    time_pairs = (HD - 4 * sixth) // 2
    time = 10000.0 ** (-np.arange(time_pairs) / time_pairs)
    space = 10000.0 ** (-np.arange(sixth) / sixth)
    pairs = np.concatenate([time, space, space])
    return np.repeat(pairs, 2).astype(np.float32)[None, :]


def row_order():
    order = np.zeros((2, 2 * MIX, MIX), np.float32)
    for ch in range(16):
        for ab in range(4):
            for side in range(2):
                order[side, side * MIX + ab * 16 + ch, ch * 4 + ab] = 1.0
    return order


def patch_order():
    pick = np.zeros((2, STRIP, 40), np.float32)
    place = np.zeros((2, MIX, HD), np.float32)
    for side in range(2):
        for patch in range(TILE_W):
            pick[side, patch, 2 * patch + side] = 1.0
        for line in range(4):
            for ch in range(16):
                place[side, line * 16 + ch, line * 32 + side * 16 + ch] = 1.0
    return pick, place


def cosine_sine(angle):
    turns = jnp.floor(angle * jnp.float32(2.0 / math.pi) + 0.5)
    rest = angle - turns * jnp.float32(1.5703125)
    rest = rest - turns * jnp.float32(4.837512969970703e-4)
    rest = rest - turns * jnp.float32(7.549789948768648e-8)
    square = rest * rest
    sine = rest + rest * square * (
        jnp.float32(-1.6666654611e-1) + square * (jnp.float32(8.3321608736e-3) - square * jnp.float32(1.9515295891e-4))
    )
    cosine = 1.0 - 0.5 * square + square * square * (
        jnp.float32(4.166664568298827e-2)
        + square * (jnp.float32(-1.388731625493765e-3) + square * jnp.float32(2.443315711809948e-5))
    )
    quarter = turns.astype(jnp.int32)
    odd = (quarter & 1) == 1
    first, second = jnp.where(odd, sine, cosine), jnp.where(odd, cosine, sine)
    first = jnp.where(((quarter + 1) & 2) == 2, -first, first)
    return first, jnp.where((quarter & 2) == 2, -second, second)


def turn_tables(positions, freq):
    count = positions.shape[1]
    spot = positions.astype(jnp.float32)
    same = lax.broadcasted_iota(jnp.int32, (count, count), 0) == lax.broadcasted_iota(jnp.int32, (count, count), 1)
    column = [jnp.sum(jnp.where(same, spot[i : i + 1], 0.0), axis=1, keepdims=True) for i in range(3)]
    lane = lax.broadcasted_iota(jnp.int32, (count, HD), 1)
    base = jnp.where(lane < 44, column[0], jnp.where(lane < 86, column[1], column[2]))
    angle = base * freq
    cosine, sine = cosine_sine(angle)
    even = lax.rem(lane, 2) == 0
    zero = jnp.zeros_like(sine)
    return cosine, jnp.where(even, -sine, zero), jnp.where(even, zero, sine)


def turn(vectors, tables):
    cosine, from_next, from_last = tables
    wide = vectors.astype(jnp.float32)
    out = wide * cosine + pltpu.roll(wide, HD - 1, 1) * from_next + pltpu.roll(wide, 1, 1) * from_last
    return out.astype(jnp.bfloat16)


def prepare_kernel(qpos, kpos, freq, order, pick, place, queries, keys, values, mixing, cache, out):
    q_tables = turn_tables(qpos[...], freq[...])
    k_tables = turn_tables(kpos[...], freq[...])
    tile = jnp.zeros((STRIP, HD), jnp.float32)
    for side in range(2):
        column = lax.dot_general(
            pick[side], cache[...], (((1,), (1,)), ((), ())), preferred_element_type=jnp.float32
        )
        tile = tile + jnp.dot(column.astype(jnp.bfloat16), place[side], preferred_element_type=jnp.float32)
    tile = tile.astype(jnp.bfloat16)
    mixed = [
        jnp.dot(order[side], mixing[...], preferred_element_type=jnp.float32).astype(jnp.bfloat16)
        for side in range(2)
    ]
    for head in range(HEADS_SEC):
        cols = slice(head * HD, (head + 1) * HD)
        out[head, 0:K_OWN, :] = turn(keys[:, cols], k_tables)
        value = values[:, cols]
        mix_low = lax.dot_general(
            value[:V_ROWS], mixed[0][:, cols], (((1,), (1,)), ((), ())), preferred_element_type=jnp.float32
        )
        mix_high = lax.dot_general(
            value[V_ROWS:], mixed[1][:, cols], (((1,), (1,)), ((), ())), preferred_element_type=jnp.float32
        )
        out[head, K_OWN:KV_ROWS, :] = (mix_low + mix_high).astype(jnp.bfloat16)
        out[head, KV_ROWS : KV_ROWS + Q_OWN, :] = turn(queries[:, cols], q_tables)
        out[head, KV_ROWS + Q_OWN : OWN_ROWS, :] = tile


def prepare(qpos, kpos, queries, keys, values, mixing, cache):
    return pl.pallas_call(
        prepare_kernel,
        in_specs=[HERE] * 11,
        out_specs=HERE,
        out_shape=jax.ShapeDtypeStruct((HEADS_SEC, OWN_ROWS, HD), jnp.bfloat16),
        compiler_params=pltpu.CompilerParams(vmem_limit_bytes=56 * MIB),
        cost_estimate=pl.CostEstimate(flops=50000000, bytes_accessed=1200000, transcendentals=0),
        name="prepare",
    )(
        qpos,
        kpos,
        jnp.asarray(frequency_row()),
        jnp.asarray(row_order(), jnp.bfloat16),
        *(jnp.asarray(part, jnp.bfloat16) for part in patch_order()),
        queries,
        keys,
        values,
        mixing.T,
        cache.transpose(0, 1, 2, 4, 3).reshape(MIX, 40),
    )


def spread_kernel(own, queries, pairs, tiles):
    for part in range(HEADS_SEC):
        lines = own[part, KV_ROWS : KV_ROWS + Q_OWN, :]
        for copy in range(4):
            queries[copy, part] = lines
        pairs[part] = own[part, 0:KV_ROWS, :]
        tiles[part] = own[part, KV_ROWS + Q_OWN : OWN_ROWS, :]


def spread(own):
    return pl.pallas_call(
        spread_kernel,
        in_specs=[HERE],
        out_specs=[HERE] * 3,
        out_shape=[
            jax.ShapeDtypeStruct((4, HEADS_SEC, Q_OWN, HD), jnp.bfloat16),
            jax.ShapeDtypeStruct((HEADS_SEC, KV_ROWS, HD), jnp.bfloat16),
            jax.ShapeDtypeStruct((HEADS_SEC, STRIP, HD), jnp.bfloat16),
        ],
        compiler_params=pltpu.CompilerParams(vmem_limit_bytes=4 * MIB),
        cost_estimate=pl.CostEstimate(flops=0, bytes_accessed=800000, transcendentals=0),
        name="spread",
    )(own)


def add_heads_kernel(parts, out):
    total = parts[0].astype(jnp.float32)
    for part in range(1, 8):
        total = total + parts[part].astype(jnp.float32)
    total = total.astype(jnp.bfloat16)
    for copy in range(4):
        out[copy] = total


def add_heads(parts):
    return pl.pallas_call(
        add_heads_kernel,
        in_specs=[HERE],
        out_specs=HERE,
        out_shape=jax.ShapeDtypeStruct((4, 4, STRIP, HD), jnp.bfloat16),
        compiler_params=pltpu.CompilerParams(vmem_limit_bytes=4 * MIB),
        cost_estimate=pl.CostEstimate(flops=100000, bytes_accessed=300000, transcendentals=0),
        name="add_heads",
    )(parts)


def attend_kernel(*refs):
    q_ref, kv_refs, o_ref = refs[0], refs[1:6], refs[6]
    k_buf, v_buf, s_even, s_odd, levels = refs[7:]
    lane = lax.broadcasted_iota(jnp.int32, (V_ROWS, HD), 1)
    ones = jnp.where(lane == MIX, 1.0, 0.0)
    at = 0
    for kv_ref in kv_refs:
        for part in range(kv_ref.shape[0]):
            k_buf[at : at + K_OWN] = kv_ref[part, 0:K_OWN, :]
            both = kv_ref[part, K_OWN:KV_ROWS, :].astype(jnp.float32)
            v_buf[at : at + V_ROWS] = jnp.where(lane < MIX, both, ones).astype(jnp.bfloat16)
            other = pltpu.roll(both, MIX, 1)
            v_buf[at + V_ROWS : at + K_OWN] = jnp.where(lane < MIX, other, ones).astype(jnp.bfloat16)
            at += K_OWN

    scale = jnp.float32(math.log2(math.e) / math.sqrt(HD))
    diagonal = lax.broadcasted_iota(jnp.int32, (GRID_W, HD), 1) == lax.broadcasted_iota(jnp.int32, (GRID_W, HD), 0)
    low_lane = lax.broadcasted_iota(jnp.int32, (HALF_W, HD), 1) < MIX

    def score(start, rows):
        return lax.dot_general(
            q_ref[start : start + rows, :],
            k_buf[...],
            (((1,), (1,)), ((), ())),
            preferred_element_type=jnp.float32,
        )

    def finish(start, rows, s_ref):
        scores = s_ref[0:rows]
        top = jnp.max(scores, axis=1, keepdims=True)
        weights = jnp.exp2((scores - top) * scale).astype(jnp.bfloat16)
        sums = jnp.dot(weights, v_buf[...], preferred_element_type=jnp.float32)
        total = sums[:, MIX : MIX + 1]
        mean = sums / total
        level = top * scale + jnp.log2(total)
        for block in range(rows // (2 * GRID_W)):
            piece, pair = divmod(start // (2 * GRID_W) + block, 4)
            lines = []
            for half in range(2):
                at = (2 * block + half) * GRID_W
                low = mean[at : at + HALF_W]
                high = pltpu.roll(mean[at + HALF_W : at + GRID_W], MIX, 1)
                lines.append(jnp.where(low_lane, low, high))
                line = jnp.sum(jnp.where(diagonal, level[at : at + GRID_W], 0.0), axis=0, keepdims=True)
                first = line.astype(jnp.bfloat16).astype(jnp.float32)
                line = line - first
                second = line.astype(jnp.bfloat16).astype(jnp.float32)
                third = line - second
                spot = piece * 8 + half * 4
                levels[pair, spot : spot + 4] = jnp.concatenate(
                    [first, second, third, jnp.zeros((1, HD), jnp.float32)], axis=0
                )
            o_ref[pair, piece * GRID_W : (piece + 1) * GRID_W] = jnp.concatenate(lines, axis=0).astype(jnp.bfloat16)

    blocks = [(0, 320), (320, 640), (960, 640), (1600, 640), (2240, 320)]
    buffers = [s_even, s_odd]
    s_even[0:320] = score(0, 320)
    for index, (start, rows) in enumerate(blocks):
        if index + 1 < len(blocks):
            after, count = blocks[index + 1]
            buffers[(index + 1) % 2][0:count] = score(after, count)
        finish(start, rows, buffers[index % 2])
    o_ref[:, 4 * GRID_W : MSG] = levels[...].astype(jnp.bfloat16)


def attend(queries, pairs):
    return pl.pallas_call(
        attend_kernel,
        in_specs=[HERE] * 6,
        out_specs=HERE,
        out_shape=jax.ShapeDtypeStruct((4, MSG, HD), jnp.bfloat16),
        scratch_shapes=[
            pltpu.VMEM((KEYS_PART, HD), jnp.bfloat16),
            pltpu.VMEM((KEYS_PART, HD), jnp.bfloat16),
            pltpu.VMEM((SUB, KEYS_PART), jnp.float32),
            pltpu.VMEM((SUB, KEYS_PART), jnp.float32),
            pltpu.VMEM((4, 32, HD), jnp.float32),
        ],
        compiler_params=pltpu.CompilerParams(vmem_limit_bytes=42 * MIB),
        cost_estimate=pl.CostEstimate(flops=4 * FRAME * KEYS_PART * HD, bytes_accessed=2000000, transcendentals=0),
        name="attend",
    )(queries.reshape(FRAME, HD), *pairs)


def combine_kernel(r_ref, o_ref):
    shares = r_ref.shape[0]
    lane = lax.broadcasted_iota(jnp.int32, (HALF_W, HD), 1)
    row = lax.broadcasted_iota(jnp.int32, (HALF_W, HD), 0)
    zeros = jnp.zeros((16, HD), jnp.float32)
    low_lane = lax.broadcasted_iota(jnp.int32, (STRIP, HD), 1) < MIX
    lines = []
    asides = [r_ref[share, 4 * GRID_W : MSG].astype(jnp.float32) for share in range(shares)]
    for patch_row in range(ROWS_BLOCK):
        at, spot = patch_row % 2 * HALF_W, patch_row * 4
        blocks = [
            r_ref[share, patch_row // 2 * GRID_W : (patch_row // 2 + 1) * GRID_W].astype(jnp.float32)[at : at + HALF_W]
            for share in range(shares)
        ]
        levels = [a[spot : spot + 1] + a[spot + 1 : spot + 2] + a[spot + 2 : spot + 3] for a in asides]
        top = levels[0]
        for level in levels[1:]:
            top = jnp.maximum(top, level)
        powers = [jnp.exp2(level - top) for level in levels]
        total = powers[0]
        for power in powers[1:]:
            total = total + power
        result = jnp.zeros((HALF_W, HD), jnp.float32)
        for block, power in zip(blocks, powers):
            weight = power / total
            low = jnp.sum(jnp.where(lane == row, weight, 0.0), axis=1, keepdims=True)
            high = jnp.sum(jnp.where(lane == row + HALF_W, weight, 0.0), axis=1, keepdims=True)
            result = result + jnp.where(lane < MIX, low, high) * block
        line = jnp.concatenate([zeros[:1], result, pltpu.roll(result, MIX, 1), zeros], axis=0)
        line = line[: 2 * HALF_W + 16]
        lines.append(line if patch_row % 2 == 0 else pltpu.roll(line, MIX, 1))
    for group in range(4):
        for tile in range(4):
            at = tile * TILE_W
            piece = jnp.where(low_lane, lines[2 * group][at : at + STRIP], lines[2 * group + 1][at : at + STRIP])
            piece = piece.astype(jnp.bfloat16)
            for copy in range(2):
                o_ref[copy * 4 + tile, group] = piece


def combine(received):
    return pl.pallas_call(
        combine_kernel,
        in_specs=[HERE],
        out_specs=HERE,
        out_shape=jax.ShapeDtypeStruct((8, 4, STRIP, HD), jnp.bfloat16),
        compiler_params=pltpu.CompilerParams(vmem_limit_bytes=8 * MIB),
        cost_estimate=pl.CostEstimate(flops=1000000, bytes_accessed=900000, transcendentals=0),
        name="combine",
    )(received)


def convolve_kernel(half, own, near, kernel, bias, o_ref, weights, rows):
    tap = {(0, 0, 1): 0, (0, 1, 0): 1, (0, 1, 1): 2, (1, 0, 0): 0, (1, 0, 1): 1, (1, 1, 0): 2}
    nothing = jnp.zeros((16, C_OUT), jnp.bfloat16)
    at = 0
    for side in range(2):
        for shift in range(2):
            for frame in range(3):
                for line in range(4):
                    for b in range(2):
                        step_x = tap.get((side, shift, b))
                        if line == 0 or step_x is None:
                            weights[at : at + 16] = nothing
                        else:
                            source = ((frame * 3 + line - 1) * 3 + step_x) * 16
                            weights[at : at + 16] = kernel[source : source + 16]
                        at += 16
    lane = lax.broadcasted_iota(jnp.int32, (STRIP, HD), 1)
    low = lane < MIX
    top = half[0] == 0
    lines = ([], [])
    for frame in range(3):
        mine = own[frame].astype(jnp.float32)
        beside = near[frame].astype(jnp.float32)
        mine_turned = pltpu.roll(mine, MIX, 1)
        beside_turned = pltpu.roll(beside, MIX, 1)
        upper = jnp.where(top, jnp.where(low, beside_turned, mine_turned), mine)
        lower = jnp.where(top, mine_turned, beside)
        lines[0].append(upper)
        lines[1].append(jnp.where(lane < 96, pltpu.roll(upper, 96, 1), pltpu.roll(lower, 96, 1)))
    spare = jnp.zeros((8, HD), jnp.float32)
    lines = [[jnp.concatenate([part, spare], axis=0) for part in parts] for parts in lines]
    for side in range(2):
        taps = jnp.concatenate(
            [
                jnp.concatenate([part[side + s : side + s + STRIP] for s in range(2) for part in parts], axis=1)
                for parts in lines
            ],
            axis=0,
        ).astype(jnp.bfloat16)
        size = 6 * HD
        sums = jnp.dot(taps, weights[side * size : (side + 1) * size, :], preferred_element_type=jnp.float32)
        sums = sums + bias[...]
        for a in range(2):
            for part in range(C_OUT // HD):
                block = sums[a * STRIP : a * STRIP + TILE_W, part * HD : (part + 1) * HD]
                rows[part, pl.ds(a * 40 + side, TILE_W, 2), :] = block
    o_ref[...] = jnp.concatenate([rows[part] for part in range(C_OUT // HD)], axis=1).astype(jnp.bfloat16)


def convolve(half, own, near, kernel, bias):
    return pl.pallas_call(
        convolve_kernel,
        in_specs=[pl.BlockSpec(memory_space=pltpu.SMEM)] + [HERE] * 4,
        out_specs=HERE,
        out_shape=jax.ShapeDtypeStruct((80, C_OUT), jnp.bfloat16),
        scratch_shapes=[pltpu.VMEM((12 * HD, C_OUT), jnp.bfloat16), pltpu.VMEM((C_OUT // HD, 80, HD), jnp.float32)],
        compiler_params=pltpu.CompilerParams(vmem_limit_bytes=8 * MIB),
        cost_estimate=pl.CostEstimate(flops=100000000, bytes_accessed=500000, transcendentals=0),
        name="convolve",
    )(half, own, near, kernel, bias)


def from_ahead(value, axis, steps):
    return lax.ppermute(value, axis, [((spot + steps) % 4, spot) for spot in range(4)])


def next_pair(value, axes):
    pairs = [(i, i + 8) for i in range(120) if i % 8 < 4] + [(i, i - 8) for i in range(8, 128) if i % 8 >= 4]
    return lax.ppermute(value, axes, pairs)


def cache_strips(tiles, tile_col):
    wide = tiles.reshape(2, 4, STRIP, HD)[:, :, :TILE_W].reshape(2, GRID_W, HD)
    wide = jnp.pad(wide, ((0, 0), (1, 3), (0, 0)))
    wide = lax.dynamic_slice_in_dim(wide, tile_col * TILE_W, STRIP, 1)
    return wide.reshape(2, STRIP, 2, MIX).transpose(2, 1, 0, 3).reshape(2, STRIP, HD)


def on_device(queries, keys, values, query_positions, key_positions, mixing, kernel, bias, cache):
    sp_index = lax.axis_index(SP)
    section = lax.axis_index("sec")
    half = lax.axis_index("y") // 4
    tile_col = sp_index % 4
    own = prepare(query_positions, key_positions, queries, keys, values, mixing, cache)
    own = lax.all_to_all(own, "y", 0, 0)
    q_copies, kv_own, tiles = spread(own)
    query_all = lax.all_to_all(q_copies, "zh", 0, 0)
    kv_last = from_ahead(kv_own, "x", 3)
    pairs = [kv_own, from_ahead(kv_own, "x", 1), kv_last, from_ahead(kv_own[:4], "x", 2), from_ahead(kv_last[4:], "x", 3)]
    cached = cache_strips(tiles, tile_col)
    query_all, pairs, cached = lax.optimization_barrier((query_all, pairs, cached))
    parts = attend(query_all, pairs)
    shares = lax.all_to_all(parts, "zh", 0, 0)
    tiles = lax.all_to_all(combine(shares), "y", 0, 0)
    strip = lax.all_to_all(add_heads(tiles).reshape(16, STRIP, HD), ("sec", "x"), 0, 0)
    strip = jnp.sum(strip.reshape(4, 4, STRIP, HD).astype(jnp.float32), axis=0).astype(jnp.bfloat16)
    strip = jnp.concatenate([cached, strip], axis=0)
    frames = lax.dynamic_slice_in_dim(strip, section, 3, 0)
    output = convolve(half.reshape(1), frames, next_pair(frames, SP), kernel, bias[None])
    return output.reshape(1, 1, 2, 40, kernel.shape[1])


def solution(mesh):
    fine = Mesh(mesh.devices.reshape(4, 4, 4, 8), ("sec", *SP))
    placed = (
        P(SP, "sec"),
        P(SP, "sec"),
        P(SP, "sec"),
        P(None, SP),
        P(None, SP),
        P("sec", None),
        P(),
        P(),
        P(None, SP, None, None, None),
    )
    return jax.shard_map(
        on_device,
        mesh=fine,
        in_specs=placed,
        out_specs=P("sec", SP, None, None, None),
        check_vma=False,
    )
```

```python
import math

import jax
import jax.numpy as jnp
import numpy as np
from jax import lax
from jax.experimental import pallas as pl
from jax.experimental.pallas import tpu as pltpu
from jax.sharding import Mesh
from jax.sharding import PartitionSpec as P

HD = 128
STRIP = 24
HEADS_SEC = 8
Q_OWN = 80
K_OWN = 96
V_ROWS = K_OWN // 2
KV_ROWS = K_OWN + V_ROWS
TILE_ROWS = 32
OWN_ROWS = KV_ROWS + Q_OWN + TILE_ROWS
MIX = 64
GRID_W = 80
HALF_W = GRID_W // 2
FRAME = 2560
KEYS_PART = 3072
Q_BLOCK = 640
ROWS_BLOCK = Q_BLOCK // GRID_W
SUB = 640
MSG = 4 * GRID_W + 32
TILE_W = 20
C_OUT = 384
SP = ("x", "zh", "y")
MIB = 1024 * 1024
HERE = pl.BlockSpec(memory_space=pltpu.VMEM)


def frequency_row():
    sixth = HD // 6
    time_pairs = (HD - 4 * sixth) // 2
    time = 10000.0 ** (-np.arange(time_pairs) / time_pairs)
    space = 10000.0 ** (-np.arange(sixth) / sixth)
    pairs = np.concatenate([time, space, space])
    return np.repeat(pairs, 2).astype(np.float32)[None, :]


def row_order():
    order = np.zeros((2, 2 * MIX, MIX), np.float32)
    for ch in range(16):
        for ab in range(4):
            for side in range(2):
                order[side, side * MIX + ab * 16 + ch, ch * 4 + ab] = 1.0
    return order


def patch_order():
    pick = np.zeros((2, TILE_ROWS, 40), np.float32)
    place = np.zeros((2, MIX, HD), np.float32)
    for side in range(2):
        for patch in range(TILE_W):
            pick[side, patch, 2 * patch + side] = 1.0
        for line in range(4):
            for ch in range(16):
                place[side, line * 16 + ch, line * 32 + side * 16 + ch] = 1.0
    return pick, place


def cosine_sine(angle):
    turns = jnp.floor(angle * jnp.float32(2.0 / math.pi) + 0.5)
    rest = angle - turns * jnp.float32(1.5703125)
    rest = rest - turns * jnp.float32(4.837512969970703e-4)
    rest = rest - turns * jnp.float32(7.549789948768648e-8)
    square = rest * rest
    sine = rest + rest * square * (
        jnp.float32(-1.6666654611e-1) + square * (jnp.float32(8.3321608736e-3) - square * jnp.float32(1.9515295891e-4))
    )
    cosine = 1.0 - 0.5 * square + square * square * (
        jnp.float32(4.166664568298827e-2)
        + square * (jnp.float32(-1.388731625493765e-3) + square * jnp.float32(2.443315711809948e-5))
    )
    quarter = turns.astype(jnp.int32)
    odd = (quarter & 1) == 1
    first, second = jnp.where(odd, sine, cosine), jnp.where(odd, cosine, sine)
    first = jnp.where(((quarter + 1) & 2) == 2, -first, first)
    return first, jnp.where((quarter & 2) == 2, -second, second)


def turn_tables(positions, freq):
    count = positions.shape[1]
    spot = positions.astype(jnp.float32)
    same = lax.broadcasted_iota(jnp.int32, (count, count), 0) == lax.broadcasted_iota(jnp.int32, (count, count), 1)
    column = [jnp.sum(jnp.where(same, spot[i : i + 1], 0.0), axis=1, keepdims=True) for i in range(3)]
    lane = lax.broadcasted_iota(jnp.int32, (count, HD), 1)
    base = jnp.where(lane < 44, column[0], jnp.where(lane < 86, column[1], column[2]))
    angle = base * freq
    cosine, sine = cosine_sine(angle)
    even = lax.rem(lane, 2) == 0
    zero = jnp.zeros_like(sine)
    return cosine, jnp.where(even, -sine, zero), jnp.where(even, zero, sine)


def turn(vectors, tables):
    cosine, from_next, from_last = tables
    wide = vectors.astype(jnp.float32)
    out = wide * cosine + pltpu.roll(wide, HD - 1, 1) * from_next + pltpu.roll(wide, 1, 1) * from_last
    return out.astype(jnp.bfloat16)


def prepare_kernel(qpos, kpos, freq, order, pick, place, queries, keys, values, mixing, cache, out):
    q_tables = turn_tables(qpos[...], freq[...])
    k_tables = turn_tables(kpos[...], freq[...])
    tile = jnp.zeros((TILE_ROWS, HD), jnp.float32)
    for side in range(2):
        column = lax.dot_general(
            pick[side], cache[...], (((1,), (1,)), ((), ())), preferred_element_type=jnp.float32
        )
        tile = tile + jnp.dot(column.astype(jnp.bfloat16), place[side], preferred_element_type=jnp.float32)
    tile = tile.astype(jnp.bfloat16)
    mixed = [
        jnp.dot(order[side], mixing[...], preferred_element_type=jnp.float32).astype(jnp.bfloat16)
        for side in range(2)
    ]
    for head in range(HEADS_SEC):
        cols = slice(head * HD, (head + 1) * HD)
        out[head, 0:K_OWN, :] = turn(keys[:, cols], k_tables)
        value = values[:, cols]
        mix_low = lax.dot_general(
            value[:V_ROWS], mixed[0][:, cols], (((1,), (1,)), ((), ())), preferred_element_type=jnp.float32
        )
        mix_high = lax.dot_general(
            value[V_ROWS:], mixed[1][:, cols], (((1,), (1,)), ((), ())), preferred_element_type=jnp.float32
        )
        out[head, K_OWN:KV_ROWS, :] = (mix_low + mix_high).astype(jnp.bfloat16)
        out[head, KV_ROWS : KV_ROWS + Q_OWN, :] = turn(queries[:, cols], q_tables)
        out[head, KV_ROWS + Q_OWN : OWN_ROWS, :] = tile


def prepare(qpos, kpos, queries, keys, values, mixing, cache):
    return pl.pallas_call(
        prepare_kernel,
        in_specs=[HERE] * 11,
        out_specs=HERE,
        out_shape=jax.ShapeDtypeStruct((HEADS_SEC, OWN_ROWS, HD), jnp.bfloat16),
        compiler_params=pltpu.CompilerParams(vmem_limit_bytes=56 * MIB),
        cost_estimate=pl.CostEstimate(flops=50000000, bytes_accessed=1200000, transcendentals=0),
        name="prepare",
    )(
        qpos,
        kpos,
        jnp.asarray(frequency_row()),
        jnp.asarray(row_order(), jnp.bfloat16),
        *(jnp.asarray(part, jnp.bfloat16) for part in patch_order()),
        queries,
        keys,
        values,
        mixing.T,
        cache.transpose(0, 1, 2, 4, 3).reshape(MIX, 40),
    )


def spread_kernel(own, queries, pairs, tiles):
    for part in range(HEADS_SEC):
        lines = own[part, KV_ROWS : KV_ROWS + Q_OWN, :]
        for copy in range(4):
            queries[copy, part] = lines
        pairs[part] = own[part, 0:KV_ROWS, :]
        tiles[part] = own[part, KV_ROWS + Q_OWN : OWN_ROWS, :]


def spread(own):
    return pl.pallas_call(
        spread_kernel,
        in_specs=[HERE],
        out_specs=[HERE] * 3,
        out_shape=[
            jax.ShapeDtypeStruct((4, HEADS_SEC, Q_OWN, HD), jnp.bfloat16),
            jax.ShapeDtypeStruct((HEADS_SEC, KV_ROWS, HD), jnp.bfloat16),
            jax.ShapeDtypeStruct((HEADS_SEC, TILE_ROWS, HD), jnp.bfloat16),
        ],
        compiler_params=pltpu.CompilerParams(vmem_limit_bytes=4 * MIB),
        cost_estimate=pl.CostEstimate(flops=0, bytes_accessed=800000, transcendentals=0),
        name="spread",
    )(own)


def add_heads_kernel(parts, out):
    terms = [parts[part].astype(jnp.float32) for part in range(8)]
    while len(terms) > 1:
        terms = [terms[i] + terms[i + 1] for i in range(0, len(terms), 2)]
    total = terms[0].astype(jnp.bfloat16)
    for copy in range(4):
        out[copy] = total


def add_heads(parts):
    return pl.pallas_call(
        add_heads_kernel,
        in_specs=[HERE],
        out_specs=HERE,
        out_shape=jax.ShapeDtypeStruct((4, 4, STRIP, HD), jnp.bfloat16),
        compiler_params=pltpu.CompilerParams(vmem_limit_bytes=4 * MIB),
        cost_estimate=pl.CostEstimate(flops=100000, bytes_accessed=300000, transcendentals=0),
        name="add_heads",
    )(parts)


def attend_kernel(*refs):
    q_ref, kv_refs, o_ref = refs[0], refs[1:6], refs[6]
    k_buf, v_buf, s_even, s_odd, levels = refs[7:]
    lane = lax.broadcasted_iota(jnp.int32, (V_ROWS, HD), 1)
    ones = jnp.where(lane == MIX, 1.0, 0.0)
    at = 0
    for kv_ref in kv_refs:
        for part in range(kv_ref.shape[0]):
            k_buf[at : at + K_OWN] = kv_ref[part, 0:K_OWN, :]
            both = kv_ref[part, K_OWN:KV_ROWS, :].astype(jnp.float32)
            v_buf[at : at + V_ROWS] = jnp.where(lane < MIX, both, ones).astype(jnp.bfloat16)
            other = pltpu.roll(both, MIX, 1)
            v_buf[at + V_ROWS : at + K_OWN] = jnp.where(lane < MIX, other, ones).astype(jnp.bfloat16)
            at += K_OWN

    scale = jnp.float32(math.log2(math.e) / math.sqrt(HD))
    diagonal = lax.broadcasted_iota(jnp.int32, (GRID_W, HD), 1) == lax.broadcasted_iota(jnp.int32, (GRID_W, HD), 0)
    low_lane = lax.broadcasted_iota(jnp.int32, (HALF_W, HD), 1) < MIX

    def score(start, rows):
        return lax.dot_general(
            q_ref[start : start + rows, :],
            k_buf[...],
            (((1,), (1,)), ((), ())),
            preferred_element_type=jnp.float32,
        )

    def finish(start, rows, s_ref):
        scores = s_ref[0:rows]
        top = jnp.max(scores, axis=1, keepdims=True)
        weights = jnp.exp2((scores - top) * scale).astype(jnp.bfloat16)
        sums = jnp.dot(weights, v_buf[...], preferred_element_type=jnp.float32)
        total = sums[:, MIX : MIX + 1]
        mean = sums / total
        level = top * scale + jnp.log2(total)
        for block in range(rows // (2 * GRID_W)):
            piece, pair = divmod(start // (2 * GRID_W) + block, 4)
            lines = []
            for half in range(2):
                at = (2 * block + half) * GRID_W
                low = mean[at : at + HALF_W]
                high = pltpu.roll(mean[at + HALF_W : at + GRID_W], MIX, 1)
                lines.append(jnp.where(low_lane, low, high))
                line = jnp.sum(jnp.where(diagonal, level[at : at + GRID_W], 0.0), axis=0, keepdims=True)
                first = line.astype(jnp.bfloat16).astype(jnp.float32)
                line = line - first
                second = line.astype(jnp.bfloat16).astype(jnp.float32)
                third = line - second
                spot = piece * 8 + half * 4
                levels[pair, spot : spot + 4] = jnp.concatenate(
                    [first, second, third, jnp.zeros((1, HD), jnp.float32)], axis=0
                )
            o_ref[pair, piece * GRID_W : (piece + 1) * GRID_W] = jnp.concatenate(lines, axis=0).astype(jnp.bfloat16)

    blocks = [(0, 320), (320, 640), (960, 640), (1600, 640), (2240, 320)]
    buffers = [s_even, s_odd]
    s_even[0:320] = score(0, 320)
    for index, (start, rows) in enumerate(blocks):
        if index + 1 < len(blocks):
            after, count = blocks[index + 1]
            buffers[(index + 1) % 2][0:count] = score(after, count)
        finish(start, rows, buffers[index % 2])
    o_ref[:, 4 * GRID_W : MSG] = levels[...].astype(jnp.bfloat16)


def attend(queries, pairs):
    return pl.pallas_call(
        attend_kernel,
        in_specs=[HERE] * 6,
        out_specs=HERE,
        out_shape=jax.ShapeDtypeStruct((4, MSG, HD), jnp.bfloat16),
        scratch_shapes=[
            pltpu.VMEM((KEYS_PART, HD), jnp.bfloat16),
            pltpu.VMEM((KEYS_PART, HD), jnp.bfloat16),
            pltpu.VMEM((SUB, KEYS_PART), jnp.float32),
            pltpu.VMEM((SUB, KEYS_PART), jnp.float32),
            pltpu.VMEM((4, 32, HD), jnp.float32),
        ],
        compiler_params=pltpu.CompilerParams(vmem_limit_bytes=42 * MIB),
        cost_estimate=pl.CostEstimate(flops=4 * FRAME * KEYS_PART * HD, bytes_accessed=2000000, transcendentals=0),
        name="attend",
    )(queries.reshape(FRAME, HD), *pairs)


def combine_kernel(r_ref, o_ref):
    shares = r_ref.shape[0]
    lane = lax.broadcasted_iota(jnp.int32, (HALF_W, HD), 1)
    row = lax.broadcasted_iota(jnp.int32, (HALF_W, HD), 0)
    zeros = jnp.zeros((16, HD), jnp.float32)
    low_lane = lax.broadcasted_iota(jnp.int32, (STRIP, HD), 1) < MIX
    lines = []
    asides = [r_ref[share, 4 * GRID_W : MSG].astype(jnp.float32) for share in range(shares)]
    for patch_row in range(ROWS_BLOCK):
        at, spot = patch_row % 2 * HALF_W, patch_row * 4
        blocks = [
            r_ref[share, patch_row // 2 * GRID_W : (patch_row // 2 + 1) * GRID_W].astype(jnp.float32)[at : at + HALF_W]
            for share in range(shares)
        ]
        levels = [a[spot : spot + 1] + a[spot + 1 : spot + 2] + a[spot + 2 : spot + 3] for a in asides]
        top = levels[0]
        for level in levels[1:]:
            top = jnp.maximum(top, level)
        powers = [jnp.exp2(level - top) for level in levels]
        total = powers[0]
        for power in powers[1:]:
            total = total + power
        result = jnp.zeros((HALF_W, HD), jnp.float32)
        for block, power in zip(blocks, powers):
            weight = power / total
            low = jnp.sum(jnp.where(lane == row, weight, 0.0), axis=1, keepdims=True)
            high = jnp.sum(jnp.where(lane == row + HALF_W, weight, 0.0), axis=1, keepdims=True)
            result = result + jnp.where(lane < MIX, low, high) * block
        line = jnp.concatenate([zeros[:1], result, pltpu.roll(result, MIX, 1), zeros], axis=0)
        line = line[: 2 * HALF_W + 16]
        lines.append(line if patch_row % 2 == 0 else pltpu.roll(line, MIX, 1))
    for group in range(4):
        for tile in range(4):
            at = tile * TILE_W
            piece = jnp.where(low_lane, lines[2 * group][at : at + STRIP], lines[2 * group + 1][at : at + STRIP])
            piece = piece.astype(jnp.bfloat16)
            for copy in range(2):
                o_ref[copy * 4 + tile, group] = piece


def combine(received):
    return pl.pallas_call(
        combine_kernel,
        in_specs=[HERE],
        out_specs=HERE,
        out_shape=jax.ShapeDtypeStruct((8, 4, STRIP, HD), jnp.bfloat16),
        compiler_params=pltpu.CompilerParams(vmem_limit_bytes=8 * MIB),
        cost_estimate=pl.CostEstimate(flops=1000000, bytes_accessed=900000, transcendentals=0),
        name="combine",
    )(received)


def convolve_kernel(half, own, near, kernel, bias, o_ref, weights, rows):
    tap = {(0, 0, 1): 0, (0, 1, 0): 1, (0, 1, 1): 2, (1, 0, 0): 0, (1, 0, 1): 1, (1, 1, 0): 2}
    nothing = jnp.zeros((16, C_OUT), jnp.bfloat16)
    at = 0
    for side in range(2):
        for shift in range(2):
            for frame in range(3):
                for line in range(4):
                    for b in range(2):
                        step_x = tap.get((side, shift, b))
                        if line == 0 or step_x is None:
                            weights[at : at + 16] = nothing
                        else:
                            source = ((frame * 3 + line - 1) * 3 + step_x) * 16
                            weights[at : at + 16] = kernel[source : source + 16]
                        at += 16
    lane = lax.broadcasted_iota(jnp.int32, (STRIP, HD), 1)
    low = lane < MIX
    top = half[0] == 0
    lines = ([], [])
    for frame in range(3):
        mine = own[frame].astype(jnp.float32)
        beside = near[frame].astype(jnp.float32)
        mine_turned = pltpu.roll(mine, MIX, 1)
        beside_turned = pltpu.roll(beside, MIX, 1)
        upper = jnp.where(top, jnp.where(low, beside_turned, mine_turned), mine)
        lower = jnp.where(top, mine_turned, beside)
        lines[0].append(upper)
        lines[1].append(jnp.where(lane < 96, pltpu.roll(upper, 96, 1), pltpu.roll(lower, 96, 1)))
    spare = jnp.zeros((8, HD), jnp.float32)
    lines = [[jnp.concatenate([part, spare], axis=0) for part in parts] for parts in lines]
    for side in range(2):
        taps = jnp.concatenate(
            [
                jnp.concatenate([part[side + s : side + s + STRIP] for s in range(2) for part in parts], axis=1)
                for parts in lines
            ],
            axis=0,
        ).astype(jnp.bfloat16)
        size = 6 * HD
        sums = jnp.dot(taps, weights[side * size : (side + 1) * size, :], preferred_element_type=jnp.float32)
        sums = sums + bias[...]
        for a in range(2):
            for part in range(C_OUT // HD):
                block = sums[a * STRIP : a * STRIP + TILE_W, part * HD : (part + 1) * HD]
                rows[part, pl.ds(a * 40 + side, TILE_W, 2), :] = block
    o_ref[...] = jnp.concatenate([rows[part] for part in range(C_OUT // HD)], axis=1).astype(jnp.bfloat16)


def convolve(half, own, near, kernel, bias):
    return pl.pallas_call(
        convolve_kernel,
        in_specs=[pl.BlockSpec(memory_space=pltpu.SMEM)] + [HERE] * 4,
        out_specs=HERE,
        out_shape=jax.ShapeDtypeStruct((80, C_OUT), jnp.bfloat16),
        scratch_shapes=[pltpu.VMEM((12 * HD, C_OUT), jnp.bfloat16), pltpu.VMEM((C_OUT // HD, 80, HD), jnp.float32)],
        compiler_params=pltpu.CompilerParams(vmem_limit_bytes=8 * MIB),
        cost_estimate=pl.CostEstimate(flops=100000000, bytes_accessed=500000, transcendentals=0),
        name="convolve",
    )(half, own, near, kernel, bias)


def from_ahead(value, axis, steps):
    return lax.ppermute(value, axis, [((spot + steps) % 4, spot) for spot in range(4)])


def next_pair(value, axes):
    pairs = [(i, i + 8) for i in range(120) if i % 8 < 4] + [(i, i - 8) for i in range(8, 128) if i % 8 >= 4]
    return lax.ppermute(value, axes, pairs)


def cache_strips(tiles, tile_col):
    wide = tiles.reshape(2, 4, TILE_ROWS, HD)[:, :, :TILE_W].reshape(2, GRID_W, HD)
    wide = jnp.pad(wide, ((0, 0), (1, 3), (0, 0)))
    wide = lax.dynamic_slice_in_dim(wide, tile_col * TILE_W, STRIP, 1)
    return wide.reshape(2, STRIP, 2, MIX).transpose(2, 1, 0, 3).reshape(2, STRIP, HD)


def on_device(queries, keys, values, query_positions, key_positions, mixing, kernel, bias, cache):
    sp_index = lax.axis_index(SP)
    section = lax.axis_index("sec")
    half = lax.axis_index("y") // 4
    tile_col = sp_index % 4
    own = prepare(query_positions, key_positions, queries, keys, values, mixing, cache)
    own = lax.all_to_all(own, "y", 0, 0)
    q_copies, kv_own, tiles = spread(own)
    query_all = lax.all_to_all(q_copies, "zh", 0, 0)
    kv_last = from_ahead(kv_own, "x", 3)
    pairs = [kv_own, from_ahead(kv_own, "x", 1), kv_last, from_ahead(kv_own[:4], "x", 2), from_ahead(kv_last[4:], "x", 3)]
    cached = cache_strips(tiles, tile_col)
    query_all, pairs, cached = lax.optimization_barrier((query_all, pairs, cached))
    parts = attend(query_all, pairs)
    shares = lax.all_to_all(parts, "zh", 0, 0)
    tiles = lax.all_to_all(combine(shares), "y", 0, 0)
    strip = lax.all_to_all(add_heads(tiles).reshape(16, STRIP, HD), ("sec", "x"), 0, 0)
    strip = jnp.sum(strip.reshape(4, 4, STRIP, HD).astype(jnp.float32), axis=0).astype(jnp.bfloat16)
    strip = jnp.concatenate([cached, strip], axis=0)
    frames = lax.dynamic_slice_in_dim(strip, section, 3, 0)
    output = convolve(half.reshape(1), frames, next_pair(frames, SP), kernel, bias[None])
    return output.reshape(1, 1, 2, 40, kernel.shape[1])


def solution(mesh):
    fine = Mesh(mesh.devices.reshape(4, 4, 4, 8), ("sec", *SP))
    placed = (
        P(SP, "sec"),
        P(SP, "sec"),
        P(SP, "sec"),
        P(None, SP),
        P(None, SP),
        P("sec", None),
        P(),
        P(),
        P(None, SP, None, None, None),
    )
    return jax.shard_map(
        on_device,
        mesh=fine,
        in_specs=placed,
        out_specs=P("sec", SP, None, None, None),
        check_vma=False,
    )
```

```python
import math

import jax
import jax.numpy as jnp
import numpy as np
from jax import lax
from jax.experimental import pallas as pl
from jax.experimental.pallas import tpu as pltpu
from jax.sharding import Mesh
from jax.sharding import PartitionSpec as P

HD = 128
STRIP = 24
HEADS_SEC = 8
Q_OWN = 80
K_OWN = 96
V_ROWS = K_OWN // 2
KV_ROWS = K_OWN + V_ROWS
TILE_ROWS = 32
OWN_ROWS = KV_ROWS + Q_OWN + TILE_ROWS
MIX = 64
GRID_W = 80
HALF_W = GRID_W // 2
FRAME = 2560
KEYS_PART = 3072
Q_BLOCK = 640
ROWS_BLOCK = Q_BLOCK // GRID_W
SUB = 640
MSG = 4 * GRID_W + 32
TILE_W = 20
C_OUT = 384
SP = ("x", "zh", "y")
MIB = 1024 * 1024
HERE = pl.BlockSpec(memory_space=pltpu.VMEM)


def frequency_row():
    sixth = HD // 6
    time_pairs = (HD - 4 * sixth) // 2
    time = 10000.0 ** (-np.arange(time_pairs) / time_pairs)
    space = 10000.0 ** (-np.arange(sixth) / sixth)
    pairs = np.concatenate([time, space, space])
    return np.repeat(pairs, 2).astype(np.float32)[None, :]


def row_order():
    order = np.zeros((2, 2 * MIX, MIX), np.float32)
    for ch in range(16):
        for ab in range(4):
            for side in range(2):
                order[side, side * MIX + ab * 16 + ch, ch * 4 + ab] = 1.0
    return order


def patch_order():
    pick = np.zeros((2, TILE_ROWS, 40), np.float32)
    place = np.zeros((2, MIX, HD), np.float32)
    for side in range(2):
        for patch in range(TILE_W):
            pick[side, patch, 2 * patch + side] = 1.0
        for line in range(4):
            for ch in range(16):
                place[side, line * 16 + ch, line * 32 + side * 16 + ch] = 1.0
    return pick, place


def cosine_sine(angle):
    turns = jnp.floor(angle * jnp.float32(2.0 / math.pi) + 0.5)
    rest = angle - turns * jnp.float32(1.5703125)
    rest = rest - turns * jnp.float32(4.837512969970703e-4)
    rest = rest - turns * jnp.float32(7.549789948768648e-8)
    square = rest * rest
    sine = rest + rest * square * (
        jnp.float32(-1.6666654611e-1) + square * (jnp.float32(8.3321608736e-3) - square * jnp.float32(1.9515295891e-4))
    )
    cosine = 1.0 - 0.5 * square + square * square * (
        jnp.float32(4.166664568298827e-2)
        + square * (jnp.float32(-1.388731625493765e-3) + square * jnp.float32(2.443315711809948e-5))
    )
    quarter = turns.astype(jnp.int32)
    odd = (quarter & 1) == 1
    first, second = jnp.where(odd, sine, cosine), jnp.where(odd, cosine, sine)
    first = jnp.where(((quarter + 1) & 2) == 2, -first, first)
    return first, jnp.where((quarter & 2) == 2, -second, second)


def turn_tables(positions, freq):
    count = positions.shape[1]
    spot = positions.astype(jnp.float32)
    same = lax.broadcasted_iota(jnp.int32, (count, count), 0) == lax.broadcasted_iota(jnp.int32, (count, count), 1)
    column = [jnp.sum(jnp.where(same, spot[i : i + 1], 0.0), axis=1, keepdims=True) for i in range(3)]
    lane = lax.broadcasted_iota(jnp.int32, (count, HD), 1)
    base = jnp.where(lane < 44, column[0], jnp.where(lane < 86, column[1], column[2]))
    angle = base * freq
    cosine, sine = cosine_sine(angle)
    even = lax.rem(lane, 2) == 0
    zero = jnp.zeros_like(sine)
    return cosine, jnp.where(even, -sine, zero), jnp.where(even, zero, sine)


def turn(vectors, tables):
    cosine, from_next, from_last = tables
    wide = vectors.astype(jnp.float32)
    out = wide * cosine + pltpu.roll(wide, HD - 1, 1) * from_next + pltpu.roll(wide, 1, 1) * from_last
    return out.astype(jnp.bfloat16)


def prepare_kernel(qpos, kpos, freq, order, pick, place, queries, keys, values, mixing, cache, out):
    q_tables = turn_tables(qpos[...], freq[...])
    k_tables = turn_tables(kpos[...], freq[...])
    tile = jnp.zeros((TILE_ROWS, HD), jnp.float32)
    for side in range(2):
        column = lax.dot_general(
            pick[side], cache[...], (((1,), (1,)), ((), ())), preferred_element_type=jnp.float32
        )
        tile = tile + jnp.dot(column.astype(jnp.bfloat16), place[side], preferred_element_type=jnp.float32)
    tile = tile.astype(jnp.bfloat16)
    mixed = [
        jnp.dot(order[side], mixing[...], preferred_element_type=jnp.float32).astype(jnp.bfloat16)
        for side in range(2)
    ]
    for head in range(HEADS_SEC):
        cols = slice(head * HD, (head + 1) * HD)
        out[head, 0:K_OWN, :] = turn(keys[:, cols], k_tables)
        value = values[:, cols]
        mix_low = lax.dot_general(
            value[:V_ROWS], mixed[0][:, cols], (((1,), (1,)), ((), ())), preferred_element_type=jnp.float32
        )
        mix_high = lax.dot_general(
            value[V_ROWS:], mixed[1][:, cols], (((1,), (1,)), ((), ())), preferred_element_type=jnp.float32
        )
        out[head, K_OWN:KV_ROWS, :] = (mix_low + mix_high).astype(jnp.bfloat16)
        out[head, KV_ROWS : KV_ROWS + Q_OWN, :] = turn(queries[:, cols], q_tables)
        out[head, KV_ROWS + Q_OWN : OWN_ROWS, :] = tile


def prepare(qpos, kpos, queries, keys, values, mixing, cache):
    return pl.pallas_call(
        prepare_kernel,
        in_specs=[HERE] * 11,
        out_specs=HERE,
        out_shape=jax.ShapeDtypeStruct((HEADS_SEC, OWN_ROWS, HD), jnp.bfloat16),
        compiler_params=pltpu.CompilerParams(vmem_limit_bytes=56 * MIB),
        cost_estimate=pl.CostEstimate(flops=50000000, bytes_accessed=1200000, transcendentals=0),
        name="prepare",
    )(
        qpos,
        kpos,
        jnp.asarray(frequency_row()),
        jnp.asarray(row_order(), jnp.bfloat16),
        *(jnp.asarray(part, jnp.bfloat16) for part in patch_order()),
        queries,
        keys,
        values,
        mixing.T,
        cache.transpose(0, 1, 2, 4, 3).reshape(MIX, 40),
    )


def spread_kernel(own, queries, pairs, tiles):
    for part in range(HEADS_SEC):
        lines = own[part, KV_ROWS : KV_ROWS + Q_OWN, :]
        for copy in range(4):
            queries[copy, part] = lines
        pairs[part] = own[part, 0:KV_ROWS, :]
        tiles[part] = own[part, KV_ROWS + Q_OWN : OWN_ROWS, :]


def spread(own):
    return pl.pallas_call(
        spread_kernel,
        in_specs=[HERE],
        out_specs=[HERE] * 3,
        out_shape=[
            jax.ShapeDtypeStruct((4, HEADS_SEC, Q_OWN, HD), jnp.bfloat16),
            jax.ShapeDtypeStruct((HEADS_SEC, KV_ROWS, HD), jnp.bfloat16),
            jax.ShapeDtypeStruct((HEADS_SEC, TILE_ROWS, HD), jnp.bfloat16),
        ],
        compiler_params=pltpu.CompilerParams(vmem_limit_bytes=4 * MIB),
        cost_estimate=pl.CostEstimate(flops=0, bytes_accessed=800000, transcendentals=0),
        name="spread",
    )(own)


def add_heads_kernel(parts, out):
    terms = [parts[part].astype(jnp.float32) for part in range(8)]
    while len(terms) > 1:
        terms = [terms[i] + terms[i + 1] for i in range(0, len(terms), 2)]
    total = terms[0].astype(jnp.bfloat16)
    for copy in range(4):
        out[copy] = total


def add_heads(parts):
    return pl.pallas_call(
        add_heads_kernel,
        in_specs=[HERE],
        out_specs=HERE,
        out_shape=jax.ShapeDtypeStruct((4, 4, STRIP, HD), jnp.bfloat16),
        compiler_params=pltpu.CompilerParams(vmem_limit_bytes=4 * MIB),
        cost_estimate=pl.CostEstimate(flops=100000, bytes_accessed=300000, transcendentals=0),
        name="add_heads",
    )(parts)


def attend_kernel(*refs):
    q_ref, kv_refs, o_ref = refs[0], refs[1:6], refs[6]
    k_buf, v_buf, s_even, s_odd, levels = refs[7:]
    lane = lax.broadcasted_iota(jnp.int32, (V_ROWS, HD), 1)
    ones = jnp.where(lane == MIX, 1.0, 0.0)
    at = 0
    for kv_ref in kv_refs:
        for part in range(kv_ref.shape[0]):
            k_buf[at : at + K_OWN] = kv_ref[part, 0:K_OWN, :]
            both = kv_ref[part, K_OWN:KV_ROWS, :].astype(jnp.float32)
            v_buf[at : at + V_ROWS] = jnp.where(lane < MIX, both, ones).astype(jnp.bfloat16)
            other = pltpu.roll(both, MIX, 1)
            v_buf[at + V_ROWS : at + K_OWN] = jnp.where(lane < MIX, other, ones).astype(jnp.bfloat16)
            at += K_OWN

    scale = jnp.float32(math.log2(math.e) / math.sqrt(HD))
    diagonal = lax.broadcasted_iota(jnp.int32, (GRID_W, HD), 1) == lax.broadcasted_iota(jnp.int32, (GRID_W, HD), 0)
    low_lane = lax.broadcasted_iota(jnp.int32, (HALF_W, HD), 1) < MIX

    def score(start, rows):
        return lax.dot_general(
            q_ref[start : start + rows, :],
            k_buf[...],
            (((1,), (1,)), ((), ())),
            preferred_element_type=jnp.float32,
        )

    def finish(start, rows, s_ref):
        scores = s_ref[0:rows]
        top = jnp.max(scores, axis=1, keepdims=True)
        weights = jnp.exp2((scores - top) * scale).astype(jnp.bfloat16)
        sums = jnp.dot(weights, v_buf[...], preferred_element_type=jnp.float32)
        total = sums[:, MIX : MIX + 1]
        mean = sums / total
        level = top * scale + jnp.log2(total)
        for block in range(rows // (2 * GRID_W)):
            piece, pair = divmod(start // (2 * GRID_W) + block, 4)
            lines = []
            for half in range(2):
                at = (2 * block + half) * GRID_W
                low = mean[at : at + HALF_W]
                high = pltpu.roll(mean[at + HALF_W : at + GRID_W], MIX, 1)
                lines.append(jnp.where(low_lane, low, high))
                line = jnp.sum(jnp.where(diagonal, level[at : at + GRID_W], 0.0), axis=0, keepdims=True)
                first = line.astype(jnp.bfloat16).astype(jnp.float32)
                line = line - first
                second = line.astype(jnp.bfloat16).astype(jnp.float32)
                third = line - second
                spot = piece * 8 + half * 4
                levels[pair, spot : spot + 4] = jnp.concatenate(
                    [first, second, third, jnp.zeros((1, HD), jnp.float32)], axis=0
                )
            o_ref[pair, piece * GRID_W : (piece + 1) * GRID_W] = jnp.concatenate(lines, axis=0).astype(jnp.bfloat16)

    blocks = [(0, 320), (320, 640), (960, 640), (1600, 640), (2240, 160), (2400, 160)]
    buffers = [s_even, s_odd]
    s_even[0:320] = score(0, 320)
    for index, (start, rows) in enumerate(blocks):
        if index + 1 < len(blocks):
            after, count = blocks[index + 1]
            buffers[(index + 1) % 2][0:count] = score(after, count)
        finish(start, rows, buffers[index % 2])
    o_ref[:, 4 * GRID_W : MSG] = levels[...].astype(jnp.bfloat16)


def attend(queries, pairs):
    return pl.pallas_call(
        attend_kernel,
        in_specs=[HERE] * 6,
        out_specs=HERE,
        out_shape=jax.ShapeDtypeStruct((4, MSG, HD), jnp.bfloat16),
        scratch_shapes=[
            pltpu.VMEM((KEYS_PART, HD), jnp.bfloat16),
            pltpu.VMEM((KEYS_PART, HD), jnp.bfloat16),
            pltpu.VMEM((SUB, KEYS_PART), jnp.float32),
            pltpu.VMEM((SUB, KEYS_PART), jnp.float32),
            pltpu.VMEM((4, 32, HD), jnp.float32),
        ],
        compiler_params=pltpu.CompilerParams(vmem_limit_bytes=42 * MIB),
        cost_estimate=pl.CostEstimate(flops=4 * FRAME * KEYS_PART * HD, bytes_accessed=2000000, transcendentals=0),
        name="attend",
    )(queries.reshape(FRAME, HD), *pairs)


def combine_kernel(r_ref, o_ref):
    shares = r_ref.shape[0]
    lane = lax.broadcasted_iota(jnp.int32, (HALF_W, HD), 1)
    row = lax.broadcasted_iota(jnp.int32, (HALF_W, HD), 0)
    zeros = jnp.zeros((16, HD), jnp.float32)
    low_lane = lax.broadcasted_iota(jnp.int32, (STRIP, HD), 1) < MIX
    lines = []
    asides = [r_ref[share, 4 * GRID_W : MSG].astype(jnp.float32) for share in range(shares)]
    for patch_row in range(ROWS_BLOCK):
        at, spot = patch_row % 2 * HALF_W, patch_row * 4
        blocks = [
            r_ref[share, patch_row // 2 * GRID_W : (patch_row // 2 + 1) * GRID_W].astype(jnp.float32)[at : at + HALF_W]
            for share in range(shares)
        ]
        levels = [a[spot : spot + 1] + a[spot + 1 : spot + 2] + a[spot + 2 : spot + 3] for a in asides]
        top = levels[0]
        for level in levels[1:]:
            top = jnp.maximum(top, level)
        powers = [jnp.exp2(level - top) for level in levels]
        total = powers[0]
        for power in powers[1:]:
            total = total + power
        result = jnp.zeros((HALF_W, HD), jnp.float32)
        for block, power in zip(blocks, powers):
            weight = power / total
            low = jnp.sum(jnp.where(lane == row, weight, 0.0), axis=1, keepdims=True)
            high = jnp.sum(jnp.where(lane == row + HALF_W, weight, 0.0), axis=1, keepdims=True)
            result = result + jnp.where(lane < MIX, low, high) * block
        line = jnp.concatenate([zeros[:1], result, pltpu.roll(result, MIX, 1), zeros], axis=0)
        line = line[: 2 * HALF_W + 16]
        lines.append(line if patch_row % 2 == 0 else pltpu.roll(line, MIX, 1))
    for group in range(4):
        for tile in range(4):
            at = tile * TILE_W
            piece = jnp.where(low_lane, lines[2 * group][at : at + STRIP], lines[2 * group + 1][at : at + STRIP])
            piece = piece.astype(jnp.bfloat16)
            for copy in range(2):
                o_ref[copy * 4 + tile, group] = piece


def combine(received):
    return pl.pallas_call(
        combine_kernel,
        in_specs=[HERE],
        out_specs=HERE,
        out_shape=jax.ShapeDtypeStruct((8, 4, STRIP, HD), jnp.bfloat16),
        compiler_params=pltpu.CompilerParams(vmem_limit_bytes=8 * MIB),
        cost_estimate=pl.CostEstimate(flops=1000000, bytes_accessed=900000, transcendentals=0),
        name="combine",
    )(received)


def convolve_kernel(half, own, near, kernel, bias, o_ref, weights, rows):
    tap = {(0, 0, 1): 0, (0, 1, 0): 1, (0, 1, 1): 2, (1, 0, 0): 0, (1, 0, 1): 1, (1, 1, 0): 2}
    nothing = jnp.zeros((16, C_OUT), jnp.bfloat16)
    at = 0
    for side in range(2):
        for shift in range(2):
            for frame in range(3):
                for line in range(4):
                    for b in range(2):
                        step_x = tap.get((side, shift, b))
                        if line == 0 or step_x is None:
                            weights[at : at + 16] = nothing
                        else:
                            source = ((frame * 3 + line - 1) * 3 + step_x) * 16
                            weights[at : at + 16] = kernel[source : source + 16]
                        at += 16
    lane = lax.broadcasted_iota(jnp.int32, (STRIP, HD), 1)
    low = lane < MIX
    top = half[0] == 0
    lines = ([], [])
    for frame in range(3):
        mine = own[frame].astype(jnp.float32)
        beside = near[frame].astype(jnp.float32)
        mine_turned = pltpu.roll(mine, MIX, 1)
        beside_turned = pltpu.roll(beside, MIX, 1)
        upper = jnp.where(top, jnp.where(low, beside_turned, mine_turned), mine)
        lower = jnp.where(top, mine_turned, beside)
        lines[0].append(upper)
        lines[1].append(jnp.where(lane < 96, pltpu.roll(upper, 96, 1), pltpu.roll(lower, 96, 1)))
    spare = jnp.zeros((8, HD), jnp.float32)
    lines = [[jnp.concatenate([part, spare], axis=0) for part in parts] for parts in lines]
    for side in range(2):
        taps = jnp.concatenate(
            [
                jnp.concatenate([part[side + s : side + s + STRIP] for s in range(2) for part in parts], axis=1)
                for parts in lines
            ],
            axis=0,
        ).astype(jnp.bfloat16)
        size = 6 * HD
        sums = jnp.dot(taps, weights[side * size : (side + 1) * size, :], preferred_element_type=jnp.float32)
        sums = sums + bias[...]
        for a in range(2):
            for part in range(C_OUT // HD):
                block = sums[a * STRIP : a * STRIP + TILE_W, part * HD : (part + 1) * HD]
                rows[part, pl.ds(a * 40 + side, TILE_W, 2), :] = block
    o_ref[...] = jnp.concatenate([rows[part] for part in range(C_OUT // HD)], axis=1).astype(jnp.bfloat16)


def convolve(half, own, near, kernel, bias):
    return pl.pallas_call(
        convolve_kernel,
        in_specs=[pl.BlockSpec(memory_space=pltpu.SMEM)] + [HERE] * 4,
        out_specs=HERE,
        out_shape=jax.ShapeDtypeStruct((80, C_OUT), jnp.bfloat16),
        scratch_shapes=[pltpu.VMEM((12 * HD, C_OUT), jnp.bfloat16), pltpu.VMEM((C_OUT // HD, 80, HD), jnp.float32)],
        compiler_params=pltpu.CompilerParams(vmem_limit_bytes=8 * MIB),
        cost_estimate=pl.CostEstimate(flops=100000000, bytes_accessed=500000, transcendentals=0),
        name="convolve",
    )(half, own, near, kernel, bias)


def from_ahead(value, axis, steps):
    return lax.ppermute(value, axis, [((spot + steps) % 4, spot) for spot in range(4)])


def next_pair(value, axes):
    pairs = [(i, i + 8) for i in range(120) if i % 8 < 4] + [(i, i - 8) for i in range(8, 128) if i % 8 >= 4]
    return lax.ppermute(value, axes, pairs)


def cache_strips(tiles, tile_col):
    wide = tiles.reshape(2, 4, TILE_ROWS, HD)[:, :, :TILE_W].reshape(2, GRID_W, HD)
    wide = jnp.pad(wide, ((0, 0), (1, 3), (0, 0)))
    wide = lax.dynamic_slice_in_dim(wide, tile_col * TILE_W, STRIP, 1)
    return wide.reshape(2, STRIP, 2, MIX).transpose(2, 1, 0, 3).reshape(2, STRIP, HD)


def on_device(queries, keys, values, query_positions, key_positions, mixing, kernel, bias, cache):
    sp_index = lax.axis_index(SP)
    section = lax.axis_index("sec")
    half = lax.axis_index("y") // 4
    tile_col = sp_index % 4
    own = prepare(query_positions, key_positions, queries, keys, values, mixing, cache)
    own = lax.all_to_all(own, "y", 0, 0)
    q_copies, kv_own, tiles = spread(own)
    query_all = lax.all_to_all(q_copies, "zh", 0, 0)
    kv_last = from_ahead(kv_own, "x", 3)
    pairs = [kv_own, from_ahead(kv_own, "x", 1), kv_last, from_ahead(kv_own[:5], "x", 2), from_ahead(kv_last[5:], "x", 3)]
    cached = cache_strips(tiles, tile_col)
    query_all, pairs, cached = lax.optimization_barrier((query_all, pairs, cached))
    parts = attend(query_all, pairs)
    shares = lax.all_to_all(parts, "zh", 0, 0)
    tiles = lax.all_to_all(combine(shares), "y", 0, 0)
    strip = lax.all_to_all(add_heads(tiles).reshape(16, STRIP, HD), ("sec", "x"), 0, 0)
    strip = jnp.sum(strip.reshape(4, 4, STRIP, HD).astype(jnp.float32), axis=0).astype(jnp.bfloat16)
    strip = jnp.concatenate([cached, strip], axis=0)
    frames = lax.dynamic_slice_in_dim(strip, section, 3, 0)
    output = convolve(half.reshape(1), frames, next_pair(frames, SP), kernel, bias[None])
    return output.reshape(1, 1, 2, 40, kernel.shape[1])


def solution(mesh):
    fine = Mesh(mesh.devices.reshape(4, 4, 4, 8), ("sec", *SP))
    placed = (
        P(SP, "sec"),
        P(SP, "sec"),
        P(SP, "sec"),
        P(None, SP),
        P(None, SP),
        P("sec", None),
        P(),
        P(),
        P(None, SP, None, None, None),
    )
    return jax.shard_map(
        on_device,
        mesh=fine,
        in_specs=placed,
        out_specs=P("sec", SP, None, None, None),
        check_vma=False,
    )
```

```python
import math

import jax
import jax.numpy as jnp
import numpy as np
from jax import lax
from jax.experimental import pallas as pl
from jax.experimental.pallas import tpu as pltpu
from jax.sharding import Mesh
from jax.sharding import PartitionSpec as P

HD = 128
STRIP = 24
HEADS_SEC = 8
Q_OWN = 80
K_OWN = 96
V_ROWS = K_OWN // 2
KV_ROWS = K_OWN + V_ROWS
TILE_ROWS = 32
OWN_ROWS = KV_ROWS + Q_OWN + TILE_ROWS
MIX = 64
GRID_W = 80
HALF_W = GRID_W // 2
FRAME = 2560
KEYS_PART = 3072
Q_BLOCK = 640
ROWS_BLOCK = Q_BLOCK // GRID_W
SUB = 640
MSG = 4 * GRID_W + 32
TILE_W = 20
C_OUT = 384
SP = ("x", "zh", "y")
MIB = 1024 * 1024
HERE = pl.BlockSpec(memory_space=pltpu.VMEM)


def frequency_row():
    sixth = HD // 6
    time_pairs = (HD - 4 * sixth) // 2
    time = 10000.0 ** (-np.arange(time_pairs) / time_pairs)
    space = 10000.0 ** (-np.arange(sixth) / sixth)
    pairs = np.concatenate([time, space, space])
    return np.repeat(pairs, 2).astype(np.float32)[None, :]


def row_order():
    order = np.zeros((2, 2 * MIX, MIX), np.float32)
    for ch in range(16):
        for ab in range(4):
            for side in range(2):
                order[side, side * MIX + ab * 16 + ch, ch * 4 + ab] = 1.0
    return order


def patch_order():
    pick = np.zeros((2, TILE_ROWS, 40), np.float32)
    place = np.zeros((2, MIX, HD), np.float32)
    for side in range(2):
        for patch in range(TILE_W):
            pick[side, patch, 2 * patch + side] = 1.0
        for line in range(4):
            for ch in range(16):
                place[side, line * 16 + ch, line * 32 + side * 16 + ch] = 1.0
    return pick, place


def cosine_sine(angle):
    turns = jnp.floor(angle * jnp.float32(2.0 / math.pi) + 0.5)
    rest = angle - turns * jnp.float32(1.5703125)
    rest = rest - turns * jnp.float32(4.837512969970703e-4)
    rest = rest - turns * jnp.float32(7.549789948768648e-8)
    square = rest * rest
    sine = rest + rest * square * (
        jnp.float32(-1.6666654611e-1) + square * (jnp.float32(8.3321608736e-3) - square * jnp.float32(1.9515295891e-4))
    )
    cosine = 1.0 - 0.5 * square + square * square * (
        jnp.float32(4.166664568298827e-2)
        + square * (jnp.float32(-1.388731625493765e-3) + square * jnp.float32(2.443315711809948e-5))
    )
    quarter = turns.astype(jnp.int32)
    odd = (quarter & 1) == 1
    first, second = jnp.where(odd, sine, cosine), jnp.where(odd, cosine, sine)
    first = jnp.where(((quarter + 1) & 2) == 2, -first, first)
    return first, jnp.where((quarter & 2) == 2, -second, second)


def turn_tables(positions, freq):
    count = positions.shape[1]
    spot = positions.astype(jnp.float32)
    same = lax.broadcasted_iota(jnp.int32, (count, count), 0) == lax.broadcasted_iota(jnp.int32, (count, count), 1)
    column = [jnp.sum(jnp.where(same, spot[i : i + 1], 0.0), axis=1, keepdims=True) for i in range(3)]
    lane = lax.broadcasted_iota(jnp.int32, (count, HD), 1)
    base = jnp.where(lane < 44, column[0], jnp.where(lane < 86, column[1], column[2]))
    angle = base * freq
    cosine, sine = cosine_sine(angle)
    even = lax.rem(lane, 2) == 0
    zero = jnp.zeros_like(sine)
    return cosine, jnp.where(even, -sine, zero), jnp.where(even, zero, sine)


def turn(vectors, tables):
    cosine, from_next, from_last = tables
    wide = vectors.astype(jnp.float32)
    out = wide * cosine + pltpu.roll(wide, HD - 1, 1) * from_next + pltpu.roll(wide, 1, 1) * from_last
    return out.astype(jnp.bfloat16)


def prepare_kernel(qpos, kpos, freq, order, pick, place, queries, keys, values, mixing, cache, out, q_kept, k_kept):
    @pl.when(pl.program_id(0) == 0)
    def _():
        for kept, spots in ((q_kept, qpos), (k_kept, kpos)):
            for index, table in enumerate(turn_tables(spots[...], freq[...])):
                kept[index] = table

    q_tables = [q_kept[index] for index in range(3)]
    k_tables = [k_kept[index] for index in range(3)]
    tile = jnp.zeros((TILE_ROWS, HD), jnp.float32)
    for side in range(2):
        column = lax.dot_general(
            pick[side], cache[...], (((1,), (1,)), ((), ())), preferred_element_type=jnp.float32
        )
        tile = tile + jnp.dot(column.astype(jnp.bfloat16), place[side], preferred_element_type=jnp.float32)
    tile = tile.astype(jnp.bfloat16)
    mixed = [
        jnp.dot(order[side], mixing[...], preferred_element_type=jnp.float32).astype(jnp.bfloat16)
        for side in range(2)
    ]
    for head in range(HEADS_SEC // 2):
        cols = slice(head * HD, (head + 1) * HD)
        out[head, 0:K_OWN, :] = turn(keys[:, cols], k_tables)
        value = values[:, cols]
        mix_low = lax.dot_general(
            value[:V_ROWS], mixed[0][:, cols], (((1,), (1,)), ((), ())), preferred_element_type=jnp.float32
        )
        mix_high = lax.dot_general(
            value[V_ROWS:], mixed[1][:, cols], (((1,), (1,)), ((), ())), preferred_element_type=jnp.float32
        )
        out[head, K_OWN:KV_ROWS, :] = (mix_low + mix_high).astype(jnp.bfloat16)
        out[head, KV_ROWS : KV_ROWS + Q_OWN, :] = turn(queries[:, cols], q_tables)
        out[head, KV_ROWS + Q_OWN : OWN_ROWS, :] = tile


def prepare(qpos, kpos, queries, keys, values, mixing, cache):
    return pl.pallas_call(
        prepare_kernel,
        grid=(2,),
        in_specs=[
            pl.BlockSpec((3, Q_OWN), lambda i: (0, 0)),
            pl.BlockSpec((3, K_OWN), lambda i: (0, 0)),
            pl.BlockSpec((1, HD), lambda i: (0, 0)),
            pl.BlockSpec((2, HD, MIX), lambda i: (0, 0, 0)),
            pl.BlockSpec((2, TILE_ROWS, 40), lambda i: (0, 0, 0)),
            pl.BlockSpec((2, MIX, HD), lambda i: (0, 0, 0)),
            pl.BlockSpec((Q_OWN, 4 * HD), lambda i: (0, i)),
            pl.BlockSpec((K_OWN, 4 * HD), lambda i: (0, i)),
            pl.BlockSpec((K_OWN, 4 * HD), lambda i: (0, i)),
            pl.BlockSpec((MIX, 4 * HD), lambda i: (0, i)),
            pl.BlockSpec((MIX, 40), lambda i: (0, 0)),
        ],
        out_specs=pl.BlockSpec((HEADS_SEC // 2, OWN_ROWS, HD), lambda i: (i, 0, 0)),
        scratch_shapes=[pltpu.VMEM((3, Q_OWN, HD), jnp.float32), pltpu.VMEM((3, K_OWN, HD), jnp.float32)],
        out_shape=jax.ShapeDtypeStruct((HEADS_SEC, OWN_ROWS, HD), jnp.bfloat16),
        compiler_params=pltpu.CompilerParams(vmem_limit_bytes=56 * MIB),
        cost_estimate=pl.CostEstimate(flops=50000000, bytes_accessed=1200000, transcendentals=0),
        name="prepare",
    )(
        qpos,
        kpos,
        jnp.asarray(frequency_row()),
        jnp.asarray(row_order(), jnp.bfloat16),
        *(jnp.asarray(part, jnp.bfloat16) for part in patch_order()),
        queries,
        keys,
        values,
        mixing.T,
        cache.transpose(0, 1, 2, 4, 3).reshape(MIX, 40),
    )


def spread_kernel(own, queries, pairs, tiles):
    for part in range(HEADS_SEC):
        lines = own[part, KV_ROWS : KV_ROWS + Q_OWN, :]
        for copy in range(4):
            queries[copy, part] = lines
        pairs[part] = own[part, 0:KV_ROWS, :]
        tiles[part] = own[part, KV_ROWS + Q_OWN : OWN_ROWS, :]


def spread(own):
    return pl.pallas_call(
        spread_kernel,
        in_specs=[HERE],
        out_specs=[HERE] * 3,
        out_shape=[
            jax.ShapeDtypeStruct((4, HEADS_SEC, Q_OWN, HD), jnp.bfloat16),
            jax.ShapeDtypeStruct((HEADS_SEC, KV_ROWS, HD), jnp.bfloat16),
            jax.ShapeDtypeStruct((HEADS_SEC, TILE_ROWS, HD), jnp.bfloat16),
        ],
        compiler_params=pltpu.CompilerParams(vmem_limit_bytes=4 * MIB),
        cost_estimate=pl.CostEstimate(flops=0, bytes_accessed=800000, transcendentals=0),
        name="spread",
    )(own)


def add_heads_kernel(parts, out):
    terms = [parts[part].astype(jnp.float32) for part in range(8)]
    while len(terms) > 1:
        terms = [terms[i] + terms[i + 1] for i in range(0, len(terms), 2)]
    total = terms[0].astype(jnp.bfloat16)
    for copy in range(4):
        out[copy] = total


def add_heads(parts):
    return pl.pallas_call(
        add_heads_kernel,
        in_specs=[HERE],
        out_specs=HERE,
        out_shape=jax.ShapeDtypeStruct((4, 4, STRIP, HD), jnp.bfloat16),
        compiler_params=pltpu.CompilerParams(vmem_limit_bytes=4 * MIB),
        cost_estimate=pl.CostEstimate(flops=100000, bytes_accessed=300000, transcendentals=0),
        name="add_heads",
    )(parts)


def attend_kernel(*refs):
    q_ref, kv_refs, o_ref = refs[0], refs[1:6], refs[6]
    k_buf, v_buf, s_even, s_odd, levels = refs[7:]
    lane = lax.broadcasted_iota(jnp.int32, (V_ROWS, HD), 1)
    ones = jnp.where(lane == MIX, 1.0, 0.0)
    at = 0
    for kv_ref in kv_refs:
        for part in range(kv_ref.shape[0]):
            k_buf[at : at + K_OWN] = kv_ref[part, 0:K_OWN, :]
            both = kv_ref[part, K_OWN:KV_ROWS, :].astype(jnp.float32)
            v_buf[at : at + V_ROWS] = jnp.where(lane < MIX, both, ones).astype(jnp.bfloat16)
            other = pltpu.roll(both, MIX, 1)
            v_buf[at + V_ROWS : at + K_OWN] = jnp.where(lane < MIX, other, ones).astype(jnp.bfloat16)
            at += K_OWN

    scale = jnp.float32(math.log2(math.e) / math.sqrt(HD))
    diagonal = lax.broadcasted_iota(jnp.int32, (GRID_W, HD), 1) == lax.broadcasted_iota(jnp.int32, (GRID_W, HD), 0)
    low_lane = lax.broadcasted_iota(jnp.int32, (HALF_W, HD), 1) < MIX

    def score(start, rows):
        return lax.dot_general(
            q_ref[start : start + rows, :],
            k_buf[...],
            (((1,), (1,)), ((), ())),
            preferred_element_type=jnp.float32,
        )

    def finish(start, rows, s_ref):
        scores = s_ref[0:rows]
        top = jnp.max(scores, axis=1, keepdims=True)
        weights = jnp.exp2((scores - top) * scale).astype(jnp.bfloat16)
        sums = jnp.dot(weights, v_buf[...], preferred_element_type=jnp.float32)
        total = sums[:, MIX : MIX + 1]
        mean = sums / total
        level = top * scale + jnp.log2(total)
        for block in range(rows // (2 * GRID_W)):
            piece, pair = divmod(start // (2 * GRID_W) + block, 4)
            lines = []
            for half in range(2):
                at = (2 * block + half) * GRID_W
                low = mean[at : at + HALF_W]
                high = pltpu.roll(mean[at + HALF_W : at + GRID_W], MIX, 1)
                lines.append(jnp.where(low_lane, low, high))
                line = jnp.sum(jnp.where(diagonal, level[at : at + GRID_W], 0.0), axis=0, keepdims=True)
                first = line.astype(jnp.bfloat16).astype(jnp.float32)
                line = line - first
                second = line.astype(jnp.bfloat16).astype(jnp.float32)
                third = line - second
                spot = piece * 8 + half * 4
                levels[pair, spot : spot + 4] = jnp.concatenate(
                    [first, second, third, jnp.zeros((1, HD), jnp.float32)], axis=0
                )
            o_ref[pair, piece * GRID_W : (piece + 1) * GRID_W] = jnp.concatenate(lines, axis=0).astype(jnp.bfloat16)

    blocks = [(0, 320), (320, 640), (960, 640), (1600, 640), (2240, 320)]
    buffers = [s_even, s_odd]
    s_even[0:320] = score(0, 320)
    for index, (start, rows) in enumerate(blocks):
        if index + 1 < len(blocks):
            after, count = blocks[index + 1]
            buffers[(index + 1) % 2][0:count] = score(after, count)
        finish(start, rows, buffers[index % 2])
    o_ref[:, 4 * GRID_W : MSG] = levels[...].astype(jnp.bfloat16)


def attend(queries, pairs):
    return pl.pallas_call(
        attend_kernel,
        in_specs=[HERE] * 6,
        out_specs=HERE,
        out_shape=jax.ShapeDtypeStruct((4, MSG, HD), jnp.bfloat16),
        scratch_shapes=[
            pltpu.VMEM((KEYS_PART, HD), jnp.bfloat16),
            pltpu.VMEM((KEYS_PART, HD), jnp.bfloat16),
            pltpu.VMEM((SUB, KEYS_PART), jnp.float32),
            pltpu.VMEM((SUB, KEYS_PART), jnp.float32),
            pltpu.VMEM((4, 32, HD), jnp.float32),
        ],
        compiler_params=pltpu.CompilerParams(vmem_limit_bytes=42 * MIB),
        cost_estimate=pl.CostEstimate(flops=4 * FRAME * KEYS_PART * HD, bytes_accessed=2000000, transcendentals=0),
        name="attend",
    )(queries.reshape(FRAME, HD), *pairs)


def combine_kernel(r_ref, o_ref):
    shares = r_ref.shape[0]
    lane = lax.broadcasted_iota(jnp.int32, (HALF_W, HD), 1)
    row = lax.broadcasted_iota(jnp.int32, (HALF_W, HD), 0)
    zeros = jnp.zeros((16, HD), jnp.float32)
    low_lane = lax.broadcasted_iota(jnp.int32, (STRIP, HD), 1) < MIX
    lines = []
    asides = [r_ref[share, 4 * GRID_W : MSG].astype(jnp.float32) for share in range(shares)]
    for patch_row in range(ROWS_BLOCK):
        at, spot = patch_row % 2 * HALF_W, patch_row * 4
        blocks = [
            r_ref[share, patch_row // 2 * GRID_W : (patch_row // 2 + 1) * GRID_W].astype(jnp.float32)[at : at + HALF_W]
            for share in range(shares)
        ]
        levels = [a[spot : spot + 1] + a[spot + 1 : spot + 2] + a[spot + 2 : spot + 3] for a in asides]
        top = levels[0]
        for level in levels[1:]:
            top = jnp.maximum(top, level)
        powers = [jnp.exp2(level - top) for level in levels]
        total = powers[0]
        for power in powers[1:]:
            total = total + power
        result = jnp.zeros((HALF_W, HD), jnp.float32)
        for block, power in zip(blocks, powers):
            weight = power / total
            low = jnp.sum(jnp.where(lane == row, weight, 0.0), axis=1, keepdims=True)
            high = jnp.sum(jnp.where(lane == row + HALF_W, weight, 0.0), axis=1, keepdims=True)
            result = result + jnp.where(lane < MIX, low, high) * block
        line = jnp.concatenate([zeros[:1], result, pltpu.roll(result, MIX, 1), zeros], axis=0)
        line = line[: 2 * HALF_W + 16]
        lines.append(line if patch_row % 2 == 0 else pltpu.roll(line, MIX, 1))
    for group in range(4):
        for tile in range(4):
            at = tile * TILE_W
            piece = jnp.where(low_lane, lines[2 * group][at : at + STRIP], lines[2 * group + 1][at : at + STRIP])
            piece = piece.astype(jnp.bfloat16)
            for copy in range(2):
                o_ref[copy * 4 + tile, group] = piece


def combine(received):
    return pl.pallas_call(
        combine_kernel,
        in_specs=[HERE],
        out_specs=HERE,
        out_shape=jax.ShapeDtypeStruct((8, 4, STRIP, HD), jnp.bfloat16),
        compiler_params=pltpu.CompilerParams(vmem_limit_bytes=8 * MIB),
        cost_estimate=pl.CostEstimate(flops=1000000, bytes_accessed=900000, transcendentals=0),
        name="combine",
    )(received)


def convolve_kernel(half, own, near, kernel, bias, o_ref, weights, rows):
    tap = {(0, 0, 1): 0, (0, 1, 0): 1, (0, 1, 1): 2, (1, 0, 0): 0, (1, 0, 1): 1, (1, 1, 0): 2}
    nothing = jnp.zeros((16, C_OUT), jnp.bfloat16)
    at = 0
    for side in range(2):
        for shift in range(2):
            for frame in range(3):
                for line in range(4):
                    for b in range(2):
                        step_x = tap.get((side, shift, b))
                        if line == 0 or step_x is None:
                            weights[at : at + 16] = nothing
                        else:
                            source = ((frame * 3 + line - 1) * 3 + step_x) * 16
                            weights[at : at + 16] = kernel[source : source + 16]
                        at += 16
    lane = lax.broadcasted_iota(jnp.int32, (STRIP, HD), 1)
    low = lane < MIX
    top = half[0] == 0
    lines = ([], [])
    for frame in range(3):
        mine = own[frame].astype(jnp.float32)
        beside = near[frame].astype(jnp.float32)
        mine_turned = pltpu.roll(mine, MIX, 1)
        beside_turned = pltpu.roll(beside, MIX, 1)
        upper = jnp.where(top, jnp.where(low, beside_turned, mine_turned), mine)
        lower = jnp.where(top, mine_turned, beside)
        lines[0].append(upper)
        lines[1].append(jnp.where(lane < 96, pltpu.roll(upper, 96, 1), pltpu.roll(lower, 96, 1)))
    spare = jnp.zeros((8, HD), jnp.float32)
    lines = [[jnp.concatenate([part, spare], axis=0) for part in parts] for parts in lines]
    for side in range(2):
        taps = jnp.concatenate(
            [
                jnp.concatenate([part[side + s : side + s + STRIP] for s in range(2) for part in parts], axis=1)
                for parts in lines
            ],
            axis=0,
        ).astype(jnp.bfloat16)
        size = 6 * HD
        sums = jnp.dot(taps, weights[side * size : (side + 1) * size, :], preferred_element_type=jnp.float32)
        sums = sums + bias[...]
        for a in range(2):
            for part in range(C_OUT // HD):
                block = sums[a * STRIP : a * STRIP + TILE_W, part * HD : (part + 1) * HD]
                rows[part, pl.ds(a * 40 + side, TILE_W, 2), :] = block
    o_ref[...] = jnp.concatenate([rows[part] for part in range(C_OUT // HD)], axis=1).astype(jnp.bfloat16)


def convolve(half, own, near, kernel, bias):
    return pl.pallas_call(
        convolve_kernel,
        in_specs=[pl.BlockSpec(memory_space=pltpu.SMEM)] + [HERE] * 4,
        out_specs=HERE,
        out_shape=jax.ShapeDtypeStruct((80, C_OUT), jnp.bfloat16),
        scratch_shapes=[pltpu.VMEM((12 * HD, C_OUT), jnp.bfloat16), pltpu.VMEM((C_OUT // HD, 80, HD), jnp.float32)],
        compiler_params=pltpu.CompilerParams(vmem_limit_bytes=8 * MIB),
        cost_estimate=pl.CostEstimate(flops=100000000, bytes_accessed=500000, transcendentals=0),
        name="convolve",
    )(half, own, near, kernel, bias)


def from_ahead(value, axis, steps):
    return lax.ppermute(value, axis, [((spot + steps) % 4, spot) for spot in range(4)])


def next_pair(value, axes):
    pairs = [(i, i + 8) for i in range(120) if i % 8 < 4] + [(i, i - 8) for i in range(8, 128) if i % 8 >= 4]
    return lax.ppermute(value, axes, pairs)


def cache_strips(tiles, tile_col):
    wide = tiles.reshape(2, 4, TILE_ROWS, HD)[:, :, :TILE_W].reshape(2, GRID_W, HD)
    wide = jnp.pad(wide, ((0, 0), (1, 3), (0, 0)))
    wide = lax.dynamic_slice_in_dim(wide, tile_col * TILE_W, STRIP, 1)
    return wide.reshape(2, STRIP, 2, MIX).transpose(2, 1, 0, 3).reshape(2, STRIP, HD)


def on_device(queries, keys, values, query_positions, key_positions, mixing, kernel, bias, cache):
    sp_index = lax.axis_index(SP)
    section = lax.axis_index("sec")
    half = lax.axis_index("y") // 4
    tile_col = sp_index % 4
    own = prepare(query_positions, key_positions, queries, keys, values, mixing, cache)
    own = lax.all_to_all(own, "y", 0, 0)
    q_copies, kv_own, tiles = spread(own)
    query_all = lax.all_to_all(q_copies, "zh", 0, 0)
    kv_last = from_ahead(kv_own, "x", 3)
    pairs = [kv_own, from_ahead(kv_own, "x", 1), kv_last, from_ahead(kv_own[:4], "x", 2), from_ahead(kv_last[4:], "x", 3)]
    cached = cache_strips(tiles, tile_col)
    query_all, pairs, cached = lax.optimization_barrier((query_all, pairs, cached))
    parts = attend(query_all, pairs)
    shares = lax.all_to_all(parts, "zh", 0, 0)
    tiles = lax.all_to_all(combine(shares), "y", 0, 0)
    strip = lax.all_to_all(add_heads(tiles).reshape(16, STRIP, HD), ("sec", "x"), 0, 0)
    strip = jnp.sum(strip.reshape(4, 4, STRIP, HD).astype(jnp.float32), axis=0).astype(jnp.bfloat16)
    strip = jnp.concatenate([cached, strip], axis=0)
    frames = lax.dynamic_slice_in_dim(strip, section, 3, 0)
    output = convolve(half.reshape(1), frames, next_pair(frames, SP), kernel, bias[None])
    return output.reshape(1, 1, 2, 40, kernel.shape[1])


def solution(mesh):
    fine = Mesh(mesh.devices.reshape(4, 4, 4, 8), ("sec", *SP))
    placed = (
        P(SP, "sec"),
        P(SP, "sec"),
        P(SP, "sec"),
        P(None, SP),
        P(None, SP),
        P("sec", None),
        P(),
        P(),
        P(None, SP, None, None, None),
    )
    return jax.shard_map(
        on_device,
        mesh=fine,
        in_specs=placed,
        out_specs=P("sec", SP, None, None, None),
        check_vma=False,
    )
```
